32 devices in a mesh: dp: 8 (over y, x, core), tensor: 4 (over z).
Axes of the slice: x: 2, y: 2, z: 4, core: 2. Of those that a mesh axis runs over, the one named last changes fastest.
Arguments:
- tokens: bfloat16 [1024, 16384], P(None, ('dp', 'tensor')), may hold values from -6 to 6
- cotangent: bfloat16 [1024, 16384], P(None, ('dp', 'tensor')), may hold values from -6 to 6
- first_gain: float32 [2048], replicated, may hold values from 0.5 to 1.5
- query_weight: bfloat16 [2048, 2048], P(None, 'tensor'), may hold values from -0.125 to 0.125
- key_matrix: bfloat16 [2048, 512], P(None, 'tensor'), may hold values from -0.125 to 0.125
- value_matrix: bfloat16 [2048, 512], P(None, 'tensor'), may hold values from -0.125 to 0.125
- output_weight: bfloat16 [2048, 2048], P('tensor'), may hold values from -1 to 1
- second_gain: float32 [2048], replicated, may hold values from 0.5 to 1.5
- gate_weight: bfloat16 [2048, 5632], P(None, 'tensor'), may hold values from -0.125 to 0.125
- up_weight: bfloat16 [2048, 5632], P(None, 'tensor'), may hold values from -0.125 to 0.125
- down_weight: bfloat16 [5632, 2048], P('tensor'), may hold values from -0.078125 to 0.078125
- seq_lengths: int32 [32], replicated, may hold values from 8 to 1024, as said below
- owner_order: int32 [32], replicated, may hold values from 0 to 31, as said below
- skip_mask: int32 [32], replicated, may hold values 0 or 1
Outputs:
- layer_output: bfloat16 [1024, 16384], P(None, ('dp', 'tensor'))
- input_grad: bfloat16 [1024, 16384], P(None, ('dp', 'tensor'))
- first_gain_grad: float32 [2048], P('dp')
- query_grad: float32 [2048, 2048], P('dp', 'tensor')
- key_grad: float32 [2048, 512], P('dp', 'tensor')
- value_grad: float32 [2048, 512], P('dp', 'tensor')
- output_grad: float32 [2048, 2048], P('tensor', 'dp')
- second_gain_grad: float32 [2048], P('dp')
- gate_grad: float32 [2048, 5632], P('dp', 'tensor')
- up_grad: float32 [2048, 5632], P('dp', 'tensor')
- down_grad: float32 [5632, 2048], P('tensor', 'dp')
The draws below stay inside these ranges and needn't reach their ends.
Inputs may be any that keep to these rules, and one draw needn't show every extreme that they name: `seq_lengths`: every length is a multiple of 8 and they sum to 8192. Taken in the order owner_order, the running sums meet every multiple of 1024, so that owner j, the j-th run of 1024 tokens in that order, holds whole sequences; the longest is exactly 1024. `owner_order`: each of 0 to 31 appears once.
All inputs are finite; a program needn't handle non-finite values.
Results may differ from the reference program's by a relative error of at most 0.018.
Values may be sent and summed in bfloat16 or wider, within the bound.
A program may use at most 256 MiB of HBM per device.

```python
import math
import jax
import jax.numpy as jnp
from jax import lax

MODEL_WIDTH = 2048
QUERY_HEADS = 16
KEY_VALUE_HEADS = 4
HEAD_WIDTH = 128
FF = 5632
TOKENS_PER_SHARD = 1024
TOKENS = 8192
NSEQ = 32
UNITS = 128
N_DP = 8


def deal_sequences(key):
    base = jax.random.fold_in(key, 1234)
    pick_key, cut_key, order_key = jax.random.split(base, 3)
    whole = jax.random.randint(pick_key, (), 0, N_DP)
    inner = UNITS - 1
    owners = jnp.repeat(jnp.arange(N_DP, dtype=jnp.int32), inner)
    offsets = jnp.tile(jnp.arange(1, UNITS, dtype=jnp.int32), N_DP)
    where_cut = owners * UNITS + offsets
    candidates = N_DP * inner
    scores = jax.random.randint(cut_key, (candidates,), 0, 1 << 19) * candidates + jnp.arange(candidates, dtype=jnp.int32)
    scores = jnp.where(owners == whole, -1, scores)
    chosen = lax.top_k(scores, NSEQ - N_DP)[1]
    bounds = jnp.concatenate([jnp.arange(N_DP + 1, dtype=jnp.int32) * UNITS, where_cut[chosen]])
    bounds = jnp.sort(bounds)
    owner_lengths = (bounds[1:] - bounds[:-1]) * N_DP
    order = jax.random.permutation(order_key, NSEQ).astype(jnp.int32)
    lengths = jnp.zeros((NSEQ,), jnp.int32).at[order].set(owner_lengths.astype(jnp.int32))
    return (lengths, order)


def draw_seq_lengths(key, part):
    return deal_sequences(key)[0]


def draw_owner_order(key, part):
    return deal_sequences(key)[1]


def place_ends(values, own_key, least, largest):
    shape = values.shape
    spot = [jax.random.randint(jax.random.fold_in(own_key, axis), (), 0, shape[axis]) for axis in range(len(shape))]
    values = values.at[tuple(spot)].set(least)
    longest = shape.index(max(shape))
    spot[longest] = (spot[longest] + 1) % shape[longest]
    return values.at[tuple(spot)].set(largest)


def block_scale(rng, extent, cuts, smallest, largest):
    gain = 1.0
    for axis_at, parts in cuts:
        steps = jax.random.uniform(jax.random.fold_in(jax.random.fold_in(rng, 6), axis_at), (parts,), jnp.float32, smallest / len(cuts), largest / len(cuts))
        gain = gain * jnp.repeat(jnp.exp(steps), extent[axis_at] // parts).reshape((-1,) + (1,) * (len(extent) - 1 - axis_at))
    return gain


def gaussian(own_key, shape, width, most, cuts=(), kind=jnp.bfloat16):
    values = jax.random.normal(own_key, shape, jnp.float32) * width
    if len(cuts) > 0:
        values = block_scale(own_key, shape, cuts, -0.22, 0.18) * values
    return jnp.clip(values, min=-most, max=most).astype(kind)


def setup_inputs(seed: int = 0) -> dict:
    seeds = jax.random.split(jax.random.key(seed), 15)
    return {
        "tokens": gaussian(seeds[0], (TOKENS_PER_SHARD, N_DP * MODEL_WIDTH), 1.0, 6.0, ((1, 32),)),
        "cotangent": gaussian(seeds[1], (TOKENS_PER_SHARD, N_DP * MODEL_WIDTH), 1.0, 6.0, ((1, 32),)),
        "first_gain": jnp.clip(1.0 + 0.1 * jax.random.normal(seeds[2], (MODEL_WIDTH,), jnp.float32), 0.5, 1.5),
        "query_weight": gaussian(seeds[3], (MODEL_WIDTH, QUERY_HEADS * HEAD_WIDTH), MODEL_WIDTH ** -0.5, 0.125, ((1, 4),)),
        "key_matrix": gaussian(seeds[4], (MODEL_WIDTH, KEY_VALUE_HEADS * HEAD_WIDTH), MODEL_WIDTH ** -0.5, 0.125, ((1, 4),)),
        "value_matrix": gaussian(seeds[5], (MODEL_WIDTH, KEY_VALUE_HEADS * HEAD_WIDTH), MODEL_WIDTH ** -0.5, 0.125, ((1, 4),)),
        "output_weight": gaussian(seeds[6], (QUERY_HEADS * HEAD_WIDTH, MODEL_WIDTH), (max(QUERY_HEADS * HEAD_WIDTH // 64, 8)) ** -0.5, 1.0, ((0, 4),)),
        "second_gain": jnp.clip(1.0 + 0.1 * jax.random.normal(seeds[7], (MODEL_WIDTH,), jnp.float32), 0.5, 1.5),
        "gate_weight": gaussian(seeds[8], (MODEL_WIDTH, FF), MODEL_WIDTH ** -0.5, 0.125, ((1, 4),)),
        "up_weight": gaussian(seeds[9], (MODEL_WIDTH, FF), MODEL_WIDTH ** -0.5, 0.125, ((1, 4),)),
        "down_weight": gaussian(seeds[10], (FF, MODEL_WIDTH), FF ** -0.5, 0.078125, ((0, 4),)),
        "seq_lengths": draw_seq_lengths(jax.random.fold_in(seeds[14], 71), 0),
        "owner_order": draw_owner_order(jax.random.fold_in(seeds[14], 71), 0),
        "skip_mask": place_ends((jax.random.randint(seeds[13], (NSEQ,), 0, 4) < 3).astype(jnp.int32), jax.random.fold_in(seeds[13], 1), 0, 1),
    }


eps = 1e-05
rope_base = 10000.0
highest = lax.Precision.HIGHEST

@jax.custom_vjp
def lower_copy(v):
    return lax.optimization_barrier(v.astype(jnp.bfloat16)).astype(jnp.float32)

@jax.custom_vjp
def low_back(v):
    return v

def low_keep(v):
    return (lower_copy(v), None)

def low_pass(kept, grad):
    return (grad,)

def back_keep(v):
    return (v, None)

def back_low(kept, grad):
    return (lower_copy(grad),)
lower_copy.defvjp(low_keep, low_pass)
low_back.defvjp(back_keep, back_low)

def rotary_tables(token_positions, head_size):
    half = head_size // 2
    freqs = rope_base ** (-(jnp.arange(half).astype(jnp.float32) * 2.0) / head_size)
    angles = token_positions.astype(jnp.float32)[:, None] * freqs[None, :]
    angles = jnp.concatenate([angles, angles], axis=1)
    return (jnp.cos(angles), jnp.sin(angles))

def rotate_half(values):
    half = values.shape[-1] // 2
    return jnp.concatenate([-values[..., half:], values[..., :half]], axis=-1)

def attend_packed_rows(pieces):
    query_rows, key, value, seq_block, pos_block = pieces
    item_count = query_rows.shape[0]
    head_group = QUERY_HEADS // KEY_VALUE_HEADS
    query_four_axes = query_rows.reshape(item_count, KEY_VALUE_HEADS, head_group, HEAD_WIDTH)
    raw = jnp.einsum('qcgd,kcd->cgqk', query_four_axes, key, precision=highest) * (1.0 / math.sqrt(HEAD_WIDTH))
    raw = low_back(raw)
    allowed = (seq_block[:, None] == seq_block[None, :]) & (pos_block[None, :] <= pos_block[:, None])
    raw = jnp.where(allowed, raw, -1e+30)
    probs = lower_copy(jax.nn.softmax(raw, axis=-1))
    out = jnp.einsum('cgqk,kcd->qcgd', probs, value, precision=highest)
    return out.reshape(item_count, QUERY_HEADS * HEAD_WIDTH)

def forward(inputs, first_gain, query_weight, key_matrix, value_matrix, output_weight, second_gain, gate_weight, up_weight, down_weight, sequence_index, token_positions, keep_rows):
    item_count = inputs.shape[0]
    scale_one = lax.rsqrt(lax.optimization_barrier(jnp.mean(inputs * inputs, axis=1, keepdims=True)) + eps)
    normed_one = lower_copy(inputs * scale_one * first_gain)
    query_pre = low_back(jnp.dot(normed_one, query_weight, precision=highest))
    key_unrotated = low_back(jnp.dot(normed_one, key_matrix, precision=highest))
    every_value = lower_copy(low_back(jnp.dot(normed_one, value_matrix, precision=highest)))
    cosine, sine = rotary_tables(token_positions, HEAD_WIDTH)

    def apply_rotation(values):
        return values * cosine[:, None, :] + rotate_half(values) * sine[:, None, :]
    every_query = lower_copy(apply_rotation(query_pre.reshape(item_count, QUERY_HEADS, HEAD_WIDTH)))
    every_key = lower_copy(apply_rotation(key_unrotated.reshape(item_count, KEY_VALUE_HEADS, HEAD_WIDTH)))
    every_value = every_value.reshape(item_count, KEY_VALUE_HEADS, HEAD_WIDTH)
    block_list = item_count // TOKENS_PER_SHARD
    attended_rows = lax.map(jax.checkpoint(attend_packed_rows), (every_query.reshape(block_list, TOKENS_PER_SHARD, QUERY_HEADS, HEAD_WIDTH), every_key.reshape(block_list, TOKENS_PER_SHARD, KEY_VALUE_HEADS, HEAD_WIDTH), every_value.reshape(block_list, TOKENS_PER_SHARD, KEY_VALUE_HEADS, HEAD_WIDTH), sequence_index.reshape(block_list, TOKENS_PER_SHARD), token_positions.reshape(block_list, TOKENS_PER_SHARD)))
    attended_rows = lower_copy(low_back(attended_rows.reshape(item_count, QUERY_HEADS * HEAD_WIDTH)))
    attn_out = low_back(jnp.dot(attended_rows, output_weight, precision=highest))
    hidden_res = inputs + keep_rows * attn_out
    scale_two = lax.rsqrt(lax.optimization_barrier(jnp.mean(hidden_res * hidden_res, axis=1, keepdims=True)) + eps)
    normed_two = lower_copy(hidden_res * scale_two * second_gain)
    gate = low_back(jnp.dot(normed_two, gate_weight, precision=highest))
    upward = low_back(jnp.dot(normed_two, up_weight, precision=highest))
    inner = lower_copy(jax.nn.silu(gate) * upward)
    ffn_out = low_back(jnp.dot(inner, down_weight, precision=highest))
    return hidden_res + keep_rows * ffn_out

def reference(tokens, cotangent, first_gain, query_weight, key_matrix, value_matrix, output_weight, second_gain, gate_weight, up_weight, down_weight, seq_lengths, owner_order, skip_mask):
    total = TOKENS
    given = tokens.reshape(total, MODEL_WIDTH)
    given_grad = cotangent.reshape(total, MODEL_WIDTH)
    starts = jnp.cumsum(seq_lengths) - seq_lengths
    owner_lengths = seq_lengths[owner_order]
    owner_ends = jnp.cumsum(owner_lengths)
    place = jnp.arange(total).astype(jnp.int32)
    which = jnp.searchsorted(owner_ends, place, side='right').astype(jnp.int32)
    offset = place - (owner_ends - owner_lengths)[which]
    sequence_index = owner_order[which].astype(jnp.int32)
    source_rows = (starts[sequence_index] + offset).astype(jnp.int32)
    token_positions = offset.astype(jnp.int32)
    keep_rows = skip_mask[sequence_index].astype(jnp.float32)[:, None]
    inputs = given[source_rows].astype(jnp.float32)
    grads_in = given_grad[source_rows].astype(jnp.float32)
    params = [first_gain.astype(jnp.float32), query_weight.astype(jnp.float32), key_matrix.astype(jnp.float32), value_matrix.astype(jnp.float32), output_weight.astype(jnp.float32), second_gain.astype(jnp.float32), gate_weight.astype(jnp.float32), up_weight.astype(jnp.float32), down_weight.astype(jnp.float32)]

    def layer(inputs, gain_one, wquery, wkey, wvalue, woutput, gain_two, wgate, wup, wdown):
        return forward(inputs, gain_one, wquery, wkey, wvalue, woutput, gain_two, wgate, wup, wdown, sequence_index, token_positions, keep_rows)
    result, pullback = jax.vjp(layer, inputs, *params)
    grads = pullback(grads_in)
    out_given = jnp.zeros((total, MODEL_WIDTH), jnp.float32).at[source_rows].set(result)
    grad_given = jnp.zeros((total, MODEL_WIDTH), jnp.float32).at[source_rows].set(grads[0])
    return (out_given.astype(jnp.bfloat16).reshape(TOKENS_PER_SHARD, N_DP * MODEL_WIDTH), grad_given.astype(jnp.bfloat16).reshape(TOKENS_PER_SHARD, N_DP * MODEL_WIDTH), grads[1], grads[2], grads[3], grads[4], grads[5], grads[6], grads[7], grads[8], grads[9])
```

```python
import math

import jax
import jax.numpy as jnp
from jax import lax
from jax.sharding import PartitionSpec as P

HEAD_WIDTH = 128


eps = 1e-05
rope_base = 10000.0


def rotary_tables(token_positions, head_size):
    half = head_size // 2
    freqs = rope_base ** (-(jnp.arange(half).astype(jnp.float32) * 2.0) / head_size)
    angles = token_positions.astype(jnp.float32)[:, None] * freqs[None, :]
    angles = jnp.concatenate([angles, angles], axis=1)
    return (jnp.cos(angles), jnp.sin(angles))


def rotate_half(values):
    half = values.shape[-1] // 2
    return jnp.concatenate([-values[..., half:], values[..., :half]], axis=-1)


def rotate_back(values):
    half = values.shape[-1] // 2
    return jnp.concatenate([values[..., half:], -values[..., :half]], axis=-1)


def matmul(left, right):
    return jnp.dot(left, right, preferred_element_type=jnp.float32)


def per_device(
    tokens,
    cotangent,
    first_gain,
    query_weight,
    key_matrix,
    value_matrix,
    output_weight,
    second_gain,
    gate_weight,
    up_weight,
    down_weight,
    seq_lengths,
    owner_order,
    skip_mask,
):
    groups = lax.axis_size("dp")
    member = lax.axis_index("dp")
    width_part = tokens.shape[1]
    row_count = tokens.shape[0]
    per_owner = row_count // groups
    seq_count = seq_lengths.shape[0]
    seq_index = jnp.arange(seq_count, dtype=jnp.int32)
    before = (seq_index[None, :] < seq_index[:, None]).astype(jnp.int32)
    unit_lengths = seq_lengths // groups
    unit_starts = jnp.sum(before * unit_lengths[None, :], axis=1)
    placed = (owner_order[:, None] == seq_index[None, :]).astype(jnp.int32)
    order_lengths = jnp.sum(placed * unit_lengths[None, :], axis=1)
    order_starts = jnp.sum(placed * unit_starts[None, :], axis=1)
    order_keep = jnp.sum(placed * skip_mask[None, :], axis=1)
    order_before = jnp.sum(before * order_lengths[None, :], axis=1)
    places = jnp.arange(row_count, dtype=jnp.int32)
    covers = (
        (places[:, None] >= order_before[None, :])
        & (places[:, None] < (order_before + order_lengths)[None, :])
    ).astype(jnp.int32)
    send_rows = places + jnp.sum(covers * (order_starts - order_before)[None, :], axis=1)
    given_before = jnp.sum(placed * order_before[:, None], axis=0)
    given_covers = (
        (places[:, None] >= unit_starts[None, :])
        & (places[:, None] < (unit_starts + unit_lengths)[None, :])
    ).astype(jnp.int32)
    slot_of = places + jnp.sum(given_covers * (given_before - unit_starts)[None, :], axis=1)
    my_places = member * per_owner + jnp.arange(per_owner, dtype=jnp.int32)
    my_covers = (
        (my_places[:, None] >= order_before[None, :])
        & (my_places[:, None] < (order_before + order_lengths)[None, :])
    ).astype(jnp.int32)
    slot_seq = jnp.sum(my_covers * seq_index[None, :], axis=1)
    slot_step = my_places - jnp.sum(my_covers * order_before[None, :], axis=1)
    slot_keep = jnp.sum(my_covers * order_keep[None, :], axis=1)
    sources = jnp.arange(groups, dtype=jnp.int32)
    token_positions = (sources[:, None] + groups * slot_step[None, :]).reshape(row_count)
    sequence_id = jnp.broadcast_to(slot_seq[None, :], (groups, per_owner)).reshape(row_count)
    keep_rows = (
        jnp.broadcast_to(slot_keep[None, :], (groups, per_owner))
        .reshape(row_count, 1)
        .astype(jnp.float32)
    )
    part_tokens, part_cotangent = (
        lax.all_to_all(tokens[send_rows], "dp", split_axis=0, concat_axis=0, tiled=True),
        lax.all_to_all(cotangent[send_rows], "dp", split_axis=0, concat_axis=0, tiled=True),
    )
    owned_tokens, owned_cotangent = (
        lax.all_gather(part_tokens, "tensor", axis=1, tiled=True),
        lax.all_gather(part_cotangent, "tensor", axis=1, tiled=True),
    )
    local_heads = query_weight.shape[1] // HEAD_WIDTH
    local_kv = key_matrix.shape[1] // HEAD_WIDTH
    group_size = local_heads // local_kv
    score_scale = 1.0 / math.sqrt(HEAD_WIDTH)
    tensor_member = lax.axis_index("tensor")
    inputs = owned_tokens.astype(jnp.float32)

    def all_sum(values):
        part = lax.psum_scatter(
            values.astype(jnp.bfloat16), "tensor", scatter_dimension=1, tiled=True
        )
        return lax.all_gather(part, "tensor", axis=1, tiled=True).astype(jnp.float32)

    def my_part(values):
        return lax.dynamic_slice_in_dim(values, tensor_member * width_part, width_part, 1)

    scale_one = lax.rsqrt(jnp.mean(inputs * inputs, axis=1, keepdims=True) + eps)
    normed_one = (inputs * scale_one * first_gain).astype(jnp.bfloat16)
    query_pre = matmul(normed_one, query_weight)
    key_unrotated = matmul(normed_one, key_matrix)
    value_pre = matmul(normed_one, value_matrix)
    cosine, sine = rotary_tables(token_positions, HEAD_WIDTH)

    def apply_rotation(values):
        return values * cosine[:, None, :] + rotate_half(values) * sine[:, None, :]

    def unrotate(values):
        return values * cosine[:, None, :] + rotate_back(values * sine[:, None, :])

    query_four_axes = (
        apply_rotation(query_pre.reshape(row_count, local_heads, HEAD_WIDTH))
        .astype(jnp.bfloat16)
        .reshape(row_count, local_kv, group_size, HEAD_WIDTH)
    )
    key_low = apply_rotation(key_unrotated.reshape(row_count, local_kv, HEAD_WIDTH)).astype(
        jnp.bfloat16
    )
    value_low = value_pre.reshape(row_count, local_kv, HEAD_WIDTH).astype(jnp.bfloat16)
    allowed = (sequence_id[:, None] == sequence_id[None, :]) & (
        token_positions[None, :] <= token_positions[:, None]
    )

    def scores_of():
        raw = (
            jnp.einsum(
                "qcgd,kcd->cgqk", query_four_axes, key_low, preferred_element_type=jnp.float32
            )
            * score_scale
        )
        return jnp.where(allowed, raw, -1e30)

    scores = scores_of()
    highest = jnp.max(scores, axis=-1, keepdims=True)
    expo = jnp.exp(scores - highest)
    denominator = jnp.sum(expo, axis=-1, keepdims=True)
    logsum = highest + jnp.log(denominator)
    probs_low = (expo / denominator).astype(jnp.bfloat16)
    attended_rows = jnp.einsum(
        "cgqk,kcd->qcgd", probs_low, value_low, preferred_element_type=jnp.float32
    )
    attended_low = attended_rows.reshape(row_count, local_heads * HEAD_WIDTH).astype(jnp.bfloat16)
    attn_term = matmul(attended_low, output_weight)
    attn_out = all_sum(attn_term)
    hidden_res = inputs + keep_rows * attn_out
    scale_two = lax.rsqrt(jnp.mean(hidden_res * hidden_res, axis=1, keepdims=True) + eps)
    normed_two = (hidden_res * scale_two * second_gain).astype(jnp.bfloat16)
    gate = matmul(normed_two, gate_weight)
    upward = matmul(normed_two, up_weight)
    gate_sig = jax.nn.sigmoid(gate)
    silu_val = gate * gate_sig
    inner_low = (silu_val * upward).astype(jnp.bfloat16)
    ffn_term = matmul(inner_low, down_weight)
    ffn_out = lax.psum_scatter(
        ffn_term.astype(jnp.bfloat16), "tensor", scatter_dimension=1, tiled=True
    ).astype(jnp.float32)
    result = my_part(hidden_res) + keep_rows * ffn_out
    grad_out = owned_cotangent.astype(jnp.float32)
    grad_ffn = (keep_rows * grad_out).astype(jnp.bfloat16)
    grad_inner = matmul(grad_ffn, down_weight.T)
    down_grad = matmul(inner_low.T, grad_ffn)
    grad_gate = (grad_inner * upward * gate_sig * (1.0 + gate * (1.0 - gate_sig))).astype(
        jnp.bfloat16
    )
    grad_up = (grad_inner * silu_val).astype(jnp.bfloat16)
    second_term = matmul(grad_gate, gate_weight.T) + matmul(grad_up, up_weight.T)
    gate_grad = matmul(normed_two.T, grad_gate)
    up_grad = matmul(normed_two.T, grad_up)
    second_back = all_sum(second_term)
    second_gain_grad = jnp.sum(second_back * hidden_res * scale_two, axis=0)
    scaled_two = second_back * second_gain
    grad_res = (
        grad_out
        + scale_two * scaled_two
        - hidden_res * scale_two**3 * jnp.mean(scaled_two * hidden_res, axis=1, keepdims=True)
    )
    grad_attn = (keep_rows * grad_res).astype(jnp.bfloat16)
    grad_attended = matmul(grad_attn, output_weight.T)
    output_grad = matmul(attended_low.T, grad_attn)
    grad_attended_low = grad_attended.reshape(row_count, local_kv, group_size, HEAD_WIDTH).astype(
        jnp.bfloat16
    )
    probs = jnp.exp(scores_of() - logsum)
    probs_again = probs.astype(jnp.bfloat16)
    grad_value = jnp.einsum(
        "cgqk,qcgd->kcd", probs_again, grad_attended_low, preferred_element_type=jnp.float32
    )
    grad_probs = jnp.einsum(
        "qcgd,kcd->cgqk", grad_attended_low, value_low, preferred_element_type=jnp.float32
    )
    grad_scores = (
        probs * (grad_probs - jnp.sum(probs * grad_probs, axis=-1, keepdims=True))
    ).astype(jnp.bfloat16)
    grad_query = (
        jnp.einsum("cgqk,kcd->qcgd", grad_scores, key_low, preferred_element_type=jnp.float32)
        * score_scale
    )
    grad_key = (
        jnp.einsum(
            "cgqk,qcgd->kcd", grad_scores, query_four_axes, preferred_element_type=jnp.float32
        )
        * score_scale
    )
    grad_query_low = (
        unrotate(grad_query.reshape(row_count, local_heads, HEAD_WIDTH))
        .reshape(row_count, local_heads * HEAD_WIDTH)
        .astype(jnp.bfloat16)
    )
    grad_key_low = unrotate(grad_key).reshape(row_count, local_kv * HEAD_WIDTH).astype(jnp.bfloat16)
    grad_value_low = grad_value.reshape(row_count, local_kv * HEAD_WIDTH).astype(jnp.bfloat16)
    first_back = lax.psum_scatter(
        (matmul(grad_query_low, query_weight.T)
        + matmul(grad_key_low, key_matrix.T)
        + matmul(grad_value_low, value_matrix.T)).astype(jnp.bfloat16),
        "tensor",
        scatter_dimension=1,
        tiled=True,
    ).astype(jnp.float32)
    query_grad = matmul(normed_one.T, grad_query_low)
    key_grad = matmul(normed_one.T, grad_key_low)
    value_grad = matmul(normed_one.T, grad_value_low)
    my_inputs = my_part(inputs)
    first_gain_part = jnp.sum(first_back * my_inputs * scale_one, axis=0)
    scaled_one = first_back * lax.dynamic_slice_in_dim(
        first_gain, tensor_member * width_part, width_part, 0
    )
    along = lax.psum(jnp.sum(scaled_one * my_inputs, axis=1, keepdims=True), "tensor") / inputs.shape[1]
    grad_in = my_part(grad_res) + scale_one * scaled_one - my_inputs * scale_one**3 * along
    out_part = result.astype(jnp.bfloat16)
    grad_part = grad_in.astype(jnp.bfloat16)
    first_gain_grad = lax.all_gather(first_gain_part, "tensor", axis=0, tiled=True)
    back_out, back_grad = (
        lax.all_to_all(out_part, "dp", split_axis=0, concat_axis=0, tiled=True),
        lax.all_to_all(grad_part, "dp", split_axis=0, concat_axis=0, tiled=True),
    )
    layer_output = back_out[slot_of]
    input_grad = back_grad[slot_of]
    gradient_set = (
        first_gain_grad,
        query_grad,
        key_grad,
        value_grad,
        output_grad,
        gate_grad,
        up_grad,
        down_grad,
        second_gain_grad,
    )
    by_width = [gradient_set[k] for k in (1, 2, 3, 5, 6)] + [gradient_set[k].T for k in (4, 7)]
    gains = jnp.stack([first_gain_grad, second_gain_grad], axis=1)
    joined = jnp.concatenate([g.astype(jnp.bfloat16) for g in by_width] + [gains.astype(jnp.bfloat16)], axis=1)
    shared = lax.psum_scatter(joined, "dp", scatter_dimension=0, tiled=True).astype(jnp.float32)
    cuts, at = [], 0
    for g in by_width:
        cuts.append(shared[:, at : at + g.shape[1]])
        at += g.shape[1]
    summed = (
        shared[:, at],
        cuts[0],
        cuts[1],
        cuts[2],
        cuts[5].T,
        cuts[3],
        cuts[4],
        cuts[6].T,
        shared[:, at + 1],
    )
    return (
        layer_output,
        input_grad,
        summed[0],
        summed[1],
        summed[2],
        summed[3],
        summed[4],
        summed[8],
        summed[5],
        summed[6],
        summed[7],
    )


def solution(mesh):
    placed = (
        P(None, ("dp", "tensor")),
        P(None, ("dp", "tensor")),
        P(),
        P(None, "tensor"),
        P(None, "tensor"),
        P(None, "tensor"),
        P("tensor", None),
        P(),
        P(None, "tensor"),
        P(None, "tensor"),
        P("tensor", None),
        P(),
        P(),
        P(),
    )
    return jax.shard_map(
        per_device,
        mesh=mesh,
        in_specs=placed,
        out_specs=(
            P(None, ("dp", "tensor")),
            P(None, ("dp", "tensor")),
            P("dp"),
            P("dp", "tensor"),
            P("dp", "tensor"),
            P("dp", "tensor"),
            P("tensor", "dp"),
            P("dp"),
            P("dp", "tensor"),
            P("dp", "tensor"),
            P("tensor", "dp"),
        ),
        check_vma=False,
    )
```

```python
import functools
import math

import jax
import jax.numpy as jnp
from jax import lax
from jax.experimental import pallas as pl
from jax.experimental.pallas import tpu as pltpu
from jax.sharding import PartitionSpec as P

HEAD_WIDTH = 128

MESH = pl.DeviceIdType.MESH
VM = pl.BlockSpec(memory_space=pltpu.VMEM)
F32 = jnp.float32
BF = jnp.bfloat16

def neighbour_barrier(z, n, axis):
    barrier = pltpu.get_barrier_semaphore()
    @pl.when(z > 0)
    def _():
        pl.semaphore_signal(barrier, inc=1, device_id={axis: z - 1}, device_id_type=MESH)
    @pl.when(z < n - 1)
    def _():
        pl.semaphore_signal(barrier, inc=1, device_id={axis: z + 1}, device_id_type=MESH)
    ends = jnp.where(z > 0, 1, 0) + jnp.where(z < n - 1, 1, 0)
    pl.semaphore_wait(barrier, ends)

def rcopy(src, dst, ss, rs, dev):
    return pltpu.make_async_remote_copy(src_ref=src, dst_ref=dst, send_sem=ss, recv_sem=rs, device_id={"tensor": dev}, device_id_type=MESH)

def ar_kernel(n, R, lag, part, out, upin, upout, us, ur, ds, dr):
    z = lax.axis_index("tensor")
    rows = part.shape[0]; half = rows // 2; C = half // R
    neighbour_barrier(z, n, "tensor")
    def body(t, _):
        for f in range(2):
            p = z if f == 0 else n - 1 - z
            step = 1 if f == 0 else -1
            c = t - lag * p
            @pl.when((c >= 0) & (c < C))
            def _():
                r = pl.ds(pl.multiple_of(f * half + c * R, R), R)
                @pl.when(p == 0)
                def _():
                    rcopy(part.at[r], upin.at[r], us.at[f, c], ur.at[f, c], z + step).start()
                @pl.when(p > 0)
                def _():
                    rcopy(upin.at[r], upin.at[r], us.at[f, c], ur.at[f, c], z).wait_recv()
                    s = (part[r, :].astype(F32) + upin[r, :].astype(F32)).astype(BF)
                    @pl.when(p < n - 1)
                    def _():
                        upout[r, :] = s
                        rcopy(upout.at[r], upin.at[r], us.at[f, c], ur.at[f, c], z + step).start()
                    @pl.when(p == n - 1)
                    def _():
                        out[r, :] = s
                        rcopy(out.at[r], out.at[r], ds.at[f, c], dr.at[f, c], z - step).start()
        for f in range(2):
            p = z if f == 0 else n - 1 - z
            step = 1 if f == 0 else -1
            c = t - lag * (2 * (n - 1) - p)
            @pl.when((c >= 0) & (c < C) & (p < n - 1))
            def _():
                r = pl.ds(pl.multiple_of(f * half + c * R, R), R)
                rcopy(out.at[r], out.at[r], ds.at[f, c], dr.at[f, c], z).wait_recv()
                @pl.when(p > 0)
                def _():
                    rcopy(out.at[r], out.at[r], ds.at[f, c], dr.at[f, c], z - step).start()
        return 0
    lax.fori_loop(0, C + 2 * lag * (n - 1), body, 0)
    def drain(c, _):
        for f in range(2):
            p = z if f == 0 else n - 1 - z
            r = pl.ds(pl.multiple_of(f * half + c * R, R), R)
            @pl.when(p < n - 1)
            def _():
                rcopy(upout.at[r], upin.at[r], us.at[f, c], ur.at[f, c], z).wait_send()
            @pl.when(p > 0)
            def _():
                rcopy(out.at[r], out.at[r], ds.at[f, c], dr.at[f, c], z).wait_send()
        return 0
    lax.fori_loop(0, C, drain, 0)

def ar(part, n, R=32, lag=5, cid=3):
    rows, w = part.shape
    C = rows // 2 // R
    return pl.pallas_call(
        functools.partial(ar_kernel, n, R, lag),
        out_shape=jax.ShapeDtypeStruct((rows, w), BF),
        in_specs=[VM], out_specs=VM,
        scratch_shapes=[pltpu.VMEM((rows, w), BF), pltpu.VMEM((rows, w), BF)] + [pltpu.SemaphoreType.DMA((2, C))] * 4,
        compiler_params=pltpu.CompilerParams(collective_id=cid, has_side_effects=True, vmem_limit_bytes=60 << 20),
    )(part)

def rs_kernel(n, R, lag, part, out, right, left, ss, rs):
    z = lax.axis_index("tensor")
    rows, w = out.shape; C = rows // R
    neighbour_barrier(z, n, "tensor")
    def at(ref, c, b):
        return ref.at[pl.ds(pl.multiple_of(c * R, R), R), pl.ds(b * w, w)]
    def body(t, _):
        for d, buf, step in ((0, right, 1), (1, left, -1)):
            p = z if d == 0 else n - 1 - z
            c = t - lag * p
            @pl.when((c >= 0) & (c < C))
            def _():
                r = pl.ds(pl.multiple_of(c * R, R), R)
                for b in (range(n - 1, 0, -1) if d == 0 else range(n - 1)):
                    on = (b > z) if d == 0 else (b < z)
                    k = pl.ds(b * w, w)
                    @pl.when(on)
                    def _():
                        @pl.when(p == 0)
                        def _():
                            rcopy(at(part, c, b), at(buf, c, b), ss.at[d, b, c], rs.at[d, b, c], z + step).start()
                        @pl.when(p > 0)
                        def _():
                            rcopy(at(buf, c, b), at(buf, c, b), ss.at[d, b, c], rs.at[d, b, c], z).wait_recv()
                            buf[r, k] = (part[r, k].astype(F32) + buf[r, k].astype(F32)).astype(BF)
                            rcopy(at(buf, c, b), at(buf, c, b), ss.at[d, b, c], rs.at[d, b, c], z + step).start()
        c = t - lag * (n - 1)
        @pl.when((c >= 0) & (c < C))
        def _():
            r = pl.ds(pl.multiple_of(c * R, R), R)
            for b in range(n):
                k = pl.ds(b * w, w)
                @pl.when(z == b)
                def _():
                    s = part[r, k].astype(F32)
                    if b > 0:
                        rcopy(at(right, c, b), at(right, c, b), ss.at[0, b, c], rs.at[0, b, c], z).wait_recv()
                        s = s + right[r, k].astype(F32)
                    if b < n - 1:
                        rcopy(at(left, c, b), at(left, c, b), ss.at[1, b, c], rs.at[1, b, c], z).wait_recv()
                        s = s + left[r, k].astype(F32)
                    out[r, :] = s.astype(BF)
        return 0
    lax.fori_loop(0, C + lag * (n - 1), body, 0)
    def drain(c, _):
        for d, buf in ((0, right), (1, left)):
            for b in range(n):
                @pl.when((b > z) if d == 0 else (b < z))
                def _():
                    rcopy(at(buf, c, b), at(buf, c, b), ss.at[d, b, c], rs.at[d, b, c], z).wait_send()
        return 0
    lax.fori_loop(0, C, drain, 0)

def rs(part, n, R=64, lag=1, cid=5):
    rows, nw = part.shape
    w = nw // n
    C = rows // R
    return pl.pallas_call(
        functools.partial(rs_kernel, n, R, lag),
        out_shape=jax.ShapeDtypeStruct((rows, w), BF),
        in_specs=[VM], out_specs=VM,
        scratch_shapes=[pltpu.VMEM((rows, nw), BF), pltpu.VMEM((rows, nw), BF)] + [pltpu.SemaphoreType.DMA((2, n, C))] * 2,
        compiler_params=pltpu.CompilerParams(collective_id=cid, has_side_effects=True, vmem_limit_bytes=60 << 20),
    )(part)


eps = 1e-05
rope_base = 10000.0


def rotary_tables(token_positions, head_size):
    half = head_size // 2
    freqs = rope_base ** (-(jnp.arange(half).astype(jnp.float32) * 2.0) / head_size)
    angles = token_positions.astype(jnp.float32)[:, None] * freqs[None, :]
    angles = jnp.concatenate([angles, angles], axis=1)
    return (jnp.cos(angles), jnp.sin(angles))


def rotate_half(values):
    half = values.shape[-1] // 2
    return jnp.concatenate([-values[..., half:], values[..., :half]], axis=-1)


def rotate_back(values):
    half = values.shape[-1] // 2
    return jnp.concatenate([values[..., half:], -values[..., :half]], axis=-1)


def matmul(left, right):
    return jnp.dot(left, right, preferred_element_type=jnp.float32)


def per_device(
    tokens,
    cotangent,
    first_gain,
    query_weight,
    key_matrix,
    value_matrix,
    output_weight,
    second_gain,
    gate_weight,
    up_weight,
    down_weight,
    seq_lengths,
    owner_order,
    skip_mask,
):
    groups = lax.axis_size("dp")
    member = lax.axis_index("dp")
    width_part = tokens.shape[1]
    row_count = tokens.shape[0]
    per_owner = row_count // groups
    seq_count = seq_lengths.shape[0]
    seq_index = jnp.arange(seq_count, dtype=jnp.int32)
    before = (seq_index[None, :] < seq_index[:, None]).astype(jnp.int32)
    unit_lengths = seq_lengths // groups
    unit_starts = jnp.sum(before * unit_lengths[None, :], axis=1)
    placed = (owner_order[:, None] == seq_index[None, :]).astype(jnp.int32)
    order_lengths = jnp.sum(placed * unit_lengths[None, :], axis=1)
    order_starts = jnp.sum(placed * unit_starts[None, :], axis=1)
    order_keep = jnp.sum(placed * skip_mask[None, :], axis=1)
    order_before = jnp.sum(before * order_lengths[None, :], axis=1)
    places = jnp.arange(row_count, dtype=jnp.int32)
    covers = (
        (places[:, None] >= order_before[None, :])
        & (places[:, None] < (order_before + order_lengths)[None, :])
    ).astype(jnp.int32)
    send_rows = places + jnp.sum(covers * (order_starts - order_before)[None, :], axis=1)
    given_before = jnp.sum(placed * order_before[:, None], axis=0)
    given_covers = (
        (places[:, None] >= unit_starts[None, :])
        & (places[:, None] < (unit_starts + unit_lengths)[None, :])
    ).astype(jnp.int32)
    slot_of = places + jnp.sum(given_covers * (given_before - unit_starts)[None, :], axis=1)
    my_places = member * per_owner + jnp.arange(per_owner, dtype=jnp.int32)
    my_covers = (
        (my_places[:, None] >= order_before[None, :])
        & (my_places[:, None] < (order_before + order_lengths)[None, :])
    ).astype(jnp.int32)
    slot_seq = jnp.sum(my_covers * seq_index[None, :], axis=1)
    slot_step = my_places - jnp.sum(my_covers * order_before[None, :], axis=1)
    slot_keep = jnp.sum(my_covers * order_keep[None, :], axis=1)
    sources = jnp.arange(groups, dtype=jnp.int32)
    token_positions = (sources[:, None] + groups * slot_step[None, :]).reshape(row_count)
    sequence_id = jnp.broadcast_to(slot_seq[None, :], (groups, per_owner)).reshape(row_count)
    keep_rows = (
        jnp.broadcast_to(slot_keep[None, :], (groups, per_owner))
        .reshape(row_count, 1)
        .astype(jnp.float32)
    )
    part_tokens, part_cotangent = (
        lax.all_to_all(tokens[send_rows], "dp", split_axis=0, concat_axis=0, tiled=True),
        lax.all_to_all(cotangent[send_rows], "dp", split_axis=0, concat_axis=0, tiled=True),
    )
    owned_tokens, owned_cotangent = (
        lax.all_gather(part_tokens, "tensor", axis=1, tiled=True),
        lax.all_gather(part_cotangent, "tensor", axis=1, tiled=True),
    )
    local_heads = query_weight.shape[1] // HEAD_WIDTH
    local_kv = key_matrix.shape[1] // HEAD_WIDTH
    group_size = local_heads // local_kv
    score_scale = 1.0 / math.sqrt(HEAD_WIDTH)
    tensor_member = lax.axis_index("tensor")
    inputs = owned_tokens.astype(jnp.float32)

    ids = iter((3, 4))

    def all_sum(values):
        return ar(values.astype(jnp.bfloat16), lax.axis_size("tensor"), cid=next(ids)).astype(
            jnp.float32
        )

    def my_part(values):
        return lax.dynamic_slice_in_dim(values, tensor_member * width_part, width_part, 1)

    scale_one = lax.rsqrt(jnp.mean(inputs * inputs, axis=1, keepdims=True) + eps)
    normed_one = (inputs * scale_one * first_gain).astype(jnp.bfloat16)
    query_pre = matmul(normed_one, query_weight)
    key_unrotated = matmul(normed_one, key_matrix)
    value_pre = matmul(normed_one, value_matrix)
    cosine, sine = rotary_tables(token_positions, HEAD_WIDTH)

    def apply_rotation(values):
        return values * cosine[:, None, :] + rotate_half(values) * sine[:, None, :]

    def unrotate(values):
        return values * cosine[:, None, :] + rotate_back(values * sine[:, None, :])

    query_four_axes = (
        apply_rotation(query_pre.reshape(row_count, local_heads, HEAD_WIDTH))
        .astype(jnp.bfloat16)
        .reshape(row_count, local_kv, group_size, HEAD_WIDTH)
    )
    key_low = apply_rotation(key_unrotated.reshape(row_count, local_kv, HEAD_WIDTH)).astype(
        jnp.bfloat16
    )
    value_low = value_pre.reshape(row_count, local_kv, HEAD_WIDTH).astype(jnp.bfloat16)
    allowed = (sequence_id[:, None] == sequence_id[None, :]) & (
        token_positions[None, :] <= token_positions[:, None]
    )

    def scores_of():
        raw = (
            jnp.einsum(
                "qcgd,kcd->cgqk", query_four_axes, key_low, preferred_element_type=jnp.float32
            )
            * score_scale
        )
        return jnp.where(allowed, raw, -1e30)

    scores = scores_of()
    highest = jnp.max(scores, axis=-1, keepdims=True)
    expo = jnp.exp(scores - highest)
    denominator = jnp.sum(expo, axis=-1, keepdims=True)
    logsum = highest + jnp.log(denominator)
    probs_low = (expo / denominator).astype(jnp.bfloat16)
    attended_rows = jnp.einsum(
        "cgqk,kcd->qcgd", probs_low, value_low, preferred_element_type=jnp.float32
    )
    attended_low = attended_rows.reshape(row_count, local_heads * HEAD_WIDTH).astype(jnp.bfloat16)
    attn_term = matmul(attended_low, output_weight)
    attn_out = all_sum(attn_term)
    hidden_res = inputs + keep_rows * attn_out
    scale_two = lax.rsqrt(jnp.mean(hidden_res * hidden_res, axis=1, keepdims=True) + eps)
    normed_two = (hidden_res * scale_two * second_gain).astype(jnp.bfloat16)
    gate = matmul(normed_two, gate_weight)
    upward = matmul(normed_two, up_weight)
    gate_sig = jax.nn.sigmoid(gate)
    silu_val = gate * gate_sig
    inner_low = (silu_val * upward).astype(jnp.bfloat16)
    ffn_term = matmul(inner_low, down_weight)
    ffn_out = lax.psum_scatter(
        ffn_term.astype(jnp.bfloat16), "tensor", scatter_dimension=1, tiled=True
    ).astype(jnp.float32)
    result = my_part(hidden_res) + keep_rows * ffn_out
    grad_out = owned_cotangent.astype(jnp.float32)
    grad_ffn = (keep_rows * grad_out).astype(jnp.bfloat16)
    grad_inner = matmul(grad_ffn, down_weight.T)
    down_grad = matmul(grad_ffn.T, inner_low)
    grad_gate = (grad_inner * upward * gate_sig * (1.0 + gate * (1.0 - gate_sig))).astype(
        jnp.bfloat16
    )
    grad_up = (grad_inner * silu_val).astype(jnp.bfloat16)
    second_term = matmul(grad_gate, gate_weight.T) + matmul(grad_up, up_weight.T)
    gate_grad = matmul(normed_two.T, grad_gate)
    up_grad = matmul(normed_two.T, grad_up)
    second_back = all_sum(second_term)
    second_gain_grad = jnp.sum(second_back * hidden_res * scale_two, axis=0)
    scaled_two = second_back * second_gain
    grad_res = (
        grad_out
        + scale_two * scaled_two
        - hidden_res * scale_two**3 * jnp.mean(scaled_two * hidden_res, axis=1, keepdims=True)
    )
    grad_attn = (keep_rows * grad_res).astype(jnp.bfloat16)
    grad_attended = matmul(grad_attn, output_weight.T)
    output_grad = matmul(grad_attn.T, attended_low)
    grad_attended_low = grad_attended.reshape(row_count, local_kv, group_size, HEAD_WIDTH).astype(
        jnp.bfloat16
    )
    probs = jnp.exp(scores_of() - logsum)
    probs_again = probs.astype(jnp.bfloat16)
    grad_value = jnp.einsum(
        "cgqk,qcgd->kcd", probs_again, grad_attended_low, preferred_element_type=jnp.float32
    )
    grad_probs = jnp.einsum(
        "qcgd,kcd->cgqk", grad_attended_low, value_low, preferred_element_type=jnp.float32
    )
    grad_scores = (
        probs * (grad_probs - jnp.sum(probs * grad_probs, axis=-1, keepdims=True))
    ).astype(jnp.bfloat16)
    grad_query = (
        jnp.einsum("cgqk,kcd->qcgd", grad_scores, key_low, preferred_element_type=jnp.float32)
        * score_scale
    )
    grad_key = (
        jnp.einsum(
            "cgqk,qcgd->kcd", grad_scores, query_four_axes, preferred_element_type=jnp.float32
        )
        * score_scale
    )
    grad_query_low = (
        unrotate(grad_query.reshape(row_count, local_heads, HEAD_WIDTH))
        .reshape(row_count, local_heads * HEAD_WIDTH)
        .astype(jnp.bfloat16)
    )
    grad_key_low = unrotate(grad_key).reshape(row_count, local_kv * HEAD_WIDTH).astype(jnp.bfloat16)
    grad_value_low = grad_value.reshape(row_count, local_kv * HEAD_WIDTH).astype(jnp.bfloat16)
    first_back = rs(
        (
            matmul(grad_query_low, query_weight.T)
            + matmul(grad_key_low, key_matrix.T)
            + matmul(grad_value_low, value_matrix.T)
        ).astype(jnp.bfloat16),
        lax.axis_size("tensor"),
    ).astype(jnp.float32)
    query_grad = matmul(normed_one.T, grad_query_low)
    key_grad = matmul(normed_one.T, grad_key_low)
    value_grad = matmul(normed_one.T, grad_value_low)
    my_inputs = my_part(inputs)
    first_gain_part = jnp.sum(first_back * my_inputs * scale_one, axis=0)
    scaled_one = first_back * lax.dynamic_slice_in_dim(
        first_gain, tensor_member * width_part, width_part, 0
    )
    along = lax.psum(jnp.sum(scaled_one * my_inputs, axis=1, keepdims=True), "tensor") / inputs.shape[1]
    grad_in = my_part(grad_res) + scale_one * scaled_one - my_inputs * scale_one**3 * along
    out_part = result.astype(jnp.bfloat16)
    grad_part = grad_in.astype(jnp.bfloat16)
    first_gain_grad = lax.all_gather(first_gain_part, "tensor", axis=0, tiled=True)
    back_out, back_grad = (
        lax.all_to_all(out_part, "dp", split_axis=0, concat_axis=0, tiled=True),
        lax.all_to_all(grad_part, "dp", split_axis=0, concat_axis=0, tiled=True),
    )
    layer_output = back_out[slot_of]
    input_grad = back_grad[slot_of]
    gradient_set = (
        first_gain_grad,
        query_grad,
        key_grad,
        value_grad,
        output_grad,
        gate_grad,
        up_grad,
        down_grad,
        second_gain_grad,
    )
    def shared(*values):
        low = [v.astype(jnp.bfloat16) for v in values]
        joined = jnp.concatenate(low, axis=1) if len(low) > 1 else low[0]
        return lax.psum_scatter(joined, "dp", scatter_dimension=0, tiled=True).astype(jnp.float32)

    gate_share, up_share, down_share, output_share = map(
        shared, (gate_grad, up_grad, down_grad, output_grad)
    )
    first = shared(
        query_grad, key_grad, value_grad, first_gain_grad[:, None], second_gain_grad[:, None]
    )
    a = query_grad.shape[1]
    b = a + key_grad.shape[1]
    c = b + value_grad.shape[1]
    summed = (
        first[:, c],
        first[:, :a],
        first[:, a:b],
        first[:, b:c],
        output_share.T,
        gate_share,
        up_share,
        down_share.T,
        first[:, c + 1],
    )
    return (
        layer_output,
        input_grad,
        summed[0],
        summed[1],
        summed[2],
        summed[3],
        summed[4],
        summed[8],
        summed[5],
        summed[6],
        summed[7],
    )


def solution(mesh):
    placed = (
        P(None, ("dp", "tensor")),
        P(None, ("dp", "tensor")),
        P(),
        P(None, "tensor"),
        P(None, "tensor"),
        P(None, "tensor"),
        P("tensor", None),
        P(),
        P(None, "tensor"),
        P(None, "tensor"),
        P("tensor", None),
        P(),
        P(),
        P(),
    )
    return jax.shard_map(
        per_device,
        mesh=mesh,
        in_specs=placed,
        out_specs=(
            P(None, ("dp", "tensor")),
            P(None, ("dp", "tensor")),
            P("dp"),
            P("dp", "tensor"),
            P("dp", "tensor"),
            P("dp", "tensor"),
            P("tensor", "dp"),
            P("dp"),
            P("dp", "tensor"),
            P("dp", "tensor"),
            P("tensor", "dp"),
        ),
        check_vma=False,
    )
```

```python
import functools
import math

import jax
import jax.numpy as jnp
from jax import lax
from jax.experimental import pallas as pl
from jax.experimental.pallas import tpu as pltpu
from jax.sharding import PartitionSpec as P

HEAD_WIDTH = 128

MESH = pl.DeviceIdType.MESH
VM = pl.BlockSpec(memory_space=pltpu.VMEM)
F32 = jnp.float32
BF = jnp.bfloat16

def neighbour_barrier(z, n, axis):
    barrier = pltpu.get_barrier_semaphore()
    @pl.when(z > 0)
    def _():
        pl.semaphore_signal(barrier, inc=1, device_id={axis: z - 1}, device_id_type=MESH)
    @pl.when(z < n - 1)
    def _():
        pl.semaphore_signal(barrier, inc=1, device_id={axis: z + 1}, device_id_type=MESH)
    ends = jnp.where(z > 0, 1, 0) + jnp.where(z < n - 1, 1, 0)
    pl.semaphore_wait(barrier, ends)

def rcopy(src, dst, ss, rs, dev):
    return pltpu.make_async_remote_copy(src_ref=src, dst_ref=dst, send_sem=ss, recv_sem=rs, device_id={"tensor": dev}, device_id_type=MESH)

def rs_kernel(n, R, lag, part, out, right, left, ss, rs):
    z = lax.axis_index("tensor")
    rows, w = out.shape; C = rows // R
    neighbour_barrier(z, n, "tensor")
    def at(ref, c, b):
        return ref.at[pl.ds(pl.multiple_of(c * R, R), R), pl.ds(b * w, w)]
    def body(t, _):
        for d, buf, step in ((0, right, 1), (1, left, -1)):
            p = z if d == 0 else n - 1 - z
            c = t - lag * p
            @pl.when((c >= 0) & (c < C))
            def _():
                r = pl.ds(pl.multiple_of(c * R, R), R)
                for b in (range(n - 1, 0, -1) if d == 0 else range(n - 1)):
                    on = (b > z) if d == 0 else (b < z)
                    k = pl.ds(b * w, w)
                    @pl.when(on)
                    def _():
                        @pl.when(p == 0)
                        def _():
                            rcopy(at(part, c, b), at(buf, c, b), ss.at[d, b, c], rs.at[d, b, c], z + step).start()
                        @pl.when(p > 0)
                        def _():
                            rcopy(at(buf, c, b), at(buf, c, b), ss.at[d, b, c], rs.at[d, b, c], z).wait_recv()
                            buf[r, k] = (part[r, k].astype(F32) + buf[r, k].astype(F32)).astype(BF)
                            rcopy(at(buf, c, b), at(buf, c, b), ss.at[d, b, c], rs.at[d, b, c], z + step).start()
        c = t - lag * (n - 1)
        @pl.when((c >= 0) & (c < C))
        def _():
            r = pl.ds(pl.multiple_of(c * R, R), R)
            for b in range(n):
                k = pl.ds(b * w, w)
                @pl.when(z == b)
                def _():
                    s = part[r, k].astype(F32)
                    if b > 0:
                        rcopy(at(right, c, b), at(right, c, b), ss.at[0, b, c], rs.at[0, b, c], z).wait_recv()
                        s = s + right[r, k].astype(F32)
                    if b < n - 1:
                        rcopy(at(left, c, b), at(left, c, b), ss.at[1, b, c], rs.at[1, b, c], z).wait_recv()
                        s = s + left[r, k].astype(F32)
                    out[r, :] = s.astype(BF)
        return 0
    lax.fori_loop(0, C + lag * (n - 1), body, 0)
    def drain(c, _):
        for d, buf in ((0, right), (1, left)):
            for b in range(n):
                @pl.when((b > z) if d == 0 else (b < z))
                def _():
                    rcopy(at(buf, c, b), at(buf, c, b), ss.at[d, b, c], rs.at[d, b, c], z).wait_send()
        return 0
    lax.fori_loop(0, C, drain, 0)

def rs(part, n, R=64, lag=1, cid=5):
    rows, nw = part.shape
    w = nw // n
    C = rows // R
    return pl.pallas_call(
        functools.partial(rs_kernel, n, R, lag),
        out_shape=jax.ShapeDtypeStruct((rows, w), BF),
        in_specs=[VM], out_specs=VM,
        scratch_shapes=[pltpu.VMEM((rows, nw), BF), pltpu.VMEM((rows, nw), BF)] + [pltpu.SemaphoreType.DMA((2, n, C))] * 2,
        compiler_params=pltpu.CompilerParams(collective_id=cid, has_side_effects=True, vmem_limit_bytes=60 << 20),
    )(part)


eps = 1e-05
rope_base = 10000.0


def nt(left, right):
    return lax.dot_general(left, right, (((1,), (1,)), ((), ())), preferred_element_type=F32)


def tn(left, right):
    return lax.dot_general(left, right, (((0,), (0,)), ((), ())), preferred_element_type=F32)


def mm(left, right):
    return jnp.dot(left, right, preferred_element_type=F32)


def spin(values, cosine, signed_sine):
    return values * cosine + pltpu.roll(values, HEAD_WIDTH // 2, 1) * signed_sine


def visible(code_row, code_col, low_col):
    return jnp.where((code_row <= code_col) & (code_row >= low_col), 0.0, -1e30)


def attend_kernel(tiles, x, gain, wq, wk, wv, wo, cosine, sine, code_row, code_col, low_col,
                  part, normed, q, k, v, o, lse):
    rows = x.shape[0]
    tile = rows // tiles
    heads = wq.shape[1] // HEAD_WIDTH
    kv = wk.shape[1] // HEAD_WIDTH
    group = heads // kv
    factor = math.log2(math.e) / math.sqrt(HEAD_WIDTH)
    for t in range(tiles):
        r = pl.ds(t * tile, tile)
        xt = x[r, :].astype(F32)
        scale = lax.rsqrt(jnp.mean(xt * xt, axis=1, keepdims=True) + eps)
        n1 = (xt * scale * gain[...]).astype(BF)
        normed[r, :] = n1
        c, s = cosine[r, :], sine[r, :]
        pre = mm(n1, wq[...])
        for h in range(heads):
            cut = slice(h * HEAD_WIDTH, (h + 1) * HEAD_WIDTH)
            q[r, cut] = spin(pre[:, cut], c, s).astype(BF)
        pre = mm(n1, wk[...])
        for h in range(kv):
            cut = slice(h * HEAD_WIDTH, (h + 1) * HEAD_WIDTH)
            k[r, cut] = spin(pre[:, cut], c, s).astype(BF)
        v[r, :] = mm(n1, wv[...]).astype(BF)
        seen = (t + 1) * tile
        bias = visible(code_row[:, :seen], code_col[r, :], low_col[r, :])
        logs = []
        for h in range(heads):
            cut = slice(h * HEAD_WIDTH, (h + 1) * HEAD_WIDTH)
            mine = slice(h // group * HEAD_WIDTH, (h // group + 1) * HEAD_WIDTH)
            scores = nt(q[r, cut], k[:seen, mine]) * factor + bias
            top = jnp.max(scores, axis=1, keepdims=True)
            expo = jnp.exp2(scores - top)
            total = jnp.sum(expo, axis=1, keepdims=True)
            probs = (expo * (1.0 / total)).astype(BF)
            o[r, cut] = mm(probs, v[:seen, mine]).astype(BF)
            logs.append(top + jnp.log2(total))
        lse[r, :] = jnp.concatenate(logs, axis=1)
        part[r, :] = mm(o[r, :], wo[...]).astype(BF)


def attend(tiles, x, gain, wq, wk, wv, wo, *tables):
    rows, width = x.shape
    heads = wq.shape[1] // HEAD_WIDTH
    shapes = [(rows, width), (rows, width), (rows, wq.shape[1]), (rows, wk.shape[1]), (rows, wv.shape[1]), (rows, wq.shape[1])]
    return pl.pallas_call(
        functools.partial(attend_kernel, tiles),
        out_shape=[jax.ShapeDtypeStruct(s, BF) for s in shapes] + [jax.ShapeDtypeStruct((rows, heads), F32)],
        in_specs=[VM] * 11,
        out_specs=[VM] * 7,
        compiler_params=pltpu.CompilerParams(vmem_limit_bytes=56 << 20),
    )(x, gain, wq, wk, wv, wo, *tables)


def attend_back_kernel(tiles, ga, wq, wk, wv, wo, q, k, v, o, lse, cosine, sine, code_row, code_col, low_col,
                       part, dqkv, dk, dv):
    rows = ga.shape[0]
    tile = rows // tiles
    heads = wq.shape[1] // HEAD_WIDTH
    kv = wk.shape[1] // HEAD_WIDTH
    group = heads // kv
    wide = heads * HEAD_WIDTH
    narrow = kv * HEAD_WIDTH
    score_scale = 1.0 / math.sqrt(HEAD_WIDTH)
    factor = math.log2(math.e) / math.sqrt(HEAD_WIDTH)
    for t in range(tiles):
        r = pl.ds(t * tile, tile)
        do = nt(ga[r, :], wo[...]).astype(BF)
        c, s = cosine[r, :], sine[r, :]
        seen = (t + 1) * tile
        bias = visible(code_row[:, :seen], code_col[r, :], low_col[r, :])
        logs = lse[r, :]
        for h in range(heads):
            cut = slice(h * HEAD_WIDTH, (h + 1) * HEAD_WIDTH)
            mine = slice(h // group * HEAD_WIDTH, (h // group + 1) * HEAD_WIDTH)
            do_h = do[:, cut]
            qh = q[r, cut]
            probs = jnp.exp2(nt(qh, k[:seen, mine]) * factor + bias - logs[:, h : h + 1])
            along = jnp.sum(do_h.astype(F32) * o[r, cut].astype(F32), axis=1, keepdims=True)
            ds = (probs * (nt(do_h, v[:seen, mine]) - along)).astype(BF)
            pb = probs.astype(BF)
            dq = mm(ds, k[:seen, mine]) * score_scale
            dqkv[r, cut] = spin(dq, c, -s).astype(BF)
            more_k = tn(ds, qh)
            more_v = tn(pb, do_h)
            if h % group == 0:
                if t > 0:
                    dk[: t * tile, mine] += more_k[: t * tile]
                    dv[: t * tile, mine] += more_v[: t * tile]
                dk[r, mine] = more_k[t * tile :]
                dv[r, mine] = more_v[t * tile :]
            else:
                dk[:seen, mine] += more_k
                dv[:seen, mine] += more_v
    for t in range(tiles):
        r = pl.ds(t * tile, tile)
        c, s = cosine[r, :], sine[r, :]
        for h in range(kv):
            cut = slice(h * HEAD_WIDTH, (h + 1) * HEAD_WIDTH)
            dqkv[r, wide + h * HEAD_WIDTH : wide + (h + 1) * HEAD_WIDTH] = spin(dk[r, cut] * score_scale, c, -s).astype(BF)
        dqkv[r, wide + narrow :] = dv[r, :].astype(BF)
        part[r, :] = (
            nt(dqkv[r, :wide], wq[...])
            + nt(dqkv[r, wide : wide + narrow], wk[...])
            + nt(dqkv[r, wide + narrow :], wv[...])
        ).astype(BF)


def attend_back(tiles, ga, wq, wk, wv, wo, *rest):
    rows, width = ga.shape
    joined = wq.shape[1] + wk.shape[1] + wv.shape[1]
    return pl.pallas_call(
        functools.partial(attend_back_kernel, tiles),
        out_shape=[jax.ShapeDtypeStruct((rows, width), BF), jax.ShapeDtypeStruct((rows, joined), BF)],
        in_specs=[VM] * 15,
        out_specs=[VM] * 2,
        scratch_shapes=[pltpu.VMEM((rows, wk.shape[1]), F32), pltpu.VMEM((rows, wv.shape[1]), F32)],
        compiler_params=pltpu.CompilerParams(vmem_limit_bytes=56 << 20),
    )(ga, wq, wk, wv, wo, *rest)


ANY = pl.BlockSpec(memory_space=pl.ANY)
LAG = 2
CHUNK = 32
BLOCK = 128


def line_row(f, c):
    per = BLOCK // CHUNK
    return pl.ds(pl.multiple_of(lax.div(c, per) * (2 * BLOCK) + f * BLOCK + lax.rem(c, per) * CHUNK, CHUNK), CHUNK)


def line_steps(n, rows):
    return rows // 2 // CHUNK + 2 * LAG * (n - 1)


def line_sum_step(n, z, t, part, up, out, sems):
    us, ur, ds, dr = sems
    count = part.shape[0] // 2 // CHUNK
    for f in range(2):
        p = z if f == 0 else n - 1 - z
        step = 1 if f == 0 else -1
        c = t - LAG * p

        @pl.when((c >= 0) & (c < count))
        def _():
            r = line_row(f, c)

            @pl.when(p == 0)
            def _():
                rcopy(part.at[r], up.at[r], us.at[f, c], ur.at[f, c], z + step).start()

            @pl.when(p > 0)
            def _():
                rcopy(up.at[r], up.at[r], us.at[f, c], ur.at[f, c], z).wait_recv()
                s = (part[r, :].astype(F32) + up[r, :].astype(F32)).astype(BF)

                @pl.when(p < n - 1)
                def _():
                    up[r, :] = s
                    rcopy(up.at[r], up.at[r], us.at[f, c], ur.at[f, c], z + step).start()

                @pl.when(p == n - 1)
                def _():
                    out[r, :] = s
                    rcopy(out.at[r], out.at[r], ds.at[f, c], dr.at[f, c], z - step).start()

    for f in range(2):
        p = z if f == 0 else n - 1 - z
        step = 1 if f == 0 else -1
        c = t - LAG * (2 * (n - 1) - p)

        @pl.when((c >= 0) & (c < count) & (p < n - 1))
        def _():
            r = line_row(f, c)
            rcopy(out.at[r], out.at[r], ds.at[f, c], dr.at[f, c], z).wait_recv()

            @pl.when(p > 0)
            def _():
                rcopy(out.at[r], out.at[r], ds.at[f, c], dr.at[f, c], z - step).start()


def line_sum_drain(n, z, part, up, out, sems):
    us, ur, ds, dr = sems
    count = part.shape[0] // 2 // CHUNK

    def drain(c, _):
        for f in range(2):
            p = z if f == 0 else n - 1 - z
            r = line_row(f, c)

            @pl.when(p < n - 1)
            def _():
                rcopy(up.at[r], up.at[r], us.at[f, c], ur.at[f, c], z).wait_send()

            @pl.when(p > 0)
            def _():
                rcopy(out.at[r], out.at[r], ds.at[f, c], dr.at[f, c], z).wait_send()

        return 0

    lax.fori_loop(0, count, drain, 0)


def line_sum_sems(rows):
    return [pltpu.SemaphoreType.DMA((2, rows // 2 // CHUNK))] * 4


def gather_cut(ref, o, c, w):
    return ref.at[pl.ds(pl.multiple_of(c * BLOCK, BLOCK), BLOCK), pl.ds(pl.multiple_of(o * w, w), w)]


def line_gather_step(n, z, t, src, out, ss, rs):
    rows, w = src.shape
    count = rows // BLOCK

    @pl.when(t < count)
    def _():
        mine = src.at[pl.ds(pl.multiple_of(t * BLOCK, BLOCK), BLOCK)]

        @pl.when(z < n - 1)
        def _():
            rcopy(mine, gather_cut(out, z, t, w), ss.at[0, z, t], rs.at[0, z, t], z + 1).start()

        @pl.when(z > 0)
        def _():
            rcopy(mine, gather_cut(out, z, t, w), ss.at[1, z, t], rs.at[1, z, t], z - 1).start()

    for hop in range(1, n):
        c = t - hop
        for d, step in ((0, 1), (1, -1)):
            o = z - hop * step

            @pl.when((c >= 0) & (c < count) & (o >= 0) & (o < n))
            def _():
                cut = gather_cut(out, o, c, w)
                rcopy(cut, cut, ss.at[d, o, c], rs.at[d, o, c], z).wait_recv()
                after = z + step

                @pl.when((after >= 0) & (after < n))
                def _():
                    rcopy(cut, cut, ss.at[d, o, c], rs.at[d, o, c], after).start()


def line_gather_drain(n, z, src, out, ss, rs):
    rows, w = src.shape

    def drain(c, _):
        for d in range(2):
            for o in range(n):
                on = (o <= z) & (z < n - 1) if d == 0 else (o >= z) & (z > 0)

                @pl.when(on)
                def _():
                    cut = gather_cut(out, o, c, w)
                    rcopy(cut, cut, ss.at[d, o, c], rs.at[d, o, c], z).wait_send()

        return 0

    lax.fori_loop(0, rows // BLOCK, drain, 0)


def middle_kernel(n, part, x, g_part, keep, gain, wg_far, wu_far, wd_far,
                  a_far, g_far, n2_far, inner_far, both_far, f_far, dn2_far,
                  wg, wu, wd, up, total, g, gate_s, upper_s, n2_s, inner_s, both_s, f_s, dn2_s,
                  us, ur, ds, dr, ss, rs, load, own, save, late):
    z = lax.axis_index("tensor")
    rows, width = part.shape
    w = g_part.shape[1]
    hidden = wg.shape[1]
    tile = 2 * BLOCK
    sums = (us, ur, ds, dr)
    loads = [pltpu.make_async_copy(a, b, load.at[i]) for i, (a, b) in enumerate(((wg_far, wg), (wu_far, wu), (wd_far, wd)))]
    for copy in loads:
        copy.start()
    mine = pltpu.make_async_copy(g_part, g.at[:, pl.ds(pl.multiple_of(z * w, w), w)], own)
    mine.start()
    neighbour_barrier(z, n, "tensor")

    def saves(d):
        r = pl.ds(pl.multiple_of(d * tile, tile), tile)
        pairs = ((n2_s, n2_far), (inner_s, inner_far), (both_s, both_far), (f_s, f_far), (dn2_s, dn2_far))
        return [pltpu.make_async_copy(a, b.at[r], save.at[i]) for i, (a, b) in enumerate(pairs)]

    first = BLOCK // CHUNK - 1 + 2 * LAG * (n - 1)

    def body(t, _):
        line_sum_step(n, z, t, part, up, total, sums)
        line_gather_step(n, z, t, g_part, g, ss, rs)
        q = t - first
        d = lax.div(jnp.maximum(q, 0), 4)
        k = lax.rem(jnp.maximum(q, 0), 4)
        r = pl.ds(pl.multiple_of(d * tile, tile), tile)

        @pl.when((q >= 0) & (k == 0))
        def _():
            @pl.when(d == 0)
            def _():
                for copy in loads:
                    copy.wait()
                mine.wait()

            @pl.when(d > 0)
            def _():
                for copy in saves(d - 1):
                    copy.wait()

            h = x[r, :].astype(F32) + keep[r, :] * total[r, :].astype(F32)
            scale = lax.rsqrt(jnp.mean(h * h, axis=1, keepdims=True) + eps)
            n2_s[...] = (h * scale * gain[...]).astype(BF)
            gate_s[...] = mm(n2_s[...], wg[...])

        @pl.when((q >= 0) & (k == 1))
        def _():
            upper_s[...] = mm(n2_s[...], wu[...])
            gate = gate_s[...]
            inner_s[...] = (gate * jax.nn.sigmoid(gate) * upper_s[...]).astype(BF)

        @pl.when((q >= 0) & (k == 2))
        def _():
            f_s[...] = mm(inner_s[...], wd[...]).astype(BF)
            gf = (keep[r, :] * g[r, :].astype(F32)).astype(BF)
            back = nt(gf, wd[...])
            gate = gate_s[...]
            s = jax.nn.sigmoid(gate)
            both_s[:, :hidden] = (back * upper_s[...] * s * (1.0 + gate * (1.0 - s))).astype(BF)
            both_s[:, hidden:] = (back * (gate * s)).astype(BF)

        @pl.when((q >= 0) & (k == 3))
        def _():
            dn2_s[...] = (nt(both_s[:, :hidden], wg[...]) + nt(both_s[:, hidden:], wu[...])).astype(BF)
            for copy in saves(d):
                copy.start()

        return 0

    lax.fori_loop(0, first + 4 * (rows // tile), body, 0)
    ends = [pltpu.make_async_copy(a, b, late.at[i]) for i, (a, b) in enumerate(((total, a_far), (g, g_far)))]
    for copy in ends:
        copy.start()
    line_sum_drain(n, z, part, up, total, sums)
    line_gather_drain(n, z, g_part, g, ss, rs)
    for copy in saves(rows // tile - 1) + ends:
        copy.wait()


def middle(n, part, x, g_part, keep, gain, wg, wu, wd):
    rows, width = part.shape
    hidden = wg.shape[1]
    tile = 2 * BLOCK
    blocks = rows // BLOCK
    widths = (width, width, width, hidden, 2 * hidden, width, width)
    return pl.pallas_call(
        functools.partial(middle_kernel, n),
        out_shape=[jax.ShapeDtypeStruct((rows, k), BF) for k in widths],
        in_specs=[VM] * 5 + [ANY] * 3,
        out_specs=[ANY] * 7,
        scratch_shapes=[
            pltpu.VMEM(wg.shape, BF),
            pltpu.VMEM(wu.shape, BF),
            pltpu.VMEM(wd.shape, BF),
            pltpu.VMEM((rows, width), BF),
            pltpu.VMEM((rows, width), BF),
            pltpu.VMEM((rows, width), BF),
            pltpu.VMEM((tile, hidden), F32),
            pltpu.VMEM((tile, hidden), F32),
            pltpu.VMEM((tile, width), BF),
            pltpu.VMEM((tile, hidden), BF),
            pltpu.VMEM((tile, 2 * hidden), BF),
            pltpu.VMEM((tile, width), BF),
            pltpu.VMEM((tile, width), BF),
            *line_sum_sems(rows),
            pltpu.SemaphoreType.DMA((2, n, blocks)),
            pltpu.SemaphoreType.DMA((2, n, blocks)),
            pltpu.SemaphoreType.DMA((3,)),
            pltpu.SemaphoreType.DMA,
            pltpu.SemaphoreType.DMA((5,)),
            pltpu.SemaphoreType.DMA((2,)),
        ],
        compiler_params=pltpu.CompilerParams(collective_id=3, has_side_effects=True, vmem_limit_bytes=62 << 20),
    )(part, x, g_part, keep, gain, wg, wu, wd)


def second_back_kernel(n, part, x, a, g, keep, gain, ga, dh, gain_grad, up, total, us, ur, ds, dr):
    z = lax.axis_index("tensor")
    rows, width = part.shape
    w = dh.shape[1]
    piece = BLOCK // 2
    sums = (us, ur, ds, dr)
    neighbour_barrier(z, n, "tensor")
    gain_grad[...] = jnp.zeros_like(gain_grad)
    first = BLOCK // CHUNK - 1 + 2 * LAG * (n - 1)

    def body(t, _):
        line_sum_step(n, z, t, part, up, total, sums)
        q = t - first

        @pl.when(q >= 0)
        def _():
            r = pl.ds(pl.multiple_of(q * piece, piece), piece)
            h = x[r, :].astype(F32) + keep[r, :] * a[r, :].astype(F32)
            scale = lax.rsqrt(jnp.mean(h * h, axis=1, keepdims=True) + eps)
            back = total[r, :].astype(F32)
            gain_grad[...] += jnp.sum(back * h * scale, axis=0, keepdims=True)
            e = back * gain[...]
            along = jnp.mean(e * h, axis=1, keepdims=True)
            full = g[r, :].astype(F32) + scale * e - h * (scale * scale * scale * along)
            ga[r, :] = (keep[r, :] * full).astype(BF)
            for b in range(n):

                @pl.when(z == b)
                def _():
                    dh[r, :] = full[:, b * w : (b + 1) * w]

        return 0

    lax.fori_loop(0, first + rows // piece, body, 0)
    line_sum_drain(n, z, part, up, total, sums)


def second_back_of(n, part, x, a, g, keep, gain):
    rows, width = part.shape
    return pl.pallas_call(
        functools.partial(second_back_kernel, n),
        out_shape=[
            jax.ShapeDtypeStruct((rows, width), BF),
            jax.ShapeDtypeStruct((rows, width // n), F32),
            jax.ShapeDtypeStruct((1, width), F32),
        ],
        in_specs=[VM] * 6,
        out_specs=[VM] * 3,
        scratch_shapes=[pltpu.VMEM((rows, width), BF), pltpu.VMEM((rows, width), BF), *line_sum_sems(rows)],
        compiler_params=pltpu.CompilerParams(collective_id=4, has_side_effects=True, vmem_limit_bytes=56 << 20),
    )(part, x, a, g, keep, gain)


def rotary_tables(token_positions, head_size):
    half = head_size // 2
    freqs = rope_base ** (-(jnp.arange(half).astype(jnp.float32) * 2.0) / head_size)
    angles = token_positions.astype(jnp.float32)[:, None] * freqs[None, :]
    angles = jnp.concatenate([angles, angles], axis=1)
    return (jnp.cos(angles), jnp.sin(angles))


def matmul(left, right):
    return jnp.dot(left, right, preferred_element_type=jnp.float32)


def per_device(
    tokens,
    cotangent,
    first_gain,
    query_weight,
    key_matrix,
    value_matrix,
    output_weight,
    second_gain,
    gate_weight,
    up_weight,
    down_weight,
    seq_lengths,
    owner_order,
    skip_mask,
):
    groups = lax.axis_size("dp")
    member = lax.axis_index("dp")
    width_part = tokens.shape[1]
    row_count = tokens.shape[0]
    per_owner = row_count // groups
    seq_count = seq_lengths.shape[0]
    seq_index = jnp.arange(seq_count, dtype=jnp.int32)
    before = (seq_index[None, :] < seq_index[:, None]).astype(jnp.int32)
    unit_lengths = seq_lengths // groups
    unit_starts = jnp.sum(before * unit_lengths[None, :], axis=1)
    placed = (owner_order[:, None] == seq_index[None, :]).astype(jnp.int32)
    order_lengths = jnp.sum(placed * unit_lengths[None, :], axis=1)
    order_starts = jnp.sum(placed * unit_starts[None, :], axis=1)
    order_keep = jnp.sum(placed * skip_mask[None, :], axis=1)
    order_before = jnp.sum(before * order_lengths[None, :], axis=1)
    places = jnp.arange(row_count, dtype=jnp.int32)
    covers = (
        (places[:, None] >= order_before[None, :])
        & (places[:, None] < (order_before + order_lengths)[None, :])
    ).astype(jnp.int32)
    send_rows = places + jnp.sum(covers * (order_starts - order_before)[None, :], axis=1)
    given_before = jnp.sum(placed * order_before[:, None], axis=0)
    given_covers = (
        (places[:, None] >= unit_starts[None, :])
        & (places[:, None] < (unit_starts + unit_lengths)[None, :])
    ).astype(jnp.int32)
    slot_of = places + jnp.sum(given_covers * (given_before - unit_starts)[None, :], axis=1)
    my_places = member * per_owner + jnp.arange(per_owner, dtype=jnp.int32)
    my_covers = (
        (my_places[:, None] >= order_before[None, :])
        & (my_places[:, None] < (order_before + order_lengths)[None, :])
    ).astype(jnp.int32)
    slot_seq = jnp.sum(my_covers * seq_index[None, :], axis=1)
    slot_step = my_places - jnp.sum(my_covers * order_before[None, :], axis=1)
    slot_keep = jnp.sum(my_covers * order_keep[None, :], axis=1)
    tiles = max(1, per_owner // 32)
    sources = jnp.arange(groups, dtype=jnp.int32)[None, :, None]

    def spread(values):
        values = values.reshape(tiles, 1, per_owner // tiles)
        return jnp.broadcast_to(values, (tiles, groups, per_owner // tiles)).reshape(row_count)

    token_positions = (
        sources + groups * slot_step.reshape(tiles, 1, per_owner // tiles)
    ).reshape(row_count)
    lowest = spread(slot_seq) * row_count
    code = lowest + token_positions
    keep_rows = spread(slot_keep).reshape(row_count, 1).astype(jnp.float32)
    chosen = (send_rows[:, None] == places[None, :]).astype(jnp.bfloat16)
    put_back = (slot_of[:, None] == places[None, :]).astype(jnp.bfloat16)

    def swap(values, first, second):
        return (
            values.reshape(first, second, per_owner // tiles, width_part)
            .transpose(1, 0, 2, 3)
            .reshape(row_count, width_part)
        )

    def to_owner(values):
        dealt = matmul(chosen, values).astype(jnp.bfloat16)
        return swap(
            lax.all_to_all(dealt, "dp", split_axis=0, concat_axis=0, tiled=True), groups, tiles
        )

    def to_given(values):
        back = lax.all_to_all(
            swap(values, tiles, groups), "dp", split_axis=0, concat_axis=0, tiled=True
        )
        return matmul(put_back, back).astype(jnp.bfloat16)

    owned_tokens = lax.all_gather(to_owner(tokens), "tensor", axis=1, tiled=True)
    part_cotangent = to_owner(cotangent)
    tensor_member = lax.axis_index("tensor")
    inputs = owned_tokens.astype(jnp.float32)

    def my_part(values):
        return lax.dynamic_slice_in_dim(values, tensor_member * width_part, width_part, 1)

    cosine, sine = rotary_tables(token_positions, HEAD_WIDTH)
    half = HEAD_WIDTH // 2
    tables = (
        cosine,
        jnp.concatenate([-sine[:, :half], sine[:, half:]], axis=1),
        code[None, :],
        code[:, None],
        lowest[:, None],
    )
    tensor_count = lax.axis_size("tensor")
    weights = (query_weight, key_matrix, value_matrix, output_weight)
    attn_part, normed_one, *kept = attend(
        tiles, owned_tokens, first_gain[None, :], *weights, *tables
    )
    attn_sum, owned_cotangent, normed_two, inner_low, both, ffn_term, second_term = middle(
        tensor_count,
        attn_part,
        owned_tokens,
        part_cotangent,
        keep_rows,
        second_gain[None, :],
        gate_weight,
        up_weight,
        down_weight,
    )
    ffn_out = lax.psum_scatter(ffn_term, "tensor", scatter_dimension=1, tiled=True)
    hidden_res = my_part(owned_tokens).astype(F32) + keep_rows * my_part(attn_sum).astype(F32)
    grad_ffn = (keep_rows * owned_cotangent.astype(F32)).astype(BF)
    hidden = gate_weight.shape[1]

    def shared(values):
        return lax.psum_scatter(
            values.astype(jnp.bfloat16), "dp", scatter_dimension=0, tiled=True
        ).astype(jnp.float32)

    both_grad = matmul(normed_two.T, both).astype(BF)
    down_grad = matmul(grad_ffn.T, inner_low).astype(BF)
    second_term, both_grad, down_grad = lax.optimization_barrier(
        (second_term, both_grad, down_grad)
    )
    both_share = shared(both_grad)
    grad_attn, grad_res, second_gain_grad = second_back_of(
        tensor_count,
        second_term,
        owned_tokens,
        attn_sum,
        owned_cotangent,
        keep_rows,
        second_gain[None, :],
    )
    grad_attn, ffn_out, both_share, down_grad = lax.optimization_barrier(
        (grad_attn, ffn_out, both_share, down_grad)
    )
    result = hidden_res + keep_rows * ffn_out.astype(F32)
    down_share = shared(down_grad)
    output_grad = matmul(grad_attn.T, kept[3])
    first_part, grad_joined = attend_back(tiles, grad_attn, *weights, *kept, *tables)
    first_back, down_share = lax.optimization_barrier((rs(first_part, tensor_count), down_share))
    first_back = first_back.astype(jnp.float32)
    joined_grad = matmul(normed_one.T, grad_joined)
    scale_one = lax.rsqrt(jnp.mean(inputs * inputs, axis=1, keepdims=True) + eps)
    my_inputs = my_part(inputs)
    first_gain_part = jnp.sum(first_back * my_inputs * scale_one, axis=0)
    scaled_one = first_back * lax.dynamic_slice_in_dim(
        first_gain, tensor_member * width_part, width_part, 0
    )
    along = lax.psum(jnp.sum(scaled_one * my_inputs, axis=1, keepdims=True), "tensor") / inputs.shape[1]
    grad_in = grad_res + scale_one * scaled_one - my_inputs * scale_one**3 * along
    out_part = result.astype(jnp.bfloat16)
    grad_part = grad_in.astype(jnp.bfloat16)
    out_part, grad_part = lax.optimization_barrier((out_part, grad_part))
    layer_output = to_given(out_part)
    input_grad = to_given(grad_part)
    gains = jnp.stack([first_gain_part, my_part(second_gain_grad)[0]])
    gains = lax.dynamic_update_slice_in_dim(
        jnp.zeros((2, inputs.shape[1]), jnp.float32), gains, tensor_member * width_part, 1
    )
    gains = lax.dynamic_slice_in_dim(
        lax.psum(gains, ("dp", "tensor")),
        member * (inputs.shape[1] // groups),
        inputs.shape[1] // groups,
        1,
    )

    output_share, first = shared(output_grad), shared(joined_grad)
    a = query_weight.shape[1]
    b = a + key_matrix.shape[1]
    summed = (
        gains[0],
        first[:, :a],
        first[:, a:b],
        first[:, b:],
        output_share.T,
        both_share[:, :hidden],
        both_share[:, hidden:],
        down_share.T,
        gains[1],
    )
    return (
        layer_output,
        input_grad,
        summed[0],
        summed[1],
        summed[2],
        summed[3],
        summed[4],
        summed[8],
        summed[5],
        summed[6],
        summed[7],
    )


def solution(mesh):
    placed = (
        P(None, ("dp", "tensor")),
        P(None, ("dp", "tensor")),
        P(),
        P(None, "tensor"),
        P(None, "tensor"),
        P(None, "tensor"),
        P("tensor", None),
        P(),
        P(None, "tensor"),
        P(None, "tensor"),
        P("tensor", None),
        P(),
        P(),
        P(),
    )
    return jax.shard_map(
        per_device,
        mesh=mesh,
        in_specs=placed,
        out_specs=(
            P(None, ("dp", "tensor")),
            P(None, ("dp", "tensor")),
            P("dp"),
            P("dp", "tensor"),
            P("dp", "tensor"),
            P("dp", "tensor"),
            P("tensor", "dp"),
            P("dp"),
            P("dp", "tensor"),
            P("dp", "tensor"),
            P("tensor", "dp"),
        ),
        check_vma=False,
    )
```

```python
import functools
import math

import jax
import jax.numpy as jnp
from jax import lax
from jax.experimental import pallas as pl
from jax.experimental.pallas import tpu as pltpu
from jax.sharding import PartitionSpec as P

HEAD_WIDTH = 128

MESH = pl.DeviceIdType.MESH
VM = pl.BlockSpec(memory_space=pltpu.VMEM)
F32 = jnp.float32
BF = jnp.bfloat16

def neighbour_barrier(z, n, axis):
    barrier = pltpu.get_barrier_semaphore()
    @pl.when(z > 0)
    def _():
        pl.semaphore_signal(barrier, inc=1, device_id={axis: z - 1}, device_id_type=MESH)
    @pl.when(z < n - 1)
    def _():
        pl.semaphore_signal(barrier, inc=1, device_id={axis: z + 1}, device_id_type=MESH)
    ends = jnp.where(z > 0, 1, 0) + jnp.where(z < n - 1, 1, 0)
    pl.semaphore_wait(barrier, ends)

def rcopy(src, dst, ss, rs, dev):
    return pltpu.make_async_remote_copy(src_ref=src, dst_ref=dst, send_sem=ss, recv_sem=rs, device_id={"tensor": dev}, device_id_type=MESH)


eps = 1e-05
rope_base = 10000.0


def nt(left, right):
    return lax.dot_general(left, right, (((1,), (1,)), ((), ())), preferred_element_type=F32)


def tn(left, right):
    return lax.dot_general(left, right, (((0,), (0,)), ((), ())), preferred_element_type=F32)


def mm(left, right):
    return jnp.dot(left, right, preferred_element_type=F32)


def spin(values, cosine, signed_sine):
    return values * cosine + pltpu.roll(values, HEAD_WIDTH // 2, 1) * signed_sine


def visible(code_row, code_col, low_col):
    return jnp.where((code_row <= code_col) & (code_row >= low_col), 0.0, -1e30)


def attend_kernel(tiles, x, gain, wq, wk, wv, wo, cosine, sine, code_row, code_col, low_col,
                  part, normed, q, k, v, o, lse, scales):
    rows = x.shape[0]
    tile = rows // tiles
    heads = wq.shape[1] // HEAD_WIDTH
    kv = wk.shape[1] // HEAD_WIDTH
    group = heads // kv
    factor = math.log2(math.e) / math.sqrt(HEAD_WIDTH)
    for t in range(tiles):
        r = pl.ds(t * tile, tile)
        xt = x[r, :].astype(F32)
        scale = lax.rsqrt(jnp.mean(xt * xt, axis=1, keepdims=True) + eps)
        scales[r, :] = scale
        n1 = (xt * scale * gain[...]).astype(BF)
        normed[r, :] = n1
        c, s = cosine[r, :], sine[r, :]
        pre = mm(n1, wq[...])
        for h in range(heads):
            cut = slice(h * HEAD_WIDTH, (h + 1) * HEAD_WIDTH)
            q[r, cut] = spin(pre[:, cut], c, s).astype(BF)
        pre = mm(n1, wk[...])
        for h in range(kv):
            cut = slice(h * HEAD_WIDTH, (h + 1) * HEAD_WIDTH)
            k[r, cut] = spin(pre[:, cut], c, s).astype(BF)
        v[r, :] = mm(n1, wv[...]).astype(BF)
        seen = (t + 1) * tile
        bias = visible(code_row[:, :seen], code_col[r, :], low_col[r, :])
        logs = []
        for h in range(heads):
            cut = slice(h * HEAD_WIDTH, (h + 1) * HEAD_WIDTH)
            mine = slice(h // group * HEAD_WIDTH, (h // group + 1) * HEAD_WIDTH)
            scores = nt(q[r, cut], k[:seen, mine]) * factor + bias
            top = jnp.max(scores, axis=1, keepdims=True)
            expo = jnp.exp2(scores - top)
            total = jnp.sum(expo, axis=1, keepdims=True)
            probs = (expo * (1.0 / total)).astype(BF)
            o[r, cut] = mm(probs, v[:seen, mine]).astype(BF)
            logs.append(top + jnp.log2(total))
        lse[r, :] = jnp.concatenate(logs, axis=1)
        part[r, :] = mm(o[r, :], wo[...]).astype(BF)


def attend(tiles, x, gain, wq, wk, wv, wo, *tables):
    rows, width = x.shape
    heads = wq.shape[1] // HEAD_WIDTH
    shapes = [(rows, width), (rows, width), (rows, wq.shape[1]), (rows, wk.shape[1]), (rows, wv.shape[1]), (rows, wq.shape[1])]
    return pl.pallas_call(
        functools.partial(attend_kernel, tiles),
        out_shape=[jax.ShapeDtypeStruct(s, BF) for s in shapes] + [jax.ShapeDtypeStruct((rows, heads), F32), jax.ShapeDtypeStruct((rows, 1), F32)],
        in_specs=[VM] * 11,
        out_specs=[VM] * 8,
        compiler_params=pltpu.CompilerParams(vmem_limit_bytes=56 << 20),
    )(x, gain, wq, wk, wv, wo, *tables)


def attend_back_tile(t, tiles, ga, wq, wk, wv, wo, q, k, v, o, lse, cosine, sine, code_row, code_col, low_col,
                     part, dqkv, dk, dv):
    rows = ga.shape[0]
    tile = rows // tiles
    heads = wq.shape[1] // HEAD_WIDTH
    kv = wk.shape[1] // HEAD_WIDTH
    group = heads // kv
    wide = heads * HEAD_WIDTH
    narrow = kv * HEAD_WIDTH
    score_scale = 1.0 / math.sqrt(HEAD_WIDTH)
    factor = math.log2(math.e) / math.sqrt(HEAD_WIDTH)
    seen = (t + 1) * tile
    block = min(tile, 256)
    for at in range(t * tile, (t + 1) * tile, block):
        r = pl.ds(at, block)
        do = nt(ga[r, :], wo[...]).astype(BF)
        c, s = cosine[r, :], sine[r, :]
        bias = visible(code_row[:, :seen], code_col[r, :], low_col[r, :])
        logs = lse[r, :]
        for h in range(heads):
            cut = slice(h * HEAD_WIDTH, (h + 1) * HEAD_WIDTH)
            mine = slice(h // group * HEAD_WIDTH, (h // group + 1) * HEAD_WIDTH)
            do_h = do[:, cut]
            qh = q[r, cut]
            probs = jnp.exp2(nt(qh, k[:seen, mine]) * factor + bias - logs[:, h : h + 1])
            along = jnp.sum(do_h.astype(F32) * o[r, cut].astype(F32), axis=1, keepdims=True)
            ds = (probs * (nt(do_h, v[:seen, mine]) - along)).astype(BF)
            pb = probs.astype(BF)
            dq = mm(ds, k[:seen, mine]) * score_scale
            dqkv[r, cut] = spin(dq, c, -s).astype(BF)
            more_k = tn(ds, qh)
            more_v = tn(pb, do_h)
            if t == tiles - 1 and at == t * tile and h % group == 0:
                dk[:seen, mine] = more_k
                dv[:seen, mine] = more_v
            else:
                dk[:seen, mine] += more_k
                dv[:seen, mine] += more_v
    for at in range(t * tile, (t + 1) * tile, block):
        r = pl.ds(at, block)
        c, s = cosine[r, :], sine[r, :]
        for h in range(kv):
            cut = slice(h * HEAD_WIDTH, (h + 1) * HEAD_WIDTH)
            low = wide + h * HEAD_WIDTH
            dqkv[r, low : low + HEAD_WIDTH] = spin(dk[r, cut] * score_scale, c, -s).astype(BF)
        dqkv[r, wide + narrow :] = dv[r, :].astype(BF)
        part[r, :] = (
            nt(dqkv[r, :wide], wq[...])
            + nt(dqkv[r, wide : wide + narrow], wk[...])
            + nt(dqkv[r, wide + narrow :], wv[...])
        ).astype(BF)


ANY = pl.BlockSpec(memory_space=pl.ANY)
LAG = 2
CHUNK = 32
BLOCK = 128


def line_row(f, c):
    per = BLOCK // CHUNK
    return pl.ds(pl.multiple_of(lax.div(c, per) * (2 * BLOCK) + f * BLOCK + lax.rem(c, per) * CHUNK, CHUNK), CHUNK)


def line_steps(n, rows):
    return rows // 2 // CHUNK + 2 * LAG * (n - 1)


def line_sum_step(n, z, t, part, up, out, sems):
    us, ur, ds, dr = sems
    count = part.shape[0] // 2 // CHUNK
    for f in range(2):
        p = z if f == 0 else n - 1 - z
        step = 1 if f == 0 else -1
        c = t - LAG * p

        @pl.when((c >= 0) & (c < count))
        def _():
            r = line_row(f, c)

            @pl.when(p == 0)
            def _():
                rcopy(part.at[r], up.at[r], us.at[f, c], ur.at[f, c], z + step).start()

            @pl.when(p > 0)
            def _():
                rcopy(up.at[r], up.at[r], us.at[f, c], ur.at[f, c], z).wait_recv()
                s = (part[r, :].astype(F32) + up[r, :].astype(F32)).astype(BF)

                @pl.when(p < n - 1)
                def _():
                    up[r, :] = s
                    rcopy(up.at[r], up.at[r], us.at[f, c], ur.at[f, c], z + step).start()

                @pl.when(p == n - 1)
                def _():
                    out[r, :] = s
                    rcopy(out.at[r], out.at[r], ds.at[f, c], dr.at[f, c], z - step).start()

    for f in range(2):
        p = z if f == 0 else n - 1 - z
        step = 1 if f == 0 else -1
        c = t - LAG * (2 * (n - 1) - p)

        @pl.when((c >= 0) & (c < count) & (p < n - 1))
        def _():
            r = line_row(f, c)
            rcopy(out.at[r], out.at[r], ds.at[f, c], dr.at[f, c], z).wait_recv()

            @pl.when(p > 0)
            def _():
                rcopy(out.at[r], out.at[r], ds.at[f, c], dr.at[f, c], z - step).start()


def line_sum_drain(n, z, part, up, out, sems):
    us, ur, ds, dr = sems
    count = part.shape[0] // 2 // CHUNK

    def drain(c, _):
        for f in range(2):
            p = z if f == 0 else n - 1 - z
            r = line_row(f, c)

            @pl.when(p < n - 1)
            def _():
                rcopy(up.at[r], up.at[r], us.at[f, c], ur.at[f, c], z).wait_send()

            @pl.when(p > 0)
            def _():
                rcopy(out.at[r], out.at[r], ds.at[f, c], dr.at[f, c], z).wait_send()

        return 0

    lax.fori_loop(0, count, drain, 0)


def line_sum_sems(rows):
    return [pltpu.SemaphoreType.DMA((2, rows // 2 // CHUNK))] * 4


def gather_cut(ref, o, c, w):
    return ref.at[pl.ds(pl.multiple_of(c * BLOCK, BLOCK), BLOCK), pl.ds(pl.multiple_of(o * w, w), w)]


def line_gather_step(n, z, t, src, out, ss, rs):
    rows, w = src.shape
    count = rows // BLOCK

    @pl.when(t < count)
    def _():
        mine = src.at[pl.ds(pl.multiple_of(t * BLOCK, BLOCK), BLOCK)]

        @pl.when(z < n - 1)
        def _():
            rcopy(mine, gather_cut(out, z, t, w), ss.at[0, z, t], rs.at[0, z, t], z + 1).start()

        @pl.when(z > 0)
        def _():
            rcopy(mine, gather_cut(out, z, t, w), ss.at[1, z, t], rs.at[1, z, t], z - 1).start()

    for hop in range(1, n):
        c = t - hop
        for d, step in ((0, 1), (1, -1)):
            o = z - hop * step

            @pl.when((c >= 0) & (c < count) & (o >= 0) & (o < n))
            def _():
                cut = gather_cut(out, o, c, w)
                rcopy(cut, cut, ss.at[d, o, c], rs.at[d, o, c], z).wait_recv()
                after = z + step

                @pl.when((after >= 0) & (after < n))
                def _():
                    rcopy(cut, cut, ss.at[d, o, c], rs.at[d, o, c], after).start()


def line_gather_drain(n, z, src, out, ss, rs):
    rows, w = src.shape

    def drain(c, _):
        for d in range(2):
            for o in range(n):
                on = (o <= z) & (z < n - 1) if d == 0 else (o >= z) & (z > 0)

                @pl.when(on)
                def _():
                    cut = gather_cut(out, o, c, w)
                    rcopy(cut, cut, ss.at[d, o, c], rs.at[d, o, c], z).wait_send()

        return 0

    lax.fori_loop(0, rows // BLOCK, drain, 0)


def middle_kernel(n, part, x, g_part, keep, gain, wg_far, wu_far, wd_far,
                  result, a_far, g_far, n2_far, inner_far, both_far, dn2_far,
                  wg, wu, wd, up, total, g, right, left, gate_s, upper_s, n2_s, inner_s, both_s, f_s, dn2_s,
                  us, ur, ds, dr, ss, rs, fs, fr, load, own, save, late):
    z = lax.axis_index("tensor")
    rows, width = part.shape
    w = g_part.shape[1]
    hidden = wg.shape[1]
    tile = 2 * BLOCK
    sums = (us, ur, ds, dr)
    loads = [pltpu.make_async_copy(a, b, load.at[i]) for i, (a, b) in enumerate(((wg_far, wg), (wu_far, wu), (wd_far, wd)))]
    for copy in loads:
        copy.start()
    mine = pltpu.make_async_copy(g_part, g.at[:, pl.ds(pl.multiple_of(z * w, w), w)], own)
    mine.start()
    neighbour_barrier(z, n, "tensor")

    def saves(d):
        r = pl.ds(pl.multiple_of(d * tile, tile), tile)
        pairs = ((n2_s, n2_far), (inner_s, inner_far), (both_s, both_far), (dn2_s, dn2_far))
        return [pltpu.make_async_copy(a, b.at[r], save.at[i]) for i, (a, b) in enumerate(pairs)]

    first = BLOCK // CHUNK - 1 + 2 * LAG * (n - 1)

    def body(t, _):
        line_sum_step(n, z, t, part, up, total, sums)

        @pl.when(lax.rem(t, 2) == 0)
        def _():
            line_gather_step(n, z, lax.div(t, 2), g_part, g, ss, rs)

        q = t - first
        d = lax.div(jnp.maximum(q, 0), 4)
        k = lax.rem(jnp.maximum(q, 0), 4)
        r = pl.ds(pl.multiple_of(d * tile, tile), tile)

        @pl.when((q >= 0) & (d < rows // tile) & (k == 0))
        def _():
            @pl.when(d == 0)
            def _():
                for copy in loads:
                    copy.wait()
                mine.wait()

            @pl.when(d > 0)
            def _():
                for copy in saves(d - 1):
                    copy.wait()

            h = x[r, :].astype(F32) + keep[r, :] * total[r, :].astype(F32)
            scale = lax.rsqrt(jnp.mean(h * h, axis=1, keepdims=True) + eps)
            n2_s[...] = (h * scale * gain[...]).astype(BF)
            gate_s[...] = mm(n2_s[...], wg[...])

        @pl.when((q >= 0) & (d < rows // tile) & (k == 1))
        def _():
            upper_s[...] = mm(n2_s[...], wu[...])
            gate = gate_s[...]
            inner_s[...] = (gate * jax.nn.sigmoid(gate) * upper_s[...]).astype(BF)

        @pl.when((q >= 0) & (d < rows // tile) & (k == 2))
        def _():
            f_s[lax.rem(d, 2)] = mm(inner_s[...], wd[...]).astype(BF)
            gf = (keep[r, :] * g[r, :].astype(F32)).astype(BF)
            back = nt(gf, wd[...])
            gate = gate_s[...]
            s = jax.nn.sigmoid(gate)
            both_s[:, :hidden] = (back * upper_s[...] * s * (1.0 + gate * (1.0 - s))).astype(BF)
            both_s[:, hidden:] = (back * (gate * s)).astype(BF)

        @pl.when((q >= 0) & (d < rows // tile) & (k == 3))
        def _():
            dn2_s[...] = (nt(both_s[:, :hidden], wg[...]) + nt(both_s[:, hidden:], wu[...])).astype(BF)
            for copy in saves(d):
                copy.start()

        scatter_step(t - first - 2)
        return 0

    chunk = tile // 4
    count = rows // chunk

    def at(ref, c, b):
        return ref.at[pl.ds(pl.multiple_of(c * chunk, chunk), chunk), pl.ds(b * w, w)]

    def scatter_copy(buf, d, c, b, to):
        return rcopy(at(buf, c, b), at(buf, c, b), fs.at[d, b, c], fr.at[d, b, c], to)

    def scatter_step(s):
        for d, buf, step in ((0, right, 1), (1, left, -1)):
            p = z if d == 0 else n - 1 - z
            c = s - p

            @pl.when((c >= 0) & (c < count))
            def _():
                r = pl.ds(pl.multiple_of(c * chunk, chunk), chunk)
                slot = lax.rem(lax.div(c, 4), 2)
                inner = pl.ds(pl.multiple_of(lax.rem(c, 4) * chunk, chunk), chunk)
                for b in range(n - 1, 0, -1) if d == 0 else range(n - 1):
                    k = pl.ds(b * w, w)

                    @pl.when((b > z) if d == 0 else (b < z))
                    def _():
                        @pl.when(p == 0)
                        def _():
                            buf[r, k] = f_s[slot, inner, k]

                        @pl.when(p > 0)
                        def _():
                            scatter_copy(buf, d, c, b, z).wait_recv()
                            buf[r, k] = (f_s[slot, inner, k].astype(F32) + buf[r, k].astype(F32)).astype(BF)

                        scatter_copy(buf, d, c, b, z + step).start()

        c = s - (n - 1)

        @pl.when((c >= 0) & (c < count))
        def _():
            r = pl.ds(pl.multiple_of(c * chunk, chunk), chunk)
            slot = lax.rem(lax.div(c, 4), 2)
            inner = pl.ds(pl.multiple_of(lax.rem(c, 4) * chunk, chunk), chunk)
            for b in range(n):
                k = pl.ds(b * w, w)

                @pl.when(z == b)
                def _():
                    f = f_s[slot, inner, k].astype(F32)
                    if b > 0:
                        scatter_copy(right, 0, c, b, z).wait_recv()
                        f = f + right[r, k].astype(F32)
                    if b < n - 1:
                        scatter_copy(left, 1, c, b, z).wait_recv()
                        f = f + left[r, k].astype(F32)
                    kept = keep[r, :]
                    h = x[r, k].astype(F32) + kept * total[r, k].astype(F32)
                    result[r, :] = (h + kept * f).astype(BF)

    lax.fori_loop(0, first + 2 + count + n, body, 0)

    def drain(c, _):
        for d, buf in ((0, right), (1, left)):
            for b in range(n):

                @pl.when((b > z) if d == 0 else (b < z))
                def _():
                    scatter_copy(buf, d, c, b, z).wait_send()

        return 0

    lax.fori_loop(0, count, drain, 0)
    ends = [pltpu.make_async_copy(a, b, late.at[i]) for i, (a, b) in enumerate(((total, a_far), (g, g_far)))]
    for copy in ends:
        copy.start()
    line_sum_drain(n, z, part, up, total, sums)
    line_gather_drain(n, z, g_part, g, ss, rs)
    for copy in saves(rows // tile - 1) + ends:
        copy.wait()


def middle(n, part, x, g_part, keep, gain, wg, wu, wd):
    rows, width = part.shape
    hidden = wg.shape[1]
    tile = 2 * BLOCK
    blocks = rows // BLOCK
    w = g_part.shape[1]
    widths = (w, width, width, width, hidden, 2 * hidden, width)
    return pl.pallas_call(
        functools.partial(middle_kernel, n),
        out_shape=[jax.ShapeDtypeStruct((rows, k), BF) for k in widths],
        in_specs=[VM] * 5 + [ANY] * 3,
        out_specs=[VM] + [ANY] * 6,
        scratch_shapes=[
            pltpu.VMEM(wg.shape, BF),
            pltpu.VMEM(wu.shape, BF),
            pltpu.VMEM(wd.shape, BF),
            pltpu.VMEM((rows, width), BF),
            pltpu.VMEM((rows, width), BF),
            pltpu.VMEM((rows, width), BF),
            pltpu.VMEM((rows, width), BF),
            pltpu.VMEM((rows, width), BF),
            pltpu.VMEM((tile, hidden), F32),
            pltpu.VMEM((tile, hidden), F32),
            pltpu.VMEM((tile, width), BF),
            pltpu.VMEM((tile, hidden), BF),
            pltpu.VMEM((tile, 2 * hidden), BF),
            pltpu.VMEM((2, tile, width), BF),
            pltpu.VMEM((tile, width), BF),
            *line_sum_sems(rows),
            pltpu.SemaphoreType.DMA((2, n, blocks)),
            pltpu.SemaphoreType.DMA((2, n, blocks)),
            pltpu.SemaphoreType.DMA((2, n, rows // tile * 4)),
            pltpu.SemaphoreType.DMA((2, n, rows // tile * 4)),
            pltpu.SemaphoreType.DMA((3,)),
            pltpu.SemaphoreType.DMA,
            pltpu.SemaphoreType.DMA((4,)),
            pltpu.SemaphoreType.DMA((2,)),
        ],
        compiler_params=pltpu.CompilerParams(collective_id=3, has_side_effects=True, vmem_limit_bytes=63 << 20),
    )(part, x, g_part, keep, gain, wg, wu, wd)


def second_back_kernel(n, part, x, a, g, keep, gain, ga, dh, gain_grad, up, total, us, ur, ds, dr):
    z = lax.axis_index("tensor")
    rows, width = part.shape
    w = dh.shape[1]
    piece = BLOCK // 2
    sums = (us, ur, ds, dr)
    neighbour_barrier(z, n, "tensor")
    gain_grad[...] = jnp.zeros_like(gain_grad)
    first = BLOCK // CHUNK - 1 + 2 * LAG * (n - 1)

    def body(t, _):
        line_sum_step(n, z, t, part, up, total, sums)
        q = t - first

        @pl.when(q >= 0)
        def _():
            r = pl.ds(pl.multiple_of(q * piece, piece), piece)
            h = x[r, :].astype(F32) + keep[r, :] * a[r, :].astype(F32)
            scale = lax.rsqrt(jnp.mean(h * h, axis=1, keepdims=True) + eps)
            back = total[r, :].astype(F32)
            gain_grad[...] += jnp.sum(back * h * scale, axis=0, keepdims=True)
            e = back * gain[...]
            along = jnp.mean(e * h, axis=1, keepdims=True)
            full = g[r, :].astype(F32) + scale * e - h * (scale * scale * scale * along)
            ga[r, :] = (keep[r, :] * full).astype(BF)
            for b in range(n):

                @pl.when(z == b)
                def _():
                    dh[r, :] = full[:, b * w : (b + 1) * w]

        return 0

    lax.fori_loop(0, first + rows // piece, body, 0)
    line_sum_drain(n, z, part, up, total, sums)


def second_back_of(n, part, x, a, g, keep, gain):
    rows, width = part.shape
    return pl.pallas_call(
        functools.partial(second_back_kernel, n),
        out_shape=[
            jax.ShapeDtypeStruct((rows, width), BF),
            jax.ShapeDtypeStruct((rows, width // n), F32),
            jax.ShapeDtypeStruct((1, width), F32),
        ],
        in_specs=[VM] * 6,
        out_specs=[VM] * 3,
        scratch_shapes=[pltpu.VMEM((rows, width), BF), pltpu.VMEM((rows, width), BF), *line_sum_sems(rows)],
        compiler_params=pltpu.CompilerParams(collective_id=4, has_side_effects=True, vmem_limit_bytes=56 << 20),
    )(part, x, a, g, keep, gain)


def peers_barrier(z, n, me, groups, everyone):
    barrier = pltpu.get_barrier_semaphore()

    def greet(off, _):
        peer = lax.rem(me + off, groups)
        pl.semaphore_signal(barrier, inc=1, device_id={"dp": peer}, device_id_type=MESH)
        return 0

    lax.fori_loop(1, groups, greet, 0)
    if everyone:
        for off in range(1, n):
            other = lax.rem(z + off, n)
            pl.semaphore_signal(barrier, inc=1, device_id={"tensor": other}, device_id_type=MESH)
        pl.semaphore_wait(barrier, groups - 1 + n - 1)
    else:

        @pl.when(z > 0)
        def _():
            pl.semaphore_signal(barrier, inc=1, device_id={"tensor": z - 1}, device_id_type=MESH)

        @pl.when(z < n - 1)
        def _():
            pl.semaphore_signal(barrier, inc=1, device_id={"tensor": z + 1}, device_id_type=MESH)

        ends = jnp.where(z > 0, 1, 0) + jnp.where(z < n - 1, 1, 0)
        pl.semaphore_wait(barrier, groups - 1 + ends)


def pcopy(src, dst, ss, rs, peer):
    return pltpu.make_async_remote_copy(
        src_ref=src, dst_ref=dst, send_sem=ss, recv_sem=rs, device_id={"dp": peer}, device_id_type=MESH
    )


def deal_in_kernel(n, groups, dealt_x, dealt_g, full, g_part, xs, xr, gs, gr, ss, rs, own):
    z = lax.axis_index("tensor")
    me = lax.axis_index("dp")
    tiles, sub, w = dealt_x.shape[1:]
    cols = pl.ds(pl.multiple_of(z * w, w), w)

    def place(t, i):
        return full.at[t, i, :, cols]

    for t in range(tiles):
        pltpu.make_async_copy(dealt_x.at[me, t], place(t, me), own.at[t]).start()
    pltpu.make_async_copy(dealt_g.at[me], g_part.at[:, me], own.at[tiles]).start()
    peers_barrier(z, n, me, groups, False)

    def send(t):
        def one(off, _):
            peer = lax.rem(me + off, groups)
            pcopy(dealt_x.at[peer, t], place(t, me), xs.at[t, peer], xr.at[t, me], peer).start()
            return 0

        lax.fori_loop(1, groups, one, 0)

    def cut(o, t):
        return full.at[t, :, :, pl.ds(pl.multiple_of(o * w, w), w)]

    for t in range(tiles):
        send(t)

    def send_g(off, _):
        peer = lax.rem(me + off, groups)
        pcopy(dealt_g.at[peer], g_part.at[:, me], gs.at[peer], gr.at[me], peer).start()
        return 0

    lax.fori_loop(1, groups, send_g, 0)
    for s in range(tiles + n - 1):
        if s < tiles:

            def got(off, _):
                peer = lax.rem(me + off, groups)
                pcopy(dealt_x.at[peer, s], place(s, peer), xs.at[s, peer], xr.at[s, peer], peer).wait_recv()
                return 0

            lax.fori_loop(1, groups, got, 0)
            pltpu.make_async_copy(dealt_x.at[me, s], place(s, me), own.at[s]).wait()

            @pl.when(z < n - 1)
            def _():
                rcopy(cut(z, s), cut(z, s), ss.at[0, z, s], rs.at[0, z, s], z + 1).start()

            @pl.when(z > 0)
            def _():
                rcopy(cut(z, s), cut(z, s), ss.at[1, z, s], rs.at[1, z, s], z - 1).start()

        for hop in range(1, n):
            c = s - hop
            if 0 <= c < tiles:
                for d, step in ((0, 1), (1, -1)):
                    o = z - hop * step

                    @pl.when((o >= 0) & (o < n))
                    def _():
                        rcopy(cut(o, c), cut(o, c), ss.at[d, o, c], rs.at[d, o, c], z).wait_recv()
                        after = z + step

                        @pl.when((after >= 0) & (after < n))
                        def _():
                            rcopy(cut(o, c), cut(o, c), ss.at[d, o, c], rs.at[d, o, c], after).start()

    def finish(off, _):
        peer = lax.rem(me + off, groups)
        copy = pcopy(dealt_g.at[peer], g_part.at[:, peer], gs.at[peer], gr.at[peer], peer)
        copy.wait_recv()
        copy.wait_send()
        for t in range(tiles):
            pcopy(dealt_x.at[peer, t], place(t, peer), xs.at[t, peer], xr.at[t, peer], peer).wait_send()
        return 0

    lax.fori_loop(1, groups, finish, 0)
    pltpu.make_async_copy(dealt_g.at[me], g_part.at[:, me], own.at[tiles]).wait()
    for c in range(tiles):
        for d in range(2):
            for o in range(n):

                @pl.when((o <= z) & (z < n - 1) if d == 0 else (o >= z) & (z > 0))
                def _():
                    rcopy(cut(o, c), cut(o, c), ss.at[d, o, c], rs.at[d, o, c], z).wait_send()


def deal_in(n, groups, dealt_x, dealt_g):
    tiles, sub, w = dealt_x.shape[1:]
    dma = pltpu.SemaphoreType.DMA
    return pl.pallas_call(
        functools.partial(deal_in_kernel, n, groups),
        out_shape=[
            jax.ShapeDtypeStruct((tiles, groups, sub, n * w), BF),
            jax.ShapeDtypeStruct((tiles, groups, sub, w), BF),
        ],
        in_specs=[VM] * 2,
        out_specs=[VM] * 2,
        scratch_shapes=[
            dma((tiles, groups)),
            dma((tiles, groups)),
            dma((groups,)),
            dma((groups,)),
            dma((2, n, tiles)),
            dma((2, n, tiles)),
            dma((tiles + 1,)),
        ],
        compiler_params=pltpu.CompilerParams(collective_id=6, has_side_effects=True, vmem_limit_bytes=48 << 20),
    )(dealt_x, dealt_g)


def exact(left, right, contract):
    return lax.dot_general(
        left, right, (contract, ((), ())), preferred_element_type=F32, precision=lax.Precision.HIGHEST
    )


def deal_out_kernel(n, groups, tiles, chunk, lag, x, dh, scale1, gain1, result, gain2, normed, *refs):
    attention = refs[:15]
    (back_out, back_dx, gains, shares, part, dqkv, dk, dv, right, left, fb, dx, lines, widths, gsrc, gdst, wsrc, wdst,
     ss, rs, os, orr, xs, xr, ls, lr, ws, wr, es, er, qs, qr, own) = refs[15:]
    ga, o = attention[0], attention[8]
    z = lax.axis_index("tensor")
    me = lax.axis_index("dp")
    rows, w = x.shape
    tile = rows // tiles
    count = rows // chunk
    per = tile // chunk
    sub = result.shape[2]
    pltpu.make_async_copy(result.at[:, me], back_out.at[me], own.at[0]).start()
    peers_barrier(z, n, me, groups, True)

    def send_out(off, _):
        peer = lax.rem(me + off, groups)
        pcopy(result.at[:, peer], back_out.at[me], os.at[peer], orr.at[me], peer).start()
        return 0

    lax.fori_loop(1, groups, send_out, 0)

    def chunk_rows(c):
        t = tiles - 1 - lax.div(c, per)
        return pl.ds(pl.multiple_of(t * tile + lax.rem(c, per) * chunk, chunk), chunk)

    def at(ref, c, b):
        return ref.at[chunk_rows(c), pl.ds(b * w, w)]

    widths[...] = jnp.zeros_like(widths)

    def others(f):
        for off in range(1, n):
            f(lax.rem(z + off, n))

    def line_copy(t, slot, other):
        cut = lines.at[slot, :, pl.ds(pl.multiple_of(t * tile, tile), tile)]
        return rcopy(cut, cut, ls.at[other, t], lr.at[slot, t], other)

    def width_copy(slot, other):
        cut = widths.at[slot]
        return rcopy(cut, cut, ws.at[other], wr.at[slot], other)

    def open_tile(t):
        r = pl.ds(pl.multiple_of(t * tile, tile), tile)
        e = fb[r, :] * gain1[...]
        xt = x[r, :].astype(F32)
        lines[z, :, r] = exact(jnp.ones((8, w), F32), e * xt, ((1,), (1,)))
        others(lambda other: line_copy(t, z, other).start())
        grown = jnp.sum(fb[r, :] * xt * scale1[r, :], axis=0, keepdims=True)
        widths[z, :, :] += jnp.broadcast_to(grown, (8, w))

        @pl.when(t == 0)
        def _():
            others(lambda other: width_copy(z, other).start())

    def close_tile(t):
        r = pl.ds(pl.multiple_of(t * tile, tile), tile)
        others(lambda other: line_copy(t, other, other).wait_recv())
        total = lines[0, :, r]
        for j in range(1, n):
            total = total + lines[j, :, r]
        along = exact(total * (1.0 / (8 * n * w)), jnp.ones((8, w), F32), ((0,), (0,)))
        e = fb[r, :] * gain1[...]
        s = scale1[r, :]
        full = dh[r, :] + s * e - x[r, :].astype(F32) * (s * s * s * along)
        dx[t] = full.astype(BF).reshape(groups, sub, w)
        pltpu.make_async_copy(dx.at[t, me], back_dx.at[me, t], own.at[1 + t]).start()

        def one(off, _):
            peer = lax.rem(me + off, groups)
            pcopy(dx.at[t, peer], back_dx.at[me, t], xs.at[t, peer], xr.at[t, me], peer).start()
            return 0

        lax.fori_loop(1, groups, one, 0)

    ow = o.shape[1]
    share = normed.shape[1] // groups
    span = max(share, 256)

    def weigh(left_ref, right_ref, at_column, kind):
        def one(j, _):
            base = lax.rem(j + lax.div(me * share, span), normed.shape[1] // span) * span
            cut = pl.ds(pl.multiple_of(base, span), span)
            wide = right_ref.shape[1]
            wsrc[cut, at_column : at_column + wide] = tn(left_ref[:, cut], right_ref[...]).astype(BF)
            for i in range(span // share):
                peer = lax.div(base, share) + i

                @pl.when(peer != me)
                def _():
                    weight_copy(kind, peer, me, peer, at_column, wide).start()

                @pl.when(peer == me)
                def _():
                    weight_own(kind, at_column, wide).start()

            return 0

        lax.fori_loop(0, normed.shape[1] // span, one, 0)

    def weight_copy(kind, block, slot, peer, at_column, wide):
        columns = pl.ds(at_column, wide)
        return pltpu.make_async_remote_copy(
            src_ref=wsrc.at[pl.ds(pl.multiple_of(block * share, share), share), columns],
            dst_ref=wdst.at[slot, :, columns],
            send_sem=qs.at[kind, block],
            recv_sem=qr.at[kind, slot],
            device_id={"dp": peer},
            device_id_type=MESH,
        )

    def weight_own(kind, at_column, wide):
        columns = pl.ds(at_column, wide)
        return pltpu.make_async_copy(
            wsrc.at[pl.ds(pl.multiple_of(me * share, share), share), columns],
            wdst.at[me, :, columns],
            own.at[2 + tiles + kind],
        )

    def flows(s, _):
        for k in range(tiles):

            @pl.when(s == k * per)
            def _():
                attend_back_tile(tiles - 1 - k, tiles, *attention, part, dqkv, dk, dv)

        @pl.when(s == 2)
        def _():
            weigh(ga, o, 0, 0)

        @pl.when(s == (tiles - 1) * per + 1)
        def _():
            weigh(normed, dqkv, ow, 1)

        for d, buf, step in ((0, right, 1), (1, left, -1)):
            p = z if d == 0 else n - 1 - z
            c = s - lag * p

            @pl.when((c >= 0) & (c < count))
            def _():
                r = chunk_rows(c)
                for b in range(n - 1, 0, -1) if d == 0 else range(n - 1):
                    k = pl.ds(b * w, w)

                    @pl.when((b > z) if d == 0 else (b < z))
                    def _():
                        @pl.when(p == 0)
                        def _():
                            rcopy(at(part, c, b), at(buf, c, b), ss.at[d, b, c], rs.at[d, b, c], z + step).start()

                        @pl.when(p > 0)
                        def _():
                            rcopy(at(buf, c, b), at(buf, c, b), ss.at[d, b, c], rs.at[d, b, c], z).wait_recv()
                            buf[r, k] = (part[r, k].astype(F32) + buf[r, k].astype(F32)).astype(BF)
                            rcopy(at(buf, c, b), at(buf, c, b), ss.at[d, b, c], rs.at[d, b, c], z + step).start()

        c = s - lag * (n - 1)

        @pl.when((c >= 0) & (c < count))
        def _():
            r = chunk_rows(c)
            for b in range(n):
                k = pl.ds(b * w, w)

                @pl.when(z == b)
                def _():
                    total = part[r, k].astype(F32)
                    if b > 0:
                        rcopy(at(right, c, b), at(right, c, b), ss.at[0, b, c], rs.at[0, b, c], z).wait_recv()
                        total = total + right[r, k].astype(F32)
                    if b < n - 1:
                        rcopy(at(left, c, b), at(left, c, b), ss.at[1, b, c], rs.at[1, b, c], z).wait_recv()
                        total = total + left[r, k].astype(F32)
                    fb[r, :] = total

        @pl.when((c >= 0) & (c < count) & (lax.rem(jnp.maximum(c, 0), per) == per - 1))
        def _():
            open_tile(tiles - 1 - lax.div(c, per))

        c = c - 2

        @pl.when((c >= 0) & (lax.rem(jnp.maximum(c, 0), per) == per - 1))
        def _():
            close_tile(tiles - 1 - lax.div(c, per))

        return 0

    lax.fori_loop(0, count + lag * (n - 1) + 2, flows, 0)

    others(lambda other: width_copy(other, other).wait_recv())
    cols = gsrc.shape[2]
    first_gain = jnp.concatenate([widths[j] for j in range(n)], axis=1)
    second_gain = jnp.broadcast_to(gain2[...], first_gain.shape)
    for i in range(groups):
        gsrc[i, :8, :] = first_gain[:, i * cols : (i + 1) * cols]
        gsrc[i, 8:, :] = second_gain[:, i * cols : (i + 1) * cols]
    pltpu.make_async_copy(gsrc.at[me], gdst.at[me], own.at[1 + tiles]).start()

    def send_gain(off, _):
        peer = lax.rem(me + off, groups)
        pcopy(gsrc.at[peer], gdst.at[me], es.at[peer], er.at[me], peer).start()
        return 0

    lax.fori_loop(1, groups, send_gain, 0)

    def got_gain(off, _):
        peer = lax.rem(me + off, groups)
        copy = pcopy(gsrc.at[peer], gdst.at[peer], es.at[peer], er.at[peer], peer)
        copy.wait_recv()
        copy.wait_send()
        return 0

    lax.fori_loop(1, groups, got_gain, 0)
    pltpu.make_async_copy(gsrc.at[me], gdst.at[me], own.at[1 + tiles]).wait()
    total = gdst[0]
    for i in range(1, groups):
        total = total + gdst[i]
    gains[...] = total

    def got_weight(off, _):
        peer = lax.rem(me + off, groups)
        for kind, (at_column, wide) in enumerate(((0, ow), (ow, dqkv.shape[1]))):
            copy = weight_copy(kind, peer, peer, peer, at_column, wide)
            copy.wait_recv()
            copy.wait_send()
        return 0

    lax.fori_loop(1, groups, got_weight, 0)
    weight_own(0, 0, ow).wait()
    weight_own(1, ow, dqkv.shape[1]).wait()
    shares[...] = wdst[0].astype(F32)
    for i in range(1, groups):
        shares[...] += wdst[i].astype(F32)

    def finish(off, _):
        peer = lax.rem(me + off, groups)
        copy = pcopy(result.at[:, peer], back_out.at[peer], os.at[peer], orr.at[peer], peer)
        copy.wait_recv()
        copy.wait_send()
        for t in range(tiles):
            copy = pcopy(dx.at[t, peer], back_dx.at[peer, t], xs.at[t, peer], xr.at[t, peer], peer)
            copy.wait_recv()
            copy.wait_send()
        return 0

    lax.fori_loop(1, groups, finish, 0)
    pltpu.make_async_copy(result.at[:, me], back_out.at[me], own.at[0]).wait()
    for t in range(tiles):
        pltpu.make_async_copy(dx.at[t, me], back_dx.at[me, t], own.at[1 + t]).wait()
        others(lambda other: line_copy(t, z, other).wait_send())
    others(lambda other: width_copy(z, other).wait_send())

    def drain(c, _):
        for d, buf in ((0, right), (1, left)):
            for b in range(n):

                @pl.when((b > z) if d == 0 else (b < z))
                def _():
                    rcopy(at(buf, c, b), at(buf, c, b), ss.at[d, b, c], rs.at[d, b, c], z).wait_send()

        return 0

    lax.fori_loop(0, count, drain, 0)


def deal_out(n, groups, tiles, x, dh, scale1, gain1, result, gain2, normed, *attention, chunk=64, lag=2):
    rows, w = x.shape
    width = n * w
    sub = rows // tiles // groups
    count = rows // chunk
    cols = width // groups
    joined = sum(a.shape[1] for a in attention[1:4])
    narrow = attention[2].shape[1]
    both = attention[8].shape[1] + joined
    dma = pltpu.SemaphoreType.DMA
    dealt = (groups, tiles, sub, w)
    return pl.pallas_call(
        functools.partial(deal_out_kernel, n, groups, tiles, chunk, lag),
        out_shape=[
            jax.ShapeDtypeStruct(dealt, BF),
            jax.ShapeDtypeStruct(dealt, BF),
            jax.ShapeDtypeStruct((16, cols), F32),
            jax.ShapeDtypeStruct((cols, both), F32),
        ],
        in_specs=[VM] * 22,
        out_specs=[VM] * 4,
        scratch_shapes=[
            pltpu.VMEM((rows, width), BF),
            pltpu.VMEM((rows, joined), BF),
            pltpu.VMEM((rows, narrow), F32),
            pltpu.VMEM((rows, narrow), F32),
            pltpu.VMEM((rows, width), BF),
            pltpu.VMEM((rows, width), BF),
            pltpu.VMEM((rows, w), F32),
            pltpu.VMEM((tiles, groups, sub, w), BF),
            pltpu.VMEM((n, 8, rows), F32),
            pltpu.VMEM((n, 8, w), F32),
            pltpu.VMEM((groups, 16, cols), F32),
            pltpu.VMEM((groups, 16, cols), F32),
            pltpu.VMEM((width, both), BF),
            pltpu.VMEM((groups, cols, both), BF),
            dma((2, n, count)),
            dma((2, n, count)),
            dma((groups,)),
            dma((groups,)),
            dma((tiles, groups)),
            dma((tiles, groups)),
            dma((n, tiles)),
            dma((n, tiles)),
            dma((n,)),
            dma((n,)),
            dma((groups,)),
            dma((groups,)),
            dma((2, groups)),
            dma((2, groups)),
            dma((tiles + 4,)),
        ],
        compiler_params=pltpu.CompilerParams(collective_id=5, has_side_effects=True, vmem_limit_bytes=62 << 20),
    )(x, dh, scale1, gain1, result.reshape(tiles, groups, sub, w), gain2, normed, *attention)


def rotary_tables(token_positions, head_size):
    half = head_size // 2
    freqs = rope_base ** (-(jnp.arange(half).astype(jnp.float32) * 2.0) / head_size)
    angles = token_positions.astype(jnp.float32)[:, None] * freqs[None, :]
    angles = jnp.concatenate([angles, angles], axis=1)
    return (jnp.cos(angles), jnp.sin(angles))


def matmul(left, right):
    return jnp.dot(left, right, preferred_element_type=jnp.float32)


def per_device(
    tokens,
    cotangent,
    first_gain,
    query_weight,
    key_matrix,
    value_matrix,
    output_weight,
    second_gain,
    gate_weight,
    up_weight,
    down_weight,
    seq_lengths,
    owner_order,
    skip_mask,
):
    groups = lax.axis_size("dp")
    member = lax.axis_index("dp")
    width_part = tokens.shape[1]
    row_count = tokens.shape[0]
    per_owner = row_count // groups
    seq_count = seq_lengths.shape[0]
    seq_index = jnp.arange(seq_count, dtype=jnp.int32)
    before = (seq_index[None, :] < seq_index[:, None]).astype(jnp.int32)
    unit_lengths = seq_lengths // groups
    unit_starts = jnp.sum(before * unit_lengths[None, :], axis=1)
    placed = (owner_order[:, None] == seq_index[None, :]).astype(jnp.int32)
    order_lengths = jnp.sum(placed * unit_lengths[None, :], axis=1)
    order_starts = jnp.sum(placed * unit_starts[None, :], axis=1)
    order_keep = jnp.sum(placed * skip_mask[None, :], axis=1)
    order_before = jnp.sum(before * order_lengths[None, :], axis=1)
    places = jnp.arange(row_count, dtype=jnp.int32)
    covers = (
        (places[:, None] >= order_before[None, :])
        & (places[:, None] < (order_before + order_lengths)[None, :])
    ).astype(jnp.int32)
    send_rows = places + jnp.sum(covers * (order_starts - order_before)[None, :], axis=1)
    given_before = jnp.sum(placed * order_before[:, None], axis=0)
    given_covers = (
        (places[:, None] >= unit_starts[None, :])
        & (places[:, None] < (unit_starts + unit_lengths)[None, :])
    ).astype(jnp.int32)
    slot_of = places + jnp.sum(given_covers * (given_before - unit_starts)[None, :], axis=1)
    my_places = member * per_owner + jnp.arange(per_owner, dtype=jnp.int32)
    my_covers = (
        (my_places[:, None] >= order_before[None, :])
        & (my_places[:, None] < (order_before + order_lengths)[None, :])
    ).astype(jnp.int32)
    slot_seq = jnp.sum(my_covers * seq_index[None, :], axis=1)
    slot_step = my_places - jnp.sum(my_covers * order_before[None, :], axis=1)
    slot_keep = jnp.sum(my_covers * order_keep[None, :], axis=1)
    tiles = max(1, per_owner // 32)
    sources = jnp.arange(groups, dtype=jnp.int32)[None, :, None]

    def spread(values):
        values = values.reshape(tiles, 1, per_owner // tiles)
        return jnp.broadcast_to(values, (tiles, groups, per_owner // tiles)).reshape(row_count)

    token_positions = (
        sources + groups * slot_step.reshape(tiles, 1, per_owner // tiles)
    ).reshape(row_count)
    lowest = spread(slot_seq) * row_count
    code = lowest + token_positions
    keep_rows = spread(slot_keep).reshape(row_count, 1).astype(jnp.float32)
    chosen = (send_rows[:, None] == places[None, :]).astype(jnp.bfloat16)
    put_back = (slot_of[:, None] == places[None, :]).astype(jnp.bfloat16)

    tensor_count = lax.axis_size("tensor")
    tensor_member = lax.axis_index("tensor")
    dealt_shape = (groups, tiles, per_owner // tiles, width_part)
    owned_tokens, part_cotangent = deal_in(
        tensor_count,
        groups,
        *(
            matmul(chosen, values).astype(BF).reshape(dealt_shape)
            for values in (tokens, cotangent)
        ),
    )
    owned_tokens = owned_tokens.reshape(row_count, -1)
    part_cotangent = part_cotangent.reshape(row_count, width_part)

    def my_part(values):
        return lax.dynamic_slice_in_dim(values, tensor_member * width_part, width_part, 1)

    cosine, sine = rotary_tables(token_positions, HEAD_WIDTH)
    half = HEAD_WIDTH // 2
    tables = (
        cosine,
        jnp.concatenate([-sine[:, :half], sine[:, half:]], axis=1),
        code[None, :],
        code[:, None],
        lowest[:, None],
    )
    weights = (query_weight, key_matrix, value_matrix, output_weight)
    attn_part, normed_one, *kept, scale_one = attend(
        tiles, owned_tokens, first_gain[None, :], *weights, *tables
    )
    result, attn_sum, owned_cotangent, normed_two, inner_low, both, second_term = middle(
        tensor_count,
        attn_part,
        owned_tokens,
        part_cotangent,
        keep_rows,
        second_gain[None, :],
        gate_weight,
        up_weight,
        down_weight,
    )
    grad_ffn = (keep_rows * owned_cotangent.astype(F32)).astype(BF)
    hidden = gate_weight.shape[1]

    def shared(values):
        return lax.psum_scatter(
            values.astype(jnp.bfloat16), "dp", scatter_dimension=0, tiled=True
        ).astype(jnp.float32)

    down_grad = matmul(grad_ffn.T, inner_low).astype(BF)
    down_grad, normed_two = lax.optimization_barrier((down_grad, normed_two))
    both_grad = matmul(normed_two.T, both).astype(BF)
    second_term, both_grad, down_grad = lax.optimization_barrier(
        (second_term, both_grad, down_grad)
    )
    both_share, down_share = shared(both_grad), shared(down_grad)
    grad_attn, grad_res, second_gain_grad = second_back_of(
        tensor_count,
        second_term,
        owned_tokens,
        attn_sum,
        owned_cotangent,
        keep_rows,
        second_gain[None, :],
    )
    down_share, grad_attn = lax.optimization_barrier((down_share, grad_attn))
    back_out, back_grad, gains, first = deal_out(
        tensor_count,
        groups,
        tiles,
        my_part(owned_tokens),
        grad_res,
        scale_one,
        my_part(first_gain[None, :]),
        result,
        second_gain_grad,
        normed_one,
        grad_attn,
        *weights,
        *kept,
        *tables,
    )
    both_share, back_out = lax.optimization_barrier((both_share, back_out))
    layer_output = matmul(put_back, back_out.reshape(row_count, width_part)).astype(BF)
    input_grad = matmul(put_back, back_grad.reshape(row_count, width_part)).astype(BF)
    o = output_weight.shape[0]
    a = o + query_weight.shape[1]
    b = a + key_matrix.shape[1]
    summed = (
        gains[0],
        first[:, o:a],
        first[:, a:b],
        first[:, b:],
        first[:, :o].T,
        both_share[:, :hidden],
        both_share[:, hidden:],
        down_share.T,
        gains[8],
    )
    return (
        layer_output,
        input_grad,
        summed[0],
        summed[1],
        summed[2],
        summed[3],
        summed[4],
        summed[8],
        summed[5],
        summed[6],
        summed[7],
    )


def solution(mesh):
    placed = (
        P(None, ("dp", "tensor")),
        P(None, ("dp", "tensor")),
        P(),
        P(None, "tensor"),
        P(None, "tensor"),
        P(None, "tensor"),
        P("tensor", None),
        P(),
        P(None, "tensor"),
        P(None, "tensor"),
        P("tensor", None),
        P(),
        P(),
        P(),
    )
    return jax.shard_map(
        per_device,
        mesh=mesh,
        in_specs=placed,
        out_specs=(
            P(None, ("dp", "tensor")),
            P(None, ("dp", "tensor")),
            P("dp"),
            P("dp", "tensor"),
            P("dp", "tensor"),
            P("dp", "tensor"),
            P("tensor", "dp"),
            P("dp"),
            P("dp", "tensor"),
            P("dp", "tensor"),
            P("tensor", "dp"),
        ),
        check_vma=False,
    )
```

```python
import functools
import math

import jax
import jax.numpy as jnp
from jax import lax
from jax.experimental import pallas as pl
from jax.experimental.pallas import tpu as pltpu
from jax.sharding import PartitionSpec as P

HEAD_WIDTH = 128

MESH = pl.DeviceIdType.MESH
VM = pl.BlockSpec(memory_space=pltpu.VMEM)
F32 = jnp.float32
BF = jnp.bfloat16

def neighbour_barrier(z, n, axis):
    barrier = pltpu.get_barrier_semaphore()
    @pl.when(z > 0)
    def _():
        pl.semaphore_signal(barrier, inc=1, device_id={axis: z - 1}, device_id_type=MESH)
    @pl.when(z < n - 1)
    def _():
        pl.semaphore_signal(barrier, inc=1, device_id={axis: z + 1}, device_id_type=MESH)
    ends = jnp.where(z > 0, 1, 0) + jnp.where(z < n - 1, 1, 0)
    pl.semaphore_wait(barrier, ends)

def rcopy(src, dst, ss, rs, dev):
    return pltpu.make_async_remote_copy(src_ref=src, dst_ref=dst, send_sem=ss, recv_sem=rs, device_id={"tensor": dev}, device_id_type=MESH)


eps = 1e-05
rope_base = 10000.0


def nt(left, right):
    return lax.dot_general(left, right, (((1,), (1,)), ((), ())), preferred_element_type=F32)


def tn(left, right):
    return lax.dot_general(left, right, (((0,), (0,)), ((), ())), preferred_element_type=F32)


def mm(left, right):
    return jnp.dot(left, right, preferred_element_type=F32)


def spin(values, cosine, signed_sine):
    return values * cosine + pltpu.roll(values, HEAD_WIDTH // 2, 1) * signed_sine


def visible(code_row, code_col, low_col):
    return jnp.where((code_row <= code_col) & (code_row >= low_col), 0.0, -1e30)


def attend_kernel(tiles, x, gain, wq, wk, wv, wo, cosine, sine, code_row, code_col, low_col,
                  part, normed, q, k, v, o, lse, scales):
    rows = x.shape[0]
    tile = rows // tiles
    heads = wq.shape[1] // HEAD_WIDTH
    kv = wk.shape[1] // HEAD_WIDTH
    group = heads // kv
    factor = math.log2(math.e) / math.sqrt(HEAD_WIDTH)
    for t in range(tiles):
        r = pl.ds(t * tile, tile)
        xt = x[r, :].astype(F32)
        scale = lax.rsqrt(jnp.mean(xt * xt, axis=1, keepdims=True) + eps)
        scales[r, :] = scale
        n1 = (xt * scale * gain[...]).astype(BF)
        normed[r, :] = n1
        c, s = cosine[r, :], sine[r, :]
        pre = mm(n1, wq[...])
        for h in range(heads):
            cut = slice(h * HEAD_WIDTH, (h + 1) * HEAD_WIDTH)
            q[r, cut] = spin(pre[:, cut], c, s).astype(BF)
        pre = mm(n1, wk[...])
        for h in range(kv):
            cut = slice(h * HEAD_WIDTH, (h + 1) * HEAD_WIDTH)
            k[r, cut] = spin(pre[:, cut], c, s).astype(BF)
        v[r, :] = mm(n1, wv[...]).astype(BF)
        seen = (t + 1) * tile
        bias = visible(code_row[:, :seen], code_col[r, :], low_col[r, :])
        logs = []
        for h in range(heads):
            cut = slice(h * HEAD_WIDTH, (h + 1) * HEAD_WIDTH)
            mine = slice(h // group * HEAD_WIDTH, (h // group + 1) * HEAD_WIDTH)
            scores = nt(q[r, cut], k[:seen, mine]) * factor + bias
            top = jnp.max(scores, axis=1, keepdims=True)
            expo = jnp.exp2(scores - top)
            total = jnp.sum(expo, axis=1, keepdims=True)
            probs = (expo * (1.0 / total)).astype(BF)
            o[r, cut] = mm(probs, v[:seen, mine]).astype(BF)
            logs.append(top + jnp.log2(total))
        lse[r, :] = jnp.concatenate(logs, axis=1)
        part[r, :] = mm(o[r, :], wo[...]).astype(BF)


def attend(tiles, x, gain, wq, wk, wv, wo, *tables):
    rows, width = x.shape
    heads = wq.shape[1] // HEAD_WIDTH
    shapes = [(rows, width), (rows, width), (rows, wq.shape[1]), (rows, wk.shape[1]), (rows, wv.shape[1]), (rows, wq.shape[1])]
    return pl.pallas_call(
        functools.partial(attend_kernel, tiles),
        out_shape=[jax.ShapeDtypeStruct(s, BF) for s in shapes] + [jax.ShapeDtypeStruct((rows, heads), F32), jax.ShapeDtypeStruct((rows, 1), F32)],
        in_specs=[VM] * 11,
        out_specs=[VM] * 8,
        compiler_params=pltpu.CompilerParams(vmem_limit_bytes=56 << 20),
    )(x, gain, wq, wk, wv, wo, *tables)


def attend_back_tile(t, tiles, ga, wq, wk, wv, wo, q, k, v, o, lse, cosine, sine, code_row, code_col, low_col,
                     part, dqkv, dk, dv):
    rows = ga.shape[0]
    tile = rows // tiles
    heads = wq.shape[1] // HEAD_WIDTH
    kv = wk.shape[1] // HEAD_WIDTH
    group = heads // kv
    wide = heads * HEAD_WIDTH
    narrow = kv * HEAD_WIDTH
    score_scale = 1.0 / math.sqrt(HEAD_WIDTH)
    factor = math.log2(math.e) / math.sqrt(HEAD_WIDTH)
    seen = (t + 1) * tile
    block = min(tile, 256)
    for at in range(t * tile, (t + 1) * tile, block):
        r = pl.ds(at, block)
        do = nt(ga[r, :], wo[...]).astype(BF)
        c, s = cosine[r, :], sine[r, :]
        bias = visible(code_row[:, :seen], code_col[r, :], low_col[r, :])
        logs = lse[r, :]
        for h in range(heads):
            cut = slice(h * HEAD_WIDTH, (h + 1) * HEAD_WIDTH)
            mine = slice(h // group * HEAD_WIDTH, (h // group + 1) * HEAD_WIDTH)
            do_h = do[:, cut]
            qh = q[r, cut]
            probs = jnp.exp2(nt(qh, k[:seen, mine]) * factor + bias - logs[:, h : h + 1])
            along = jnp.sum(do_h.astype(F32) * o[r, cut].astype(F32), axis=1, keepdims=True)
            ds = (probs * (nt(do_h, v[:seen, mine]) - along)).astype(BF)
            pb = probs.astype(BF)
            dq = mm(ds, k[:seen, mine]) * score_scale
            dqkv[r, cut] = spin(dq, c, -s).astype(BF)
            more_k = tn(ds, qh)
            more_v = tn(pb, do_h)
            if t == tiles - 1 and at == t * tile and h % group == 0:
                dk[:seen, mine] = more_k
                dv[:seen, mine] = more_v
            else:
                dk[:seen, mine] += more_k
                dv[:seen, mine] += more_v
    for at in range(t * tile, (t + 1) * tile, block):
        r = pl.ds(at, block)
        c, s = cosine[r, :], sine[r, :]
        for h in range(kv):
            cut = slice(h * HEAD_WIDTH, (h + 1) * HEAD_WIDTH)
            low = wide + h * HEAD_WIDTH
            dqkv[r, low : low + HEAD_WIDTH] = spin(dk[r, cut] * score_scale, c, -s).astype(BF)
        dqkv[r, wide + narrow :] = dv[r, :].astype(BF)
        part[r, :] = (
            nt(dqkv[r, :wide], wq[...])
            + nt(dqkv[r, wide : wide + narrow], wk[...])
            + nt(dqkv[r, wide + narrow :], wv[...])
        ).astype(BF)


ANY = pl.BlockSpec(memory_space=pl.ANY)
LAG = 2
CHUNK = 32
BLOCK = 128


def line_row(f, c):
    per = BLOCK // CHUNK
    return pl.ds(pl.multiple_of(lax.div(c, per) * (2 * BLOCK) + f * BLOCK + lax.rem(c, per) * CHUNK, CHUNK), CHUNK)


def line_steps(n, rows):
    return rows // 2 // CHUNK + 2 * LAG * (n - 1)


def line_sum_step(n, z, t, part, up, out, sems):
    us, ur, ds, dr = sems
    count = part.shape[0] // 2 // CHUNK
    for f in range(2):
        p = z if f == 0 else n - 1 - z
        step = 1 if f == 0 else -1
        c = t - LAG * p

        @pl.when((c >= 0) & (c < count))
        def _():
            r = line_row(f, c)

            @pl.when(p == 0)
            def _():
                rcopy(part.at[r], up.at[r], us.at[f, c], ur.at[f, c], z + step).start()

            @pl.when(p > 0)
            def _():
                rcopy(up.at[r], up.at[r], us.at[f, c], ur.at[f, c], z).wait_recv()
                s = (part[r, :].astype(F32) + up[r, :].astype(F32)).astype(BF)

                @pl.when(p < n - 1)
                def _():
                    up[r, :] = s
                    rcopy(up.at[r], up.at[r], us.at[f, c], ur.at[f, c], z + step).start()

                @pl.when(p == n - 1)
                def _():
                    out[r, :] = s
                    rcopy(out.at[r], out.at[r], ds.at[f, c], dr.at[f, c], z - step).start()

    for f in range(2):
        p = z if f == 0 else n - 1 - z
        step = 1 if f == 0 else -1
        c = t - LAG * (2 * (n - 1) - p)

        @pl.when((c >= 0) & (c < count) & (p < n - 1))
        def _():
            r = line_row(f, c)
            rcopy(out.at[r], out.at[r], ds.at[f, c], dr.at[f, c], z).wait_recv()

            @pl.when(p > 0)
            def _():
                rcopy(out.at[r], out.at[r], ds.at[f, c], dr.at[f, c], z - step).start()


def line_sum_drain(n, z, part, up, out, sems):
    us, ur, ds, dr = sems
    count = part.shape[0] // 2 // CHUNK

    def drain(c, _):
        for f in range(2):
            p = z if f == 0 else n - 1 - z
            r = line_row(f, c)

            @pl.when(p < n - 1)
            def _():
                rcopy(up.at[r], up.at[r], us.at[f, c], ur.at[f, c], z).wait_send()

            @pl.when(p > 0)
            def _():
                rcopy(out.at[r], out.at[r], ds.at[f, c], dr.at[f, c], z).wait_send()

        return 0

    lax.fori_loop(0, count, drain, 0)


def line_sum_sems(rows):
    return [pltpu.SemaphoreType.DMA((2, rows // 2 // CHUNK))] * 4


def gather_cut(ref, o, c, w):
    return ref.at[pl.ds(pl.multiple_of(c * BLOCK, BLOCK), BLOCK), pl.ds(pl.multiple_of(o * w, w), w)]


def line_gather_step(n, z, t, src, out, ss, rs):
    rows, w = src.shape
    count = rows // BLOCK

    @pl.when(t < count)
    def _():
        mine = src.at[pl.ds(pl.multiple_of(t * BLOCK, BLOCK), BLOCK)]

        @pl.when(z < n - 1)
        def _():
            rcopy(mine, gather_cut(out, z, t, w), ss.at[0, z, t], rs.at[0, z, t], z + 1).start()

        @pl.when(z > 0)
        def _():
            rcopy(mine, gather_cut(out, z, t, w), ss.at[1, z, t], rs.at[1, z, t], z - 1).start()

    for hop in range(1, n):
        c = t - hop
        for d, step in ((0, 1), (1, -1)):
            o = z - hop * step

            @pl.when((c >= 0) & (c < count) & (o >= 0) & (o < n))
            def _():
                cut = gather_cut(out, o, c, w)
                rcopy(cut, cut, ss.at[d, o, c], rs.at[d, o, c], z).wait_recv()
                after = z + step

                @pl.when((after >= 0) & (after < n))
                def _():
                    rcopy(cut, cut, ss.at[d, o, c], rs.at[d, o, c], after).start()


def line_gather_drain(n, z, src, out, ss, rs):
    rows, w = src.shape

    def drain(c, _):
        for d in range(2):
            for o in range(n):
                on = (o <= z) & (z < n - 1) if d == 0 else (o >= z) & (z > 0)

                @pl.when(on)
                def _():
                    cut = gather_cut(out, o, c, w)
                    rcopy(cut, cut, ss.at[d, o, c], rs.at[d, o, c], z).wait_send()

        return 0

    lax.fori_loop(0, rows // BLOCK, drain, 0)


def middle_kernel(n, part, x, g_part, keep, gain, wg_far, wu_far, wd_far,
                  result, a_far, g_far, n2_far, inner_far, both_far, dn2_far,
                  wg, wu, wd, up, total, g, right, left, gate_s, upper_s, n2_s, inner_s, both_s, f_s, dn2_s,
                  us, ur, ds, dr, ss, rs, fs, fr, load, own, save, late):
    z = lax.axis_index("tensor")
    rows, width = part.shape
    w = g_part.shape[1]
    hidden = wg.shape[1]
    tile = 2 * BLOCK
    sums = (us, ur, ds, dr)
    loads = [pltpu.make_async_copy(a, b, load.at[i]) for i, (a, b) in enumerate(((wg_far, wg), (wu_far, wu), (wd_far, wd)))]
    for copy in loads:
        copy.start()
    mine = pltpu.make_async_copy(g_part, g.at[:, pl.ds(pl.multiple_of(z * w, w), w)], own)
    mine.start()
    neighbour_barrier(z, n, "tensor")

    def saves(d):
        r = pl.ds(pl.multiple_of(d * tile, tile), tile)
        pairs = ((n2_s, n2_far), (inner_s, inner_far), (both_s, both_far), (dn2_s, dn2_far))
        return [pltpu.make_async_copy(a, b.at[r], save.at[i]) for i, (a, b) in enumerate(pairs)]

    first = BLOCK // CHUNK - 1 + 2 * LAG * (n - 1)

    def body(t, _):
        line_sum_step(n, z, t, part, up, total, sums)

        @pl.when(lax.rem(t, 2) == 0)
        def _():
            line_gather_step(n, z, lax.div(t, 2), g_part, g, ss, rs)

        q = t - first
        d = lax.div(jnp.maximum(q, 0), 4)
        k = lax.rem(jnp.maximum(q, 0), 4)
        r = pl.ds(pl.multiple_of(d * tile, tile), tile)

        @pl.when((q >= 0) & (d < rows // tile) & (k == 0))
        def _():
            @pl.when(d == 0)
            def _():
                for copy in loads:
                    copy.wait()
                mine.wait()

            @pl.when(d > 0)
            def _():
                for copy in saves(d - 1):
                    copy.wait()

            h = x[r, :].astype(F32) + keep[r, :] * total[r, :].astype(F32)
            scale = lax.rsqrt(jnp.mean(h * h, axis=1, keepdims=True) + eps)
            n2_s[...] = (h * scale * gain[...]).astype(BF)
            gate_s[...] = mm(n2_s[...], wg[...])

        @pl.when((q >= 0) & (d < rows // tile) & (k == 1))
        def _():
            upper_s[...] = mm(n2_s[...], wu[...])
            gate = gate_s[...]
            inner_s[...] = (gate * jax.nn.sigmoid(gate) * upper_s[...]).astype(BF)

        @pl.when((q >= 0) & (d < rows // tile) & (k == 2))
        def _():
            f_s[lax.rem(d, 2)] = mm(inner_s[...], wd[...]).astype(BF)
            gf = (keep[r, :] * g[r, :].astype(F32)).astype(BF)
            back = nt(gf, wd[...])
            gate = gate_s[...]
            s = jax.nn.sigmoid(gate)
            both_s[:, :hidden] = (back * upper_s[...] * s * (1.0 + gate * (1.0 - s))).astype(BF)
            both_s[:, hidden:] = (back * (gate * s)).astype(BF)

        @pl.when((q >= 0) & (d < rows // tile) & (k == 3))
        def _():
            dn2_s[...] = (nt(both_s[:, :hidden], wg[...]) + nt(both_s[:, hidden:], wu[...])).astype(BF)
            for copy in saves(d):
                copy.start()

        scatter_step(t - first - 2)
        return 0

    chunk = tile // 4
    count = rows // chunk

    def at(ref, c, b):
        return ref.at[pl.ds(pl.multiple_of(c * chunk, chunk), chunk), pl.ds(b * w, w)]

    def scatter_copy(buf, d, c, b, to):
        return rcopy(at(buf, c, b), at(buf, c, b), fs.at[d, b, c], fr.at[d, b, c], to)

    def scatter_step(s):
        for d, buf, step in ((0, right, 1), (1, left, -1)):
            p = z if d == 0 else n - 1 - z
            c = s - p

            @pl.when((c >= 0) & (c < count))
            def _():
                r = pl.ds(pl.multiple_of(c * chunk, chunk), chunk)
                slot = lax.rem(lax.div(c, 4), 2)
                inner = pl.ds(pl.multiple_of(lax.rem(c, 4) * chunk, chunk), chunk)
                for b in range(n - 1, 0, -1) if d == 0 else range(n - 1):
                    k = pl.ds(b * w, w)

                    @pl.when((b > z) if d == 0 else (b < z))
                    def _():
                        @pl.when(p == 0)
                        def _():
                            buf[r, k] = f_s[slot, inner, k]

                        @pl.when(p > 0)
                        def _():
                            scatter_copy(buf, d, c, b, z).wait_recv()
                            buf[r, k] = (f_s[slot, inner, k].astype(F32) + buf[r, k].astype(F32)).astype(BF)

                        scatter_copy(buf, d, c, b, z + step).start()

        c = s - (n - 1)

        @pl.when((c >= 0) & (c < count))
        def _():
            r = pl.ds(pl.multiple_of(c * chunk, chunk), chunk)
            slot = lax.rem(lax.div(c, 4), 2)
            inner = pl.ds(pl.multiple_of(lax.rem(c, 4) * chunk, chunk), chunk)
            for b in range(n):
                k = pl.ds(b * w, w)

                @pl.when(z == b)
                def _():
                    f = f_s[slot, inner, k].astype(F32)
                    if b > 0:
                        scatter_copy(right, 0, c, b, z).wait_recv()
                        f = f + right[r, k].astype(F32)
                    if b < n - 1:
                        scatter_copy(left, 1, c, b, z).wait_recv()
                        f = f + left[r, k].astype(F32)
                    kept = keep[r, :]
                    h = x[r, k].astype(F32) + kept * total[r, k].astype(F32)
                    result[r, :] = (h + kept * f).astype(BF)

    lax.fori_loop(0, first + 2 + count + n, body, 0)

    def drain(c, _):
        for d, buf in ((0, right), (1, left)):
            for b in range(n):

                @pl.when((b > z) if d == 0 else (b < z))
                def _():
                    scatter_copy(buf, d, c, b, z).wait_send()

        return 0

    lax.fori_loop(0, count, drain, 0)
    ends = [pltpu.make_async_copy(a, b, late.at[i]) for i, (a, b) in enumerate(((total, a_far), (g, g_far)))]
    for copy in ends:
        copy.start()
    line_sum_drain(n, z, part, up, total, sums)
    line_gather_drain(n, z, g_part, g, ss, rs)
    for copy in saves(rows // tile - 1) + ends:
        copy.wait()


def middle(n, part, x, g_part, keep, gain, wg, wu, wd):
    rows, width = part.shape
    hidden = wg.shape[1]
    tile = 2 * BLOCK
    blocks = rows // BLOCK
    w = g_part.shape[1]
    widths = (w, width, width, width, hidden, 2 * hidden, width)
    return pl.pallas_call(
        functools.partial(middle_kernel, n),
        out_shape=[jax.ShapeDtypeStruct((rows, k), BF) for k in widths],
        in_specs=[VM] * 5 + [ANY] * 3,
        out_specs=[VM] + [ANY] * 6,
        scratch_shapes=[
            pltpu.VMEM(wg.shape, BF),
            pltpu.VMEM(wu.shape, BF),
            pltpu.VMEM(wd.shape, BF),
            pltpu.VMEM((rows, width), BF),
            pltpu.VMEM((rows, width), BF),
            pltpu.VMEM((rows, width), BF),
            pltpu.VMEM((rows, width), BF),
            pltpu.VMEM((rows, width), BF),
            pltpu.VMEM((tile, hidden), F32),
            pltpu.VMEM((tile, hidden), F32),
            pltpu.VMEM((tile, width), BF),
            pltpu.VMEM((tile, hidden), BF),
            pltpu.VMEM((tile, 2 * hidden), BF),
            pltpu.VMEM((2, tile, width), BF),
            pltpu.VMEM((tile, width), BF),
            *line_sum_sems(rows),
            pltpu.SemaphoreType.DMA((2, n, blocks)),
            pltpu.SemaphoreType.DMA((2, n, blocks)),
            pltpu.SemaphoreType.DMA((2, n, rows // tile * 4)),
            pltpu.SemaphoreType.DMA((2, n, rows // tile * 4)),
            pltpu.SemaphoreType.DMA((3,)),
            pltpu.SemaphoreType.DMA,
            pltpu.SemaphoreType.DMA((4,)),
            pltpu.SemaphoreType.DMA((2,)),
        ],
        compiler_params=pltpu.CompilerParams(collective_id=3, has_side_effects=True, vmem_limit_bytes=63 << 20),
    )(part, x, g_part, keep, gain, wg, wu, wd)


def second_back_kernel(n, part, x, a, g, keep, gain, inner_far, ga, dh, gain_grad, grad_far,
                       up, total, inner, stage, us, ur, ds, dr, load, save):
    z = lax.axis_index("tensor")
    rows, width = part.shape
    w = dh.shape[1]
    piece = BLOCK // 2
    sums = (us, ur, ds, dr)
    loads = [pltpu.make_async_copy(inner_far, inner, load.at[0])]
    for copy in loads:
        copy.start()
    neighbour_barrier(z, n, "tensor")
    span = stage.shape[1]
    spans = width // span

    def saved(j):
        slot = lax.rem(j, 2)
        return pltpu.make_async_copy(stage.at[slot], grad_far.at[pl.ds(pl.multiple_of(j * span, span), span)], save.at[slot])

    gain_grad[...] = jnp.zeros_like(gain_grad)
    first = BLOCK // CHUNK - 1 + 2 * LAG * (n - 1)

    def body(t, _):
        line_sum_step(n, z, t, part, up, total, sums)
        j = t - 3

        @pl.when((j >= 0) & (j < spans))
        def _():
            @pl.when(j == 0)
            def _():
                for copy in loads:
                    copy.wait()

            @pl.when(j >= 2)
            def _():
                saved(j - 2).wait()

            cut = pl.ds(pl.multiple_of(j * span, span), span)
            gf = (keep[...] * g[:, cut].astype(F32)).astype(BF)
            stage[lax.rem(j, 2)] = tn(gf, inner[...]).astype(BF)
            saved(j).start()

        q = t - first

        @pl.when(q >= 0)
        def _():
            r = pl.ds(pl.multiple_of(q * piece, piece), piece)
            h = x[r, :].astype(F32) + keep[r, :] * a[r, :].astype(F32)
            scale = lax.rsqrt(jnp.mean(h * h, axis=1, keepdims=True) + eps)
            back = total[r, :].astype(F32)
            gain_grad[...] += jnp.sum(back * h * scale, axis=0, keepdims=True)
            e = back * gain[...]
            along = jnp.mean(e * h, axis=1, keepdims=True)
            full = g[r, :].astype(F32) + scale * e - h * (scale * scale * scale * along)
            ga[r, :] = (keep[r, :] * full).astype(BF)
            for b in range(n):

                @pl.when(z == b)
                def _():
                    dh[r, :] = full[:, b * w : (b + 1) * w]

        return 0

    lax.fori_loop(0, first + rows // piece, body, 0)
    line_sum_drain(n, z, part, up, total, sums)
    for j in range(spans - 2, spans):
        saved(j).wait()


def second_back_of(n, part, x, a, g, keep, gain, inner):
    rows, width = part.shape
    return pl.pallas_call(
        functools.partial(second_back_kernel, n),
        out_shape=[
            jax.ShapeDtypeStruct((rows, width), BF),
            jax.ShapeDtypeStruct((rows, width // n), F32),
            jax.ShapeDtypeStruct((1, width), F32),
            jax.ShapeDtypeStruct((width, inner.shape[1]), BF),
        ],
        in_specs=[VM] * 6 + [ANY],
        out_specs=[VM] * 3 + [ANY],
        scratch_shapes=[
            pltpu.VMEM((rows, width), BF),
            pltpu.VMEM((rows, width), BF),
            pltpu.VMEM(inner.shape, BF),
            pltpu.VMEM((2, 256, inner.shape[1]), BF),
            *line_sum_sems(rows),
            pltpu.SemaphoreType.DMA((2,)),
            pltpu.SemaphoreType.DMA((2,)),
        ],
        compiler_params=pltpu.CompilerParams(collective_id=4, has_side_effects=True, vmem_limit_bytes=60 << 20),
    )(part, x, a, g, keep, gain, inner)


def peers_barrier(z, n, me, groups, everyone):
    barrier = pltpu.get_barrier_semaphore()

    def greet(off, _):
        peer = lax.rem(me + off, groups)
        pl.semaphore_signal(barrier, inc=1, device_id={"dp": peer}, device_id_type=MESH)
        return 0

    lax.fori_loop(1, groups, greet, 0)
    if everyone:
        for off in range(1, n):
            other = lax.rem(z + off, n)
            pl.semaphore_signal(barrier, inc=1, device_id={"tensor": other}, device_id_type=MESH)
        pl.semaphore_wait(barrier, groups - 1 + n - 1)
    else:

        @pl.when(z > 0)
        def _():
            pl.semaphore_signal(barrier, inc=1, device_id={"tensor": z - 1}, device_id_type=MESH)

        @pl.when(z < n - 1)
        def _():
            pl.semaphore_signal(barrier, inc=1, device_id={"tensor": z + 1}, device_id_type=MESH)

        ends = jnp.where(z > 0, 1, 0) + jnp.where(z < n - 1, 1, 0)
        pl.semaphore_wait(barrier, groups - 1 + ends)


def pcopy(src, dst, ss, rs, peer):
    return pltpu.make_async_remote_copy(
        src_ref=src, dst_ref=dst, send_sem=ss, recv_sem=rs, device_id={"dp": peer}, device_id_type=MESH
    )


def deal_in_kernel(n, groups, dealt_x, dealt_g, full, g_part, xs, xr, gs, gr, ss, rs, own):
    z = lax.axis_index("tensor")
    me = lax.axis_index("dp")
    tiles, sub, w = dealt_x.shape[1:]
    cols = pl.ds(pl.multiple_of(z * w, w), w)

    def place(t, i):
        return full.at[t, i, :, cols]

    for t in range(tiles):
        pltpu.make_async_copy(dealt_x.at[me, t], place(t, me), own.at[t]).start()
    pltpu.make_async_copy(dealt_g.at[me], g_part.at[:, me], own.at[tiles]).start()
    peers_barrier(z, n, me, groups, False)

    def send(t):
        def one(off, _):
            peer = lax.rem(me + off, groups)
            pcopy(dealt_x.at[peer, t], place(t, me), xs.at[t, peer], xr.at[t, me], peer).start()
            return 0

        lax.fori_loop(1, groups, one, 0)

    def cut(o, t):
        return full.at[t, :, :, pl.ds(pl.multiple_of(o * w, w), w)]

    for t in range(tiles):
        send(t)

    def send_g(off, _):
        peer = lax.rem(me + off, groups)
        pcopy(dealt_g.at[peer], g_part.at[:, me], gs.at[peer], gr.at[me], peer).start()
        return 0

    lax.fori_loop(1, groups, send_g, 0)
    for s in range(tiles + n - 1):
        if s < tiles:

            def got(off, _):
                peer = lax.rem(me + off, groups)
                pcopy(dealt_x.at[peer, s], place(s, peer), xs.at[s, peer], xr.at[s, peer], peer).wait_recv()
                return 0

            lax.fori_loop(1, groups, got, 0)
            pltpu.make_async_copy(dealt_x.at[me, s], place(s, me), own.at[s]).wait()

            @pl.when(z < n - 1)
            def _():
                rcopy(cut(z, s), cut(z, s), ss.at[0, z, s], rs.at[0, z, s], z + 1).start()

            @pl.when(z > 0)
            def _():
                rcopy(cut(z, s), cut(z, s), ss.at[1, z, s], rs.at[1, z, s], z - 1).start()

        for hop in range(1, n):
            c = s - hop
            if 0 <= c < tiles:
                for d, step in ((0, 1), (1, -1)):
                    o = z - hop * step

                    @pl.when((o >= 0) & (o < n))
                    def _():
                        rcopy(cut(o, c), cut(o, c), ss.at[d, o, c], rs.at[d, o, c], z).wait_recv()
                        after = z + step

                        @pl.when((after >= 0) & (after < n))
                        def _():
                            rcopy(cut(o, c), cut(o, c), ss.at[d, o, c], rs.at[d, o, c], after).start()

    def finish(off, _):
        peer = lax.rem(me + off, groups)
        copy = pcopy(dealt_g.at[peer], g_part.at[:, peer], gs.at[peer], gr.at[peer], peer)
        copy.wait_recv()
        copy.wait_send()
        for t in range(tiles):
            pcopy(dealt_x.at[peer, t], place(t, peer), xs.at[t, peer], xr.at[t, peer], peer).wait_send()
        return 0

    lax.fori_loop(1, groups, finish, 0)
    pltpu.make_async_copy(dealt_g.at[me], g_part.at[:, me], own.at[tiles]).wait()
    for c in range(tiles):
        for d in range(2):
            for o in range(n):

                @pl.when((o <= z) & (z < n - 1) if d == 0 else (o >= z) & (z > 0))
                def _():
                    rcopy(cut(o, c), cut(o, c), ss.at[d, o, c], rs.at[d, o, c], z).wait_send()


def deal_in(n, groups, dealt_x, dealt_g):
    tiles, sub, w = dealt_x.shape[1:]
    dma = pltpu.SemaphoreType.DMA
    return pl.pallas_call(
        functools.partial(deal_in_kernel, n, groups),
        out_shape=[
            jax.ShapeDtypeStruct((tiles, groups, sub, n * w), BF),
            jax.ShapeDtypeStruct((tiles, groups, sub, w), BF),
        ],
        in_specs=[VM] * 2,
        out_specs=[VM] * 2,
        scratch_shapes=[
            dma((tiles, groups)),
            dma((tiles, groups)),
            dma((groups,)),
            dma((groups,)),
            dma((2, n, tiles)),
            dma((2, n, tiles)),
            dma((tiles + 1,)),
        ],
        compiler_params=pltpu.CompilerParams(collective_id=6, has_side_effects=True, vmem_limit_bytes=48 << 20),
    )(dealt_x, dealt_g)


def exact(left, right, contract):
    return lax.dot_general(
        left, right, (contract, ((), ())), preferred_element_type=F32, precision=lax.Precision.HIGHEST
    )


def deal_out_kernel(n, groups, tiles, chunk, lag, x, dh, scale1, gain1, result, gain2, normed, *refs):
    attention = refs[:15]
    (back_out, back_dx, gains, shares, part, dqkv, dk, dv, right, left, fb, dx, lines, widths, gsrc, gdst, wsrc, wdst, pair,
     ss, rs, os, orr, xs, xr, ls, lr, ws, wr, es, er, qs, qr, ps, pr, own) = refs[15:]
    ga, o = attention[0], attention[8]
    z = lax.axis_index("tensor")
    me = lax.axis_index("dp")
    rows, w = x.shape
    tile = rows // tiles
    count = rows // chunk
    per = tile // chunk
    sub = result.shape[2]
    pltpu.make_async_copy(result.at[:, me], back_out.at[me], own.at[0]).start()
    peers_barrier(z, n, me, groups, True)

    def send_out(off, _):
        peer = lax.rem(me + off, groups)
        pcopy(result.at[:, peer], back_out.at[me], os.at[peer], orr.at[me], peer).start()
        return 0

    lax.fori_loop(1, groups, send_out, 0)

    def chunk_rows(c):
        t = tiles - 1 - lax.div(c, per)
        return pl.ds(pl.multiple_of(t * tile + lax.rem(c, per) * chunk, chunk), chunk)

    def at(ref, c, b):
        return ref.at[chunk_rows(c), pl.ds(b * w, w)]

    widths[...] = jnp.zeros_like(widths)

    def others(f):
        for off in range(1, n):
            f(lax.rem(z + off, n))

    def line_copy(t, slot, other):
        cut = lines.at[slot, :, pl.ds(pl.multiple_of(t * tile, tile), tile)]
        return rcopy(cut, cut, ls.at[other, t], lr.at[slot, t], other)

    def width_copy(slot, other):
        cut = widths.at[slot]
        return rcopy(cut, cut, ws.at[other], wr.at[slot], other)

    def open_tile(t):
        r = pl.ds(pl.multiple_of(t * tile, tile), tile)
        e = fb[r, :] * gain1[...]
        xt = x[r, :].astype(F32)
        lines[z, :, r] = exact(jnp.ones((8, w), F32), e * xt, ((1,), (1,)))
        others(lambda other: line_copy(t, z, other).start())
        grown = jnp.sum(fb[r, :] * xt * scale1[r, :], axis=0, keepdims=True)
        widths[z, :, :] += jnp.broadcast_to(grown, (8, w))

        @pl.when(t == 0)
        def _():
            others(lambda other: width_copy(z, other).start())

    def close_tile(t):
        r = pl.ds(pl.multiple_of(t * tile, tile), tile)
        others(lambda other: line_copy(t, other, other).wait_recv())
        total = lines[0, :, r]
        for j in range(1, n):
            total = total + lines[j, :, r]
        along = exact(total * (1.0 / (8 * n * w)), jnp.ones((8, w), F32), ((0,), (0,)))
        e = fb[r, :] * gain1[...]
        s = scale1[r, :]
        full = dh[r, :] + s * e - x[r, :].astype(F32) * (s * s * s * along)
        dx[t] = full.astype(BF).reshape(groups, sub, w)
        pltpu.make_async_copy(dx.at[t, me], back_dx.at[me, t], own.at[1 + t]).start()

        def one(off, _):
            peer = lax.rem(me + off, groups)
            pcopy(dx.at[t, peer], back_dx.at[me, t], xs.at[t, peer], xr.at[t, me], peer).start()
            return 0

        lax.fori_loop(1, groups, one, 0)

    ow = o.shape[1]
    share = normed.shape[1] // groups
    span = max(share, 256)

    half = groups // 2
    seat = lax.div(me, 2)
    parity = lax.rem(me, 2)
    partner = me + 1 - 2 * parity

    def rows_of(owner):
        return pl.ds(pl.multiple_of(owner * share, share), share)

    def weight_copy(kind, src, dst, sems, to, slot, at_column, wide):
        columns = pl.ds(at_column, wide)
        return pltpu.make_async_remote_copy(
            src_ref=wsrc.at[rows_of(src), columns],
            dst_ref=dst.at[slot, :, columns],
            send_sem=sems[0].at[kind, lax.div(src, 2)],
            recv_sem=sems[1].at[kind, slot],
            device_id={"dp": to},
            device_id_type=MESH,
        )

    def weigh(left_ref, right_ref, at_column, kind):
        wide = right_ref.shape[1]

        def one(j, _):
            base = pl.multiple_of(j * span, span)
            cut = pl.ds(base, span)
            wsrc[cut, at_column : at_column + wide] = tn(left_ref[:, cut], right_ref[...]).astype(BF)
            for i in range(span // share):
                owner = lax.div(base, share) + i

                @pl.when(lax.rem(owner, 2) != parity)
                def _():
                    weight_copy(kind, owner, pair, (ps, pr), partner, lax.div(owner, 2), at_column, wide).start()

            return 0

        lax.fori_loop(0, normed.shape[1] // span, one, 0)

    def join(at_column, wide, kind):
        columns = slice(at_column, at_column + wide)

        def one(off, _):
            m = lax.rem(seat + off, half)
            owner = 2 * m + parity
            weight_copy(kind, owner, pair, (ps, pr), partner, m, at_column, wide).wait_recv()
            r = rows_of(owner)
            total = (wsrc[r, columns].astype(F32) + pair[m, :, columns].astype(F32)).astype(BF)

            @pl.when(owner == me)
            def _():
                wdst[seat, :, columns] = total

            @pl.when(owner != me)
            def _():
                wsrc[r, columns] = total
                weight_copy(kind, owner, wdst, (qs, qr), owner, seat, at_column, wide).start()

            return 0

        lax.fori_loop(1, half + 1, one, 0)

    joined = ((0, ow), (ow, dqkv.shape[1]))

    def flows(s, _):
        for k in range(tiles):

            @pl.when(s == k * per)
            def _():
                attend_back_tile(tiles - 1 - k, tiles, *attention, part, dqkv, dk, dv)

        @pl.when(s == 2)
        def _():
            weigh(ga, o, 0, 0)

        @pl.when(s == 5)
        def _():
            join(*joined[0], 0)

        @pl.when(s == (tiles - 1) * per + 3)
        def _():
            join(*joined[1], 1)

        @pl.when(s == (tiles - 1) * per + 1)
        def _():
            weigh(normed, dqkv, ow, 1)

        for d, buf, step in ((0, right, 1), (1, left, -1)):
            p = z if d == 0 else n - 1 - z
            c = s - lag * p

            @pl.when((c >= 0) & (c < count))
            def _():
                r = chunk_rows(c)
                for b in range(n - 1, 0, -1) if d == 0 else range(n - 1):
                    k = pl.ds(b * w, w)

                    @pl.when((b > z) if d == 0 else (b < z))
                    def _():
                        @pl.when(p == 0)
                        def _():
                            rcopy(at(part, c, b), at(buf, c, b), ss.at[d, b, c], rs.at[d, b, c], z + step).start()

                        @pl.when(p > 0)
                        def _():
                            rcopy(at(buf, c, b), at(buf, c, b), ss.at[d, b, c], rs.at[d, b, c], z).wait_recv()
                            buf[r, k] = (part[r, k].astype(F32) + buf[r, k].astype(F32)).astype(BF)
                            rcopy(at(buf, c, b), at(buf, c, b), ss.at[d, b, c], rs.at[d, b, c], z + step).start()

        c = s - lag * (n - 1)

        @pl.when((c >= 0) & (c < count))
        def _():
            r = chunk_rows(c)
            for b in range(n):
                k = pl.ds(b * w, w)

                @pl.when(z == b)
                def _():
                    total = part[r, k].astype(F32)
                    if b > 0:
                        rcopy(at(right, c, b), at(right, c, b), ss.at[0, b, c], rs.at[0, b, c], z).wait_recv()
                        total = total + right[r, k].astype(F32)
                    if b < n - 1:
                        rcopy(at(left, c, b), at(left, c, b), ss.at[1, b, c], rs.at[1, b, c], z).wait_recv()
                        total = total + left[r, k].astype(F32)
                    fb[r, :] = total

        @pl.when((c >= 0) & (c < count) & (lax.rem(jnp.maximum(c, 0), per) == per - 1))
        def _():
            open_tile(tiles - 1 - lax.div(c, per))

        c = c - 2

        @pl.when((c >= 0) & (lax.rem(jnp.maximum(c, 0), per) == per - 1))
        def _():
            close_tile(tiles - 1 - lax.div(c, per))

        return 0

    lax.fori_loop(0, count + lag * (n - 1) + 2, flows, 0)

    others(lambda other: width_copy(other, other).wait_recv())
    cols = gsrc.shape[2]
    first_gain = jnp.concatenate([widths[j] for j in range(n)], axis=1)
    second_gain = jnp.broadcast_to(gain2[...], first_gain.shape)
    for i in range(groups):
        gsrc[i, :8, :] = first_gain[:, i * cols : (i + 1) * cols]
        gsrc[i, 8:, :] = second_gain[:, i * cols : (i + 1) * cols]
    pltpu.make_async_copy(gsrc.at[me], gdst.at[me], own.at[1 + tiles]).start()

    def send_gain(off, _):
        peer = lax.rem(me + off, groups)
        pcopy(gsrc.at[peer], gdst.at[me], es.at[peer], er.at[me], peer).start()
        return 0

    lax.fori_loop(1, groups, send_gain, 0)

    def got_gain(off, _):
        peer = lax.rem(me + off, groups)
        copy = pcopy(gsrc.at[peer], gdst.at[peer], es.at[peer], er.at[peer], peer)
        copy.wait_recv()
        copy.wait_send()
        return 0

    lax.fori_loop(1, groups, got_gain, 0)
    pltpu.make_async_copy(gsrc.at[me], gdst.at[me], own.at[1 + tiles]).wait()
    total = gdst[0]
    for i in range(1, groups):
        total = total + gdst[i]
    gains[...] = total

    def got_weight(off, _):
        m = lax.rem(seat + off, half)
        for kind, (at_column, wide) in enumerate(joined):
            copy = weight_copy(kind, 2 * m + parity, wdst, (qs, qr), me, m, at_column, wide)
            copy.wait_recv()
            copy.wait_send()
        return 0

    def sent_weight(m, _):
        for kind, (at_column, wide) in enumerate(joined):
            weight_copy(kind, 2 * m + 1 - parity, pair, (ps, pr), partner, m, at_column, wide).wait_send()
        return 0

    lax.fori_loop(1, half, got_weight, 0)
    lax.fori_loop(0, half, sent_weight, 0)
    shares[...] = wdst[0].astype(F32)
    for i in range(1, half):
        shares[...] += wdst[i].astype(F32)

    def finish(off, _):
        peer = lax.rem(me + off, groups)
        copy = pcopy(result.at[:, peer], back_out.at[peer], os.at[peer], orr.at[peer], peer)
        copy.wait_recv()
        copy.wait_send()
        for t in range(tiles):
            copy = pcopy(dx.at[t, peer], back_dx.at[peer, t], xs.at[t, peer], xr.at[t, peer], peer)
            copy.wait_recv()
            copy.wait_send()
        return 0

    lax.fori_loop(1, groups, finish, 0)
    pltpu.make_async_copy(result.at[:, me], back_out.at[me], own.at[0]).wait()
    for t in range(tiles):
        pltpu.make_async_copy(dx.at[t, me], back_dx.at[me, t], own.at[1 + t]).wait()
        others(lambda other: line_copy(t, z, other).wait_send())
    others(lambda other: width_copy(z, other).wait_send())

    def drain(c, _):
        for d, buf in ((0, right), (1, left)):
            for b in range(n):

                @pl.when((b > z) if d == 0 else (b < z))
                def _():
                    rcopy(at(buf, c, b), at(buf, c, b), ss.at[d, b, c], rs.at[d, b, c], z).wait_send()

        return 0

    lax.fori_loop(0, count, drain, 0)


def deal_out(n, groups, tiles, x, dh, scale1, gain1, result, gain2, normed, *attention, chunk=64, lag=2):
    rows, w = x.shape
    width = n * w
    sub = rows // tiles // groups
    count = rows // chunk
    cols = width // groups
    joined = sum(a.shape[1] for a in attention[1:4])
    narrow = attention[2].shape[1]
    both = attention[8].shape[1] + joined
    dma = pltpu.SemaphoreType.DMA
    dealt = (groups, tiles, sub, w)
    return pl.pallas_call(
        functools.partial(deal_out_kernel, n, groups, tiles, chunk, lag),
        out_shape=[
            jax.ShapeDtypeStruct(dealt, BF),
            jax.ShapeDtypeStruct(dealt, BF),
            jax.ShapeDtypeStruct((16, cols), F32),
            jax.ShapeDtypeStruct((cols, both), F32),
        ],
        in_specs=[VM] * 22,
        out_specs=[VM] * 4,
        scratch_shapes=[
            pltpu.VMEM((rows, width), BF),
            pltpu.VMEM((rows, joined), BF),
            pltpu.VMEM((rows, narrow), F32),
            pltpu.VMEM((rows, narrow), F32),
            pltpu.VMEM((rows, width), BF),
            pltpu.VMEM((rows, width), BF),
            pltpu.VMEM((rows, w), F32),
            pltpu.VMEM((tiles, groups, sub, w), BF),
            pltpu.VMEM((n, 8, rows), F32),
            pltpu.VMEM((n, 8, w), F32),
            pltpu.VMEM((groups, 16, cols), F32),
            pltpu.VMEM((groups, 16, cols), F32),
            pltpu.VMEM((width, both), BF),
            pltpu.VMEM((groups // 2, cols, both), BF),
            pltpu.VMEM((groups // 2, cols, both), BF),
            dma((2, n, count)),
            dma((2, n, count)),
            dma((groups,)),
            dma((groups,)),
            dma((tiles, groups)),
            dma((tiles, groups)),
            dma((n, tiles)),
            dma((n, tiles)),
            dma((n,)),
            dma((n,)),
            dma((groups,)),
            dma((groups,)),
            dma((2, groups // 2)),
            dma((2, groups // 2)),
            dma((2, groups // 2)),
            dma((2, groups // 2)),
            dma((tiles + 2,)),
        ],
        compiler_params=pltpu.CompilerParams(collective_id=5, has_side_effects=True, vmem_limit_bytes=62 << 20),
    )(x, dh, scale1, gain1, result.reshape(tiles, groups, sub, w), gain2, normed, *attention)


def rotary_tables(token_positions, head_size):
    half = head_size // 2
    freqs = rope_base ** (-(jnp.arange(half).astype(jnp.float32) * 2.0) / head_size)
    angles = token_positions.astype(jnp.float32)[:, None] * freqs[None, :]
    angles = jnp.concatenate([angles, angles], axis=1)
    return (jnp.cos(angles), jnp.sin(angles))


def matmul(left, right):
    return jnp.dot(left, right, preferred_element_type=jnp.float32)


def per_device(
    tokens,
    cotangent,
    first_gain,
    query_weight,
    key_matrix,
    value_matrix,
    output_weight,
    second_gain,
    gate_weight,
    up_weight,
    down_weight,
    seq_lengths,
    owner_order,
    skip_mask,
):
    groups = lax.axis_size("dp")
    member = lax.axis_index("dp")
    width_part = tokens.shape[1]
    row_count = tokens.shape[0]
    per_owner = row_count // groups
    seq_count = seq_lengths.shape[0]
    seq_index = jnp.arange(seq_count, dtype=jnp.int32)
    before = (seq_index[None, :] < seq_index[:, None]).astype(jnp.int32)
    unit_lengths = seq_lengths // groups
    unit_starts = jnp.sum(before * unit_lengths[None, :], axis=1)
    placed = (owner_order[:, None] == seq_index[None, :]).astype(jnp.int32)
    order_lengths = jnp.sum(placed * unit_lengths[None, :], axis=1)
    order_starts = jnp.sum(placed * unit_starts[None, :], axis=1)
    order_keep = jnp.sum(placed * skip_mask[None, :], axis=1)
    order_before = jnp.sum(before * order_lengths[None, :], axis=1)
    places = jnp.arange(row_count, dtype=jnp.int32)
    covers = (
        (places[:, None] >= order_before[None, :])
        & (places[:, None] < (order_before + order_lengths)[None, :])
    ).astype(jnp.int32)
    send_rows = places + jnp.sum(covers * (order_starts - order_before)[None, :], axis=1)
    given_before = jnp.sum(placed * order_before[:, None], axis=0)
    given_covers = (
        (places[:, None] >= unit_starts[None, :])
        & (places[:, None] < (unit_starts + unit_lengths)[None, :])
    ).astype(jnp.int32)
    slot_of = places + jnp.sum(given_covers * (given_before - unit_starts)[None, :], axis=1)
    my_places = member * per_owner + jnp.arange(per_owner, dtype=jnp.int32)
    my_covers = (
        (my_places[:, None] >= order_before[None, :])
        & (my_places[:, None] < (order_before + order_lengths)[None, :])
    ).astype(jnp.int32)
    slot_seq = jnp.sum(my_covers * seq_index[None, :], axis=1)
    slot_step = my_places - jnp.sum(my_covers * order_before[None, :], axis=1)
    slot_keep = jnp.sum(my_covers * order_keep[None, :], axis=1)
    tiles = max(1, per_owner // 32)
    sources = jnp.arange(groups, dtype=jnp.int32)[None, :, None]

    def spread(values):
        values = values.reshape(tiles, 1, per_owner // tiles)
        return jnp.broadcast_to(values, (tiles, groups, per_owner // tiles)).reshape(row_count)

    token_positions = (
        sources + groups * slot_step.reshape(tiles, 1, per_owner // tiles)
    ).reshape(row_count)
    lowest = spread(slot_seq) * row_count
    code = lowest + token_positions
    keep_rows = spread(slot_keep).reshape(row_count, 1).astype(jnp.float32)
    chosen = (send_rows[:, None] == places[None, :]).astype(jnp.bfloat16)
    put_back = (slot_of[:, None] == places[None, :]).astype(jnp.bfloat16)

    tensor_count = lax.axis_size("tensor")
    tensor_member = lax.axis_index("tensor")
    dealt_shape = (groups, tiles, per_owner // tiles, width_part)
    owned_tokens, part_cotangent = deal_in(
        tensor_count,
        groups,
        *(
            matmul(chosen, values).astype(BF).reshape(dealt_shape)
            for values in (tokens, cotangent)
        ),
    )
    owned_tokens = owned_tokens.reshape(row_count, -1)
    part_cotangent = part_cotangent.reshape(row_count, width_part)

    def my_part(values):
        return lax.dynamic_slice_in_dim(values, tensor_member * width_part, width_part, 1)

    cosine, sine = rotary_tables(token_positions, HEAD_WIDTH)
    half = HEAD_WIDTH // 2
    tables = (
        cosine,
        jnp.concatenate([-sine[:, :half], sine[:, half:]], axis=1),
        code[None, :],
        code[:, None],
        lowest[:, None],
    )
    weights = (query_weight, key_matrix, value_matrix, output_weight)
    attn_part, normed_one, *kept, scale_one = attend(
        tiles, owned_tokens, first_gain[None, :], *weights, *tables
    )
    result, attn_sum, owned_cotangent, normed_two, inner_low, both, second_term = middle(
        tensor_count,
        attn_part,
        owned_tokens,
        part_cotangent,
        keep_rows,
        second_gain[None, :],
        gate_weight,
        up_weight,
        down_weight,
    )
    hidden = gate_weight.shape[1]

    def shared(values):
        return lax.psum_scatter(
            values.astype(jnp.bfloat16), "dp", scatter_dimension=0, tiled=True
        ).astype(jnp.float32)

    both_grad = matmul(normed_two.T, both).astype(BF)
    second_term, both_grad = lax.optimization_barrier((second_term, both_grad))
    both_share = shared(both_grad)
    grad_attn, grad_res, second_gain_grad, down_grad = second_back_of(
        tensor_count,
        second_term,
        owned_tokens,
        attn_sum,
        owned_cotangent,
        keep_rows,
        second_gain[None, :],
        inner_low,
    )
    both_share, down_grad, grad_attn = lax.optimization_barrier(
        (both_share, down_grad, grad_attn)
    )
    down_share = shared(down_grad)
    back_out, back_grad, gains, first = deal_out(
        tensor_count,
        groups,
        tiles,
        my_part(owned_tokens),
        grad_res,
        scale_one,
        my_part(first_gain[None, :]),
        result,
        second_gain_grad,
        normed_one,
        grad_attn,
        *weights,
        *kept,
        *tables,
    )
    down_share, back_out = lax.optimization_barrier((down_share, back_out))
    layer_output = matmul(put_back, back_out.reshape(row_count, width_part)).astype(BF)
    input_grad = matmul(put_back, back_grad.reshape(row_count, width_part)).astype(BF)
    o = output_weight.shape[0]
    a = o + query_weight.shape[1]
    b = a + key_matrix.shape[1]
    summed = (
        gains[0],
        first[:, o:a],
        first[:, a:b],
        first[:, b:],
        first[:, :o].T,
        both_share[:, :hidden],
        both_share[:, hidden:],
        down_share.T,
        gains[8],
    )
    return (
        layer_output,
        input_grad,
        summed[0],
        summed[1],
        summed[2],
        summed[3],
        summed[4],
        summed[8],
        summed[5],
        summed[6],
        summed[7],
    )


def solution(mesh):
    placed = (
        P(None, ("dp", "tensor")),
        P(None, ("dp", "tensor")),
        P(),
        P(None, "tensor"),
        P(None, "tensor"),
        P(None, "tensor"),
        P("tensor", None),
        P(),
        P(None, "tensor"),
        P(None, "tensor"),
        P("tensor", None),
        P(),
        P(),
        P(),
    )
    return jax.shard_map(
        per_device,
        mesh=mesh,
        in_specs=placed,
        out_specs=(
            P(None, ("dp", "tensor")),
            P(None, ("dp", "tensor")),
            P("dp"),
            P("dp", "tensor"),
            P("dp", "tensor"),
            P("dp", "tensor"),
            P("tensor", "dp"),
            P("dp"),
            P("dp", "tensor"),
            P("dp", "tensor"),
            P("tensor", "dp"),
        ),
        check_vma=False,
    )
```

```python
import functools
import math

import jax
import jax.numpy as jnp
from jax import lax
from jax.experimental import pallas as pl
from jax.experimental.pallas import tpu as pltpu
from jax.sharding import PartitionSpec as P

HEAD_WIDTH = 128

MESH = pl.DeviceIdType.MESH
VM = pl.BlockSpec(memory_space=pltpu.VMEM)
F32 = jnp.float32
BF = jnp.bfloat16

def neighbour_barrier(z, n, axis):
    barrier = pltpu.get_barrier_semaphore()
    @pl.when(z > 0)
    def _():
        pl.semaphore_signal(barrier, inc=1, device_id={axis: z - 1}, device_id_type=MESH)
    @pl.when(z < n - 1)
    def _():
        pl.semaphore_signal(barrier, inc=1, device_id={axis: z + 1}, device_id_type=MESH)
    ends = jnp.where(z > 0, 1, 0) + jnp.where(z < n - 1, 1, 0)
    pl.semaphore_wait(barrier, ends)

def rcopy(src, dst, ss, rs, dev):
    return pltpu.make_async_remote_copy(src_ref=src, dst_ref=dst, send_sem=ss, recv_sem=rs, device_id={"tensor": dev}, device_id_type=MESH)


eps = 1e-05
rope_base = 10000.0


def nt(left, right):
    return lax.dot_general(left, right, (((1,), (1,)), ((), ())), preferred_element_type=F32)


def tn(left, right):
    return lax.dot_general(left, right, (((0,), (0,)), ((), ())), preferred_element_type=F32)


def mm(left, right):
    return jnp.dot(left, right, preferred_element_type=F32)


def spin(values, cosine, signed_sine):
    return values * cosine + pltpu.roll(values, HEAD_WIDTH // 2, 1) * signed_sine


def visible(code_row, code_col, low_col):
    return jnp.where((code_row <= code_col) & (code_row >= low_col), 0.0, -1e30)


def attend_tile(t, tiles, xt, gain, wq, wk, wv, wo, cosine, sine, code_row, code_col, low_col,
                part, normed, q, k, v, o, lse, scales):
    rows = normed.shape[0]
    tile = rows // tiles
    heads = wq.shape[1] // HEAD_WIDTH
    kv = wk.shape[1] // HEAD_WIDTH
    group = heads // kv
    factor = math.log2(math.e) / math.sqrt(HEAD_WIDTH)
    r = pl.ds(t * tile, tile)
    xt = xt.astype(F32)
    scale = lax.rsqrt(jnp.mean(xt * xt, axis=1, keepdims=True) + eps)
    scales[r, :] = scale
    n1 = (xt * scale * gain[...]).astype(BF)
    normed[r, :] = n1
    c, s = cosine[r, :], sine[r, :]
    pre = mm(n1, wq[...])
    for h in range(heads):
        cut = slice(h * HEAD_WIDTH, (h + 1) * HEAD_WIDTH)
        q[r, cut] = spin(pre[:, cut], c, s).astype(BF)
    pre = mm(n1, wk[...])
    for h in range(kv):
        cut = slice(h * HEAD_WIDTH, (h + 1) * HEAD_WIDTH)
        k[r, cut] = spin(pre[:, cut], c, s).astype(BF)
    v[r, :] = mm(n1, wv[...]).astype(BF)
    seen = (t + 1) * tile
    block = min(tile, 256)
    for at in range(t * tile, (t + 1) * tile, block):
        r = pl.ds(at, block)
        bias = visible(code_row[:, :seen], code_col[r, :], low_col[r, :])
        logs = []
        for h in range(heads):
            cut = slice(h * HEAD_WIDTH, (h + 1) * HEAD_WIDTH)
            mine = slice(h // group * HEAD_WIDTH, (h // group + 1) * HEAD_WIDTH)
            scores = nt(q[r, cut], k[:seen, mine]) * factor + bias
            top = jnp.max(scores, axis=1, keepdims=True)
            expo = jnp.exp2(scores - top)
            total = jnp.sum(expo, axis=1, keepdims=True)
            probs = (expo * (1.0 / total)).astype(BF)
            o[r, cut] = mm(probs, v[:seen, mine]).astype(BF)
            logs.append(top + jnp.log2(total))
        lse[r, :] = jnp.concatenate(logs, axis=1)
        part[r, :] = mm(o[r, :], wo[...]).astype(BF)


def attend_back_tile(t, tiles, ga, wq, wk, wv, wo, q, k, v, o, lse, cosine, sine, code_row, code_col, low_col,
                     part, dqkv, dk, dv):
    rows = ga.shape[0]
    tile = rows // tiles
    heads = wq.shape[1] // HEAD_WIDTH
    kv = wk.shape[1] // HEAD_WIDTH
    group = heads // kv
    wide = heads * HEAD_WIDTH
    narrow = kv * HEAD_WIDTH
    score_scale = 1.0 / math.sqrt(HEAD_WIDTH)
    factor = math.log2(math.e) / math.sqrt(HEAD_WIDTH)
    seen = (t + 1) * tile
    block = min(tile, 256)
    for at in range(t * tile, (t + 1) * tile, block):
        r = pl.ds(at, block)
        do = nt(ga[r, :], wo[...]).astype(BF)
        c, s = cosine[r, :], sine[r, :]
        bias = visible(code_row[:, :seen], code_col[r, :], low_col[r, :])
        logs = lse[r, :]
        for h in range(heads):
            cut = slice(h * HEAD_WIDTH, (h + 1) * HEAD_WIDTH)
            mine = slice(h // group * HEAD_WIDTH, (h // group + 1) * HEAD_WIDTH)
            do_h = do[:, cut]
            qh = q[r, cut]
            probs = jnp.exp2(nt(qh, k[:seen, mine]) * factor + bias - logs[:, h : h + 1])
            along = jnp.sum(do_h.astype(F32) * o[r, cut].astype(F32), axis=1, keepdims=True)
            ds = (probs * (nt(do_h, v[:seen, mine]) - along)).astype(BF)
            pb = probs.astype(BF)
            dq = mm(ds, k[:seen, mine]) * score_scale
            dqkv[r, cut] = spin(dq, c, -s).astype(BF)
            more_k = tn(ds, qh)
            more_v = tn(pb, do_h)
            if t == tiles - 1 and at == t * tile and h % group == 0:
                dk[:seen, mine] = more_k
                dv[:seen, mine] = more_v
            else:
                dk[:seen, mine] += more_k
                dv[:seen, mine] += more_v
    for at in range(t * tile, (t + 1) * tile, block):
        r = pl.ds(at, block)
        c, s = cosine[r, :], sine[r, :]
        for h in range(kv):
            cut = slice(h * HEAD_WIDTH, (h + 1) * HEAD_WIDTH)
            low = wide + h * HEAD_WIDTH
            dqkv[r, low : low + HEAD_WIDTH] = spin(dk[r, cut] * score_scale, c, -s).astype(BF)
        dqkv[r, wide + narrow :] = dv[r, :].astype(BF)
        part[r, :] = (
            nt(dqkv[r, :wide], wq[...])
            + nt(dqkv[r, wide : wide + narrow], wk[...])
            + nt(dqkv[r, wide + narrow :], wv[...])
        ).astype(BF)


ANY = pl.BlockSpec(memory_space=pl.ANY)
LAG = 2
CHUNK = 32
BLOCK = 128


def line_row(f, c):
    per = BLOCK // CHUNK
    return pl.ds(pl.multiple_of(lax.div(c, per) * (2 * BLOCK) + f * BLOCK + lax.rem(c, per) * CHUNK, CHUNK), CHUNK)


def line_steps(n, rows):
    return rows // 2 // CHUNK + 2 * LAG * (n - 1)


def line_sum_step(n, z, t, part, up, out, sems):
    us, ur, ds, dr = sems
    count = part.shape[0] // 2 // CHUNK
    for f in range(2):
        p = z if f == 0 else n - 1 - z
        step = 1 if f == 0 else -1
        c = t - LAG * p

        @pl.when((c >= 0) & (c < count))
        def _():
            r = line_row(f, c)

            @pl.when(p == 0)
            def _():
                rcopy(part.at[r], up.at[r], us.at[f, c], ur.at[f, c], z + step).start()

            @pl.when(p > 0)
            def _():
                rcopy(up.at[r], up.at[r], us.at[f, c], ur.at[f, c], z).wait_recv()
                s = (part[r, :].astype(F32) + up[r, :].astype(F32)).astype(BF)

                @pl.when(p < n - 1)
                def _():
                    up[r, :] = s
                    rcopy(up.at[r], up.at[r], us.at[f, c], ur.at[f, c], z + step).start()

                @pl.when(p == n - 1)
                def _():
                    out[r, :] = s
                    rcopy(out.at[r], out.at[r], ds.at[f, c], dr.at[f, c], z - step).start()

    for f in range(2):
        p = z if f == 0 else n - 1 - z
        step = 1 if f == 0 else -1
        c = t - LAG * (2 * (n - 1) - p)

        @pl.when((c >= 0) & (c < count) & (p < n - 1))
        def _():
            r = line_row(f, c)
            rcopy(out.at[r], out.at[r], ds.at[f, c], dr.at[f, c], z).wait_recv()

            @pl.when(p > 0)
            def _():
                rcopy(out.at[r], out.at[r], ds.at[f, c], dr.at[f, c], z - step).start()


def line_sum_drain(n, z, part, up, out, sems):
    us, ur, ds, dr = sems
    count = part.shape[0] // 2 // CHUNK

    def drain(c, _):
        for f in range(2):
            p = z if f == 0 else n - 1 - z
            r = line_row(f, c)

            @pl.when(p < n - 1)
            def _():
                rcopy(up.at[r], up.at[r], us.at[f, c], ur.at[f, c], z).wait_send()

            @pl.when(p > 0)
            def _():
                rcopy(out.at[r], out.at[r], ds.at[f, c], dr.at[f, c], z).wait_send()

        return 0

    lax.fori_loop(0, count, drain, 0)


def line_sum_sems(rows):
    return [pltpu.SemaphoreType.DMA((2, rows // 2 // CHUNK))] * 4


def gather_cut(ref, o, c, w):
    return ref.at[pl.ds(pl.multiple_of(c * BLOCK, BLOCK), BLOCK), pl.ds(pl.multiple_of(o * w, w), w)]


def line_gather_step(n, z, t, src, out, ss, rs):
    rows, w = src.shape
    count = rows // BLOCK

    @pl.when(t < count)
    def _():
        mine = src.at[pl.ds(pl.multiple_of(t * BLOCK, BLOCK), BLOCK)]

        @pl.when(z < n - 1)
        def _():
            rcopy(mine, gather_cut(out, z, t, w), ss.at[0, z, t], rs.at[0, z, t], z + 1).start()

        @pl.when(z > 0)
        def _():
            rcopy(mine, gather_cut(out, z, t, w), ss.at[1, z, t], rs.at[1, z, t], z - 1).start()

    for hop in range(1, n):
        c = t - hop
        for d, step in ((0, 1), (1, -1)):
            o = z - hop * step

            @pl.when((c >= 0) & (c < count) & (o >= 0) & (o < n))
            def _():
                cut = gather_cut(out, o, c, w)
                rcopy(cut, cut, ss.at[d, o, c], rs.at[d, o, c], z).wait_recv()
                after = z + step

                @pl.when((after >= 0) & (after < n))
                def _():
                    rcopy(cut, cut, ss.at[d, o, c], rs.at[d, o, c], after).start()


def line_gather_drain(n, z, src, out, ss, rs):
    rows, w = src.shape

    def drain(c, _):
        for d in range(2):
            for o in range(n):
                on = (o <= z) & (z < n - 1) if d == 0 else (o >= z) & (z > 0)

                @pl.when(on)
                def _():
                    cut = gather_cut(out, o, c, w)
                    rcopy(cut, cut, ss.at[d, o, c], rs.at[d, o, c], z).wait_send()

        return 0

    lax.fori_loop(0, rows // BLOCK, drain, 0)


def middle_kernel(n, part, x, g_part, keep, gain, wg_far, wu_far, wd_far,
                  result, a_far, g_far, n2_far, inner_far, both_far, dn2_far,
                  wg, wu, wd, up, total, g, right, left, gate_s, upper_s, n2_s, inner_s, both_s, f_s, dn2_s,
                  us, ur, ds, dr, ss, rs, fs, fr, load, own, save, late):
    z = lax.axis_index("tensor")
    rows, width = part.shape
    w = g_part.shape[1]
    hidden = wg.shape[1]
    tile = 2 * BLOCK
    sums = (us, ur, ds, dr)
    loads = [pltpu.make_async_copy(a, b, load.at[i]) for i, (a, b) in enumerate(((wg_far, wg), (wu_far, wu), (wd_far, wd)))]
    for copy in loads:
        copy.start()
    mine = pltpu.make_async_copy(g_part, g.at[:, pl.ds(pl.multiple_of(z * w, w), w)], own)
    mine.start()
    neighbour_barrier(z, n, "tensor")

    def saves(d):
        r = pl.ds(pl.multiple_of(d * tile, tile), tile)
        pairs = ((n2_s, n2_far), (inner_s, inner_far), (both_s, both_far), (dn2_s, dn2_far))
        return [pltpu.make_async_copy(a, b.at[r], save.at[i]) for i, (a, b) in enumerate(pairs)]

    first = BLOCK // CHUNK - 1 + 2 * LAG * (n - 1)

    def body(t, _):
        line_sum_step(n, z, t, part, up, total, sums)

        @pl.when(lax.rem(t, 2) == 0)
        def _():
            line_gather_step(n, z, lax.div(t, 2), g_part, g, ss, rs)

        q = t - first
        d = lax.div(jnp.maximum(q, 0), 4)
        k = lax.rem(jnp.maximum(q, 0), 4)
        r = pl.ds(pl.multiple_of(d * tile, tile), tile)

        @pl.when((q >= 0) & (d < rows // tile) & (k == 0))
        def _():
            @pl.when(d == 0)
            def _():
                for copy in loads:
                    copy.wait()
                mine.wait()

            @pl.when(d > 0)
            def _():
                for copy in saves(d - 1):
                    copy.wait()

            h = x[r, :].astype(F32) + keep[r, :] * total[r, :].astype(F32)
            scale = lax.rsqrt(jnp.mean(h * h, axis=1, keepdims=True) + eps)
            n2_s[...] = (h * scale * gain[...]).astype(BF)
            gate_s[...] = mm(n2_s[...], wg[...])

        @pl.when((q >= 0) & (d < rows // tile) & (k == 1))
        def _():
            upper_s[...] = mm(n2_s[...], wu[...])
            gate = gate_s[...]
            inner_s[...] = (gate * jax.nn.sigmoid(gate) * upper_s[...]).astype(BF)

        @pl.when((q >= 0) & (d < rows // tile) & (k == 2))
        def _():
            f_s[lax.rem(d, 2)] = mm(inner_s[...], wd[...]).astype(BF)
            gf = (keep[r, :] * g[r, :].astype(F32)).astype(BF)
            back = nt(gf, wd[...])
            gate = gate_s[...]
            s = jax.nn.sigmoid(gate)
            both_s[:, :hidden] = (back * upper_s[...] * s * (1.0 + gate * (1.0 - s))).astype(BF)
            both_s[:, hidden:] = (back * (gate * s)).astype(BF)

        @pl.when((q >= 0) & (d < rows // tile) & (k == 3))
        def _():
            dn2_s[...] = (nt(both_s[:, :hidden], wg[...]) + nt(both_s[:, hidden:], wu[...])).astype(BF)
            for copy in saves(d):
                copy.start()

        scatter_step(t - first - 2)
        return 0

    chunk = tile // 4
    count = rows // chunk

    def at(ref, c, b):
        return ref.at[pl.ds(pl.multiple_of(c * chunk, chunk), chunk), pl.ds(b * w, w)]

    def scatter_copy(buf, d, c, b, to):
        return rcopy(at(buf, c, b), at(buf, c, b), fs.at[d, b, c], fr.at[d, b, c], to)

    def scatter_step(s):
        for d, buf, step in ((0, right, 1), (1, left, -1)):
            p = z if d == 0 else n - 1 - z
            c = s - p

            @pl.when((c >= 0) & (c < count))
            def _():
                r = pl.ds(pl.multiple_of(c * chunk, chunk), chunk)
                slot = lax.rem(lax.div(c, 4), 2)
                inner = pl.ds(pl.multiple_of(lax.rem(c, 4) * chunk, chunk), chunk)
                for b in range(n - 1, 0, -1) if d == 0 else range(n - 1):
                    k = pl.ds(b * w, w)

                    @pl.when((b > z) if d == 0 else (b < z))
                    def _():
                        @pl.when(p == 0)
                        def _():
                            buf[r, k] = f_s[slot, inner, k]

                        @pl.when(p > 0)
                        def _():
                            scatter_copy(buf, d, c, b, z).wait_recv()
                            buf[r, k] = (f_s[slot, inner, k].astype(F32) + buf[r, k].astype(F32)).astype(BF)

                        scatter_copy(buf, d, c, b, z + step).start()

        c = s - (n - 1)

        @pl.when((c >= 0) & (c < count))
        def _():
            r = pl.ds(pl.multiple_of(c * chunk, chunk), chunk)
            slot = lax.rem(lax.div(c, 4), 2)
            inner = pl.ds(pl.multiple_of(lax.rem(c, 4) * chunk, chunk), chunk)
            for b in range(n):
                k = pl.ds(b * w, w)

                @pl.when(z == b)
                def _():
                    f = f_s[slot, inner, k].astype(F32)
                    if b > 0:
                        scatter_copy(right, 0, c, b, z).wait_recv()
                        f = f + right[r, k].astype(F32)
                    if b < n - 1:
                        scatter_copy(left, 1, c, b, z).wait_recv()
                        f = f + left[r, k].astype(F32)
                    kept = keep[r, :]
                    h = x[r, k].astype(F32) + kept * total[r, k].astype(F32)
                    result[r, :] = (h + kept * f).astype(BF)

    lax.fori_loop(0, first + 2 + count + n, body, 0)

    def drain(c, _):
        for d, buf in ((0, right), (1, left)):
            for b in range(n):

                @pl.when((b > z) if d == 0 else (b < z))
                def _():
                    scatter_copy(buf, d, c, b, z).wait_send()

        return 0

    lax.fori_loop(0, count, drain, 0)
    ends = [pltpu.make_async_copy(a, b, late.at[i]) for i, (a, b) in enumerate(((total, a_far), (g, g_far)))]
    for copy in ends:
        copy.start()
    line_sum_drain(n, z, part, up, total, sums)
    line_gather_drain(n, z, g_part, g, ss, rs)
    for copy in saves(rows // tile - 1) + ends:
        copy.wait()


def middle(n, part, x, g_part, keep, gain, wg, wu, wd):
    rows, width = part.shape
    hidden = wg.shape[1]
    tile = 2 * BLOCK
    blocks = rows // BLOCK
    w = g_part.shape[1]
    widths = (w, width, width, width, hidden, 2 * hidden, width)
    return pl.pallas_call(
        functools.partial(middle_kernel, n),
        out_shape=[jax.ShapeDtypeStruct((rows, k), BF) for k in widths],
        in_specs=[VM] * 5 + [ANY] * 3,
        out_specs=[VM] + [ANY] * 6,
        scratch_shapes=[
            pltpu.VMEM(wg.shape, BF),
            pltpu.VMEM(wu.shape, BF),
            pltpu.VMEM(wd.shape, BF),
            pltpu.VMEM((rows, width), BF),
            pltpu.VMEM((rows, width), BF),
            pltpu.VMEM((rows, width), BF),
            pltpu.VMEM((rows, width), BF),
            pltpu.VMEM((rows, width), BF),
            pltpu.VMEM((tile, hidden), F32),
            pltpu.VMEM((tile, hidden), F32),
            pltpu.VMEM((tile, width), BF),
            pltpu.VMEM((tile, hidden), BF),
            pltpu.VMEM((tile, 2 * hidden), BF),
            pltpu.VMEM((2, tile, width), BF),
            pltpu.VMEM((tile, width), BF),
            *line_sum_sems(rows),
            pltpu.SemaphoreType.DMA((2, n, blocks)),
            pltpu.SemaphoreType.DMA((2, n, blocks)),
            pltpu.SemaphoreType.DMA((2, n, rows // tile * 4)),
            pltpu.SemaphoreType.DMA((2, n, rows // tile * 4)),
            pltpu.SemaphoreType.DMA((3,)),
            pltpu.SemaphoreType.DMA,
            pltpu.SemaphoreType.DMA((4,)),
            pltpu.SemaphoreType.DMA((2,)),
        ],
        compiler_params=pltpu.CompilerParams(collective_id=3, has_side_effects=True, vmem_limit_bytes=63 << 20),
    )(part, x, g_part, keep, gain, wg, wu, wd)


def second_back_kernel(n, part, x, a, g, keep, gain, inner_far, ga, dh, gain_grad, grad_far,
                       up, total, inner, stage, us, ur, ds, dr, load, save):
    z = lax.axis_index("tensor")
    rows, width = part.shape
    w = dh.shape[1]
    piece = BLOCK // 2
    sums = (us, ur, ds, dr)
    loads = [pltpu.make_async_copy(inner_far, inner, load.at[0])]
    for copy in loads:
        copy.start()
    neighbour_barrier(z, n, "tensor")
    span = stage.shape[1]
    spans = width // span

    def saved(j):
        slot = lax.rem(j, 2)
        return pltpu.make_async_copy(stage.at[slot], grad_far.at[pl.ds(pl.multiple_of(j * span, span), span)], save.at[slot])

    gain_grad[...] = jnp.zeros_like(gain_grad)
    first = BLOCK // CHUNK - 1 + 2 * LAG * (n - 1)

    def body(t, _):
        line_sum_step(n, z, t, part, up, total, sums)
        j = t - 3

        @pl.when((j >= 0) & (j < spans))
        def _():
            @pl.when(j == 0)
            def _():
                for copy in loads:
                    copy.wait()

            @pl.when(j >= 2)
            def _():
                saved(j - 2).wait()

            cut = pl.ds(pl.multiple_of(j * span, span), span)
            gf = (keep[...] * g[:, cut].astype(F32)).astype(BF)
            stage[lax.rem(j, 2)] = tn(gf, inner[...]).astype(BF)
            saved(j).start()

        q = t - first

        @pl.when(q >= 0)
        def _():
            r = pl.ds(pl.multiple_of(q * piece, piece), piece)
            h = x[r, :].astype(F32) + keep[r, :] * a[r, :].astype(F32)
            scale = lax.rsqrt(jnp.mean(h * h, axis=1, keepdims=True) + eps)
            back = total[r, :].astype(F32)
            gain_grad[...] += jnp.sum(back * h * scale, axis=0, keepdims=True)
            e = back * gain[...]
            along = jnp.mean(e * h, axis=1, keepdims=True)
            full = g[r, :].astype(F32) + scale * e - h * (scale * scale * scale * along)
            ga[r, :] = (keep[r, :] * full).astype(BF)
            for b in range(n):

                @pl.when(z == b)
                def _():
                    dh[r, :] = full[:, b * w : (b + 1) * w]

        return 0

    lax.fori_loop(0, first + rows // piece, body, 0)
    line_sum_drain(n, z, part, up, total, sums)
    for j in range(spans - 2, spans):
        saved(j).wait()


def second_back_of(n, part, x, a, g, keep, gain, inner):
    rows, width = part.shape
    return pl.pallas_call(
        functools.partial(second_back_kernel, n),
        out_shape=[
            jax.ShapeDtypeStruct((rows, width), BF),
            jax.ShapeDtypeStruct((rows, width // n), F32),
            jax.ShapeDtypeStruct((1, width), F32),
            jax.ShapeDtypeStruct((width, inner.shape[1]), BF),
        ],
        in_specs=[VM] * 6 + [ANY],
        out_specs=[VM] * 3 + [ANY],
        scratch_shapes=[
            pltpu.VMEM((rows, width), BF),
            pltpu.VMEM((rows, width), BF),
            pltpu.VMEM(inner.shape, BF),
            pltpu.VMEM((2, 256, inner.shape[1]), BF),
            *line_sum_sems(rows),
            pltpu.SemaphoreType.DMA((2,)),
            pltpu.SemaphoreType.DMA((2,)),
        ],
        compiler_params=pltpu.CompilerParams(collective_id=4, has_side_effects=True, vmem_limit_bytes=60 << 20),
    )(part, x, a, g, keep, gain, inner)


def peers_barrier(z, n, me, groups, everyone):
    barrier = pltpu.get_barrier_semaphore()

    def greet(off, _):
        peer = lax.rem(me + off, groups)
        pl.semaphore_signal(barrier, inc=1, device_id={"dp": peer}, device_id_type=MESH)
        return 0

    lax.fori_loop(1, groups, greet, 0)
    if everyone:
        for off in range(1, n):
            other = lax.rem(z + off, n)
            pl.semaphore_signal(barrier, inc=1, device_id={"tensor": other}, device_id_type=MESH)
        pl.semaphore_wait(barrier, groups - 1 + n - 1)
    else:

        @pl.when(z > 0)
        def _():
            pl.semaphore_signal(barrier, inc=1, device_id={"tensor": z - 1}, device_id_type=MESH)

        @pl.when(z < n - 1)
        def _():
            pl.semaphore_signal(barrier, inc=1, device_id={"tensor": z + 1}, device_id_type=MESH)

        ends = jnp.where(z > 0, 1, 0) + jnp.where(z < n - 1, 1, 0)
        pl.semaphore_wait(barrier, groups - 1 + ends)


def pcopy(src, dst, ss, rs, peer):
    return pltpu.make_async_remote_copy(
        src_ref=src, dst_ref=dst, send_sem=ss, recv_sem=rs, device_id={"dp": peer}, device_id_type=MESH
    )


def deal_in_kernel(n, groups, dealt_x, dealt_g, gain, cosine, sine, code_row, code_col, low_col, *refs):
    far, (full, g_part, x_part), results = refs[:4], refs[4:7], refs[7:15]
    near, (xs, xr, gs, gr, ss, rs, own, load) = refs[15:19], refs[19:]
    loads = [pltpu.make_async_copy(a, b, load.at[i]) for i, (a, b) in enumerate(zip(far, near))]
    for copy in loads:
        copy.start()
    z = lax.axis_index("tensor")
    me = lax.axis_index("dp")
    tiles, sub, w = dealt_x.shape[1:]
    cols = pl.ds(pl.multiple_of(z * w, w), w)

    def place(t, i):
        return full.at[t, i, :, cols]

    for t in range(tiles):
        pltpu.make_async_copy(dealt_x.at[me, t], place(t, me), own.at[t]).start()
    pltpu.make_async_copy(dealt_g.at[me], g_part.at[:, me], own.at[tiles]).start()
    peers_barrier(z, n, me, groups, False)

    def send(t):
        def one(off, _):
            peer = lax.rem(me + off, groups)
            pcopy(dealt_x.at[peer, t], place(t, me), xs.at[t, peer], xr.at[t, me], peer).start()
            return 0

        lax.fori_loop(1, groups, one, 0)

    def cut(o, t):
        return full.at[t, :, :, pl.ds(pl.multiple_of(o * w, w), w)]

    for t in range(tiles):
        send(t)

    def send_g(off, _):
        peer = lax.rem(me + off, groups)
        pcopy(dealt_g.at[peer], g_part.at[:, me], gs.at[peer], gr.at[me], peer).start()
        return 0

    lax.fori_loop(1, groups, send_g, 0)
    for s in range(tiles + n - 1):
        if s < tiles:

            def got(off, _):
                peer = lax.rem(me + off, groups)
                pcopy(dealt_x.at[peer, s], place(s, peer), xs.at[s, peer], xr.at[s, peer], peer).wait_recv()
                return 0

            lax.fori_loop(1, groups, got, 0)
            pltpu.make_async_copy(dealt_x.at[me, s], place(s, me), own.at[s]).wait()

            @pl.when(z < n - 1)
            def _():
                rcopy(cut(z, s), cut(z, s), ss.at[0, z, s], rs.at[0, z, s], z + 1).start()

            @pl.when(z > 0)
            def _():
                rcopy(cut(z, s), cut(z, s), ss.at[1, z, s], rs.at[1, z, s], z - 1).start()

        for hop in range(1, n):
            c = s - hop
            if 0 <= c < tiles:
                for d, step in ((0, 1), (1, -1)):
                    o = z - hop * step

                    @pl.when((o >= 0) & (o < n))
                    def _():
                        rcopy(cut(o, c), cut(o, c), ss.at[d, o, c], rs.at[d, o, c], z).wait_recv()
                        after = z + step

                        @pl.when((after >= 0) & (after < n))
                        def _():
                            rcopy(cut(o, c), cut(o, c), ss.at[d, o, c], rs.at[d, o, c], after).start()

        if s == tiles - 1:
            pltpu.make_async_copy(full.at[:, :, :, cols], x_part, own.at[tiles + 1]).start()
        t = s - (n - 1)
        if t >= 0:
            if t == 0:
                for copy in loads:
                    copy.wait()
            attend_tile(
                t,
                tiles,
                full[t].reshape(groups * sub, n * w),
                gain,
                *near,
                cosine,
                sine,
                code_row,
                code_col,
                low_col,
                *results,
            )

    def finish(off, _):
        peer = lax.rem(me + off, groups)
        copy = pcopy(dealt_g.at[peer], g_part.at[:, peer], gs.at[peer], gr.at[peer], peer)
        copy.wait_recv()
        copy.wait_send()
        for t in range(tiles):
            pcopy(dealt_x.at[peer, t], place(t, peer), xs.at[t, peer], xr.at[t, peer], peer).wait_send()
        return 0

    lax.fori_loop(1, groups, finish, 0)
    pltpu.make_async_copy(dealt_g.at[me], g_part.at[:, me], own.at[tiles]).wait()
    pltpu.make_async_copy(full.at[:, :, :, cols], x_part, own.at[tiles + 1]).wait()
    for c in range(tiles):
        for d in range(2):
            for o in range(n):

                @pl.when((o <= z) & (z < n - 1) if d == 0 else (o >= z) & (z > 0))
                def _():
                    rcopy(cut(o, c), cut(o, c), ss.at[d, o, c], rs.at[d, o, c], z).wait_send()


def deal_in(n, groups, dealt_x, dealt_g, gain, weights, tables):
    tiles, sub, w = dealt_x.shape[1:]
    rows = tiles * groups * sub
    wq, wk, wv, wo = weights
    dma = pltpu.SemaphoreType.DMA
    widths = (n * w, n * w, wq.shape[1], wk.shape[1], wv.shape[1], wq.shape[1])
    return pl.pallas_call(
        functools.partial(deal_in_kernel, n, groups),
        out_shape=[
            jax.ShapeDtypeStruct((tiles, groups, sub, n * w), BF),
            jax.ShapeDtypeStruct((tiles, groups, sub, w), BF),
            jax.ShapeDtypeStruct((tiles, groups, sub, w), BF),
            *(jax.ShapeDtypeStruct((rows, k), BF) for k in widths),
            jax.ShapeDtypeStruct((rows, wq.shape[1] // HEAD_WIDTH), F32),
            jax.ShapeDtypeStruct((rows, 1), F32),
        ],
        in_specs=[VM] * 8 + [ANY] * 4,
        out_specs=[VM] * 11,
        scratch_shapes=[
            *(pltpu.VMEM(a.shape, BF) for a in weights),
            dma((tiles, groups)),
            dma((tiles, groups)),
            dma((groups,)),
            dma((groups,)),
            dma((2, n, tiles)),
            dma((2, n, tiles)),
            dma((tiles + 2,)),
            dma((4,)),
        ],
        compiler_params=pltpu.CompilerParams(collective_id=6, has_side_effects=True, vmem_limit_bytes=60 << 20),
    )(dealt_x, dealt_g, gain, *tables, *weights)


def exact(left, right, contract):
    return lax.dot_general(
        left, right, (contract, ((), ())), preferred_element_type=F32, precision=lax.Precision.HIGHEST
    )


def deal_out_kernel(n, groups, tiles, chunk, lag, x, dh, scale1, gain1, result, gain2, normed, *refs):
    attention = refs[:15]
    (back_out, back_dx, gains, o_share, q_share, k_share, v_share, part, dqkv, dk, dv, right, left, fb, dx, lines, widths, gsrc, gdst, wsrc, wdst, pair,
     ss, rs, os, orr, xs, xr, ls, lr, ws, wr, es, er, qs, qr, ps, pr, own) = refs[15:]
    ga, o = attention[0], attention[8]
    z = lax.axis_index("tensor")
    me = lax.axis_index("dp")
    rows, w = x.shape
    tile = rows // tiles
    count = rows // chunk
    per = tile // chunk
    sub = result.shape[2]
    pltpu.make_async_copy(result.at[:, me], back_out.at[me], own.at[0]).start()
    peers_barrier(z, n, me, groups, True)

    def send_out(off, _):
        peer = lax.rem(me + off, groups)
        pcopy(result.at[:, peer], back_out.at[me], os.at[peer], orr.at[me], peer).start()
        return 0

    lax.fori_loop(1, groups, send_out, 0)

    def chunk_rows(c):
        t = tiles - 1 - lax.div(c, per)
        return pl.ds(pl.multiple_of(t * tile + lax.rem(c, per) * chunk, chunk), chunk)

    def at(ref, c, b):
        return ref.at[chunk_rows(c), pl.ds(b * w, w)]

    widths[...] = jnp.zeros_like(widths)

    def others(f):
        for off in range(1, n):
            f(lax.rem(z + off, n))

    def line_copy(t, slot, other):
        cut = lines.at[slot, :, pl.ds(pl.multiple_of(t * tile, tile), tile)]
        return rcopy(cut, cut, ls.at[other, t], lr.at[slot, t], other)

    def width_copy(slot, other):
        cut = widths.at[slot]
        return rcopy(cut, cut, ws.at[other], wr.at[slot], other)

    def open_tile(t):
        r = pl.ds(pl.multiple_of(t * tile, tile), tile)
        e = fb[r, :] * gain1[pl.ds(z, 1), :]
        xt = x[r, :].astype(F32)
        lines[z, :, r] = exact(jnp.ones((8, w), F32), e * xt, ((1,), (1,)))
        others(lambda other: line_copy(t, z, other).start())
        grown = jnp.sum(fb[r, :] * xt * scale1[r, :], axis=0, keepdims=True)
        widths[z, :, :] += jnp.broadcast_to(grown, (8, w))

        @pl.when(t == 0)
        def _():
            others(lambda other: width_copy(z, other).start())

    def close_tile(t):
        r = pl.ds(pl.multiple_of(t * tile, tile), tile)
        others(lambda other: line_copy(t, other, other).wait_recv())
        total = lines[0, :, r]
        for j in range(1, n):
            total = total + lines[j, :, r]
        along = exact(total * (1.0 / (8 * n * w)), jnp.ones((8, w), F32), ((0,), (0,)))
        e = fb[r, :] * gain1[pl.ds(z, 1), :]
        s = scale1[r, :]
        full = dh[r, :] + s * e - x[r, :].astype(F32) * (s * s * s * along)
        dx[t] = full.astype(BF).reshape(groups, sub, w)
        pltpu.make_async_copy(dx.at[t, me], back_dx.at[me, t], own.at[1 + t]).start()

        def one(off, _):
            peer = lax.rem(me + off, groups)
            pcopy(dx.at[t, peer], back_dx.at[me, t], xs.at[t, peer], xr.at[t, me], peer).start()
            return 0

        lax.fori_loop(1, groups, one, 0)

    ow = o.shape[1]
    share = normed.shape[1] // groups
    span = max(share, 256)

    half = groups // 2
    seat = lax.div(me, 2)
    parity = lax.rem(me, 2)
    partner = me + 1 - 2 * parity

    def rows_of(owner):
        return pl.ds(pl.multiple_of(owner * share, share), share)

    def weight_copy(kind, src, dst, sems, to, slot, at_column, wide):
        columns = pl.ds(at_column, wide)
        return pltpu.make_async_remote_copy(
            src_ref=wsrc.at[rows_of(src), columns],
            dst_ref=dst.at[slot, :, columns],
            send_sem=sems[0].at[kind, lax.div(src, 2)],
            recv_sem=sems[1].at[kind, slot],
            device_id={"dp": to},
            device_id_type=MESH,
        )

    def weigh(left_ref, right_ref, at_column, kind):
        wide = right_ref.shape[1]

        def one(j, _):
            base = pl.multiple_of(j * span, span)
            cut = pl.ds(base, span)
            wsrc[cut, at_column : at_column + wide] = tn(left_ref[:, cut], right_ref[...]).astype(BF)
            for i in range(span // share):
                owner = lax.div(base, share) + i

                @pl.when(lax.rem(owner, 2) != parity)
                def _():
                    weight_copy(kind, owner, pair, (ps, pr), partner, lax.div(owner, 2), at_column, wide).start()

            return 0

        lax.fori_loop(0, normed.shape[1] // span, one, 0)

    def join(at_column, wide, kind):
        columns = slice(at_column, at_column + wide)

        def one(off, _):
            m = lax.rem(seat + off, half)
            owner = 2 * m + parity
            weight_copy(kind, owner, pair, (ps, pr), partner, m, at_column, wide).wait_recv()
            r = rows_of(owner)
            total = (wsrc[r, columns].astype(F32) + pair[m, :, columns].astype(F32)).astype(BF)

            @pl.when(owner == me)
            def _():
                wdst[seat, :, columns] = total

            @pl.when(owner != me)
            def _():
                wsrc[r, columns] = total
                weight_copy(kind, owner, wdst, (qs, qr), owner, seat, at_column, wide).start()

            return 0

        lax.fori_loop(1, half + 1, one, 0)

    joined = ((0, ow), (ow, dqkv.shape[1]))

    def flows(s, _):
        for k in range(tiles):

            @pl.when(s == k * per)
            def _():
                attend_back_tile(tiles - 1 - k, tiles, *attention, part, dqkv, dk, dv)

        @pl.when(s == 2)
        def _():
            weigh(ga, o, 0, 0)

        @pl.when(s == 5)
        def _():
            join(*joined[0], 0)

        @pl.when(s == (tiles - 1) * per + 3)
        def _():
            join(*joined[1], 1)

        @pl.when(s == (tiles - 1) * per + 1)
        def _():
            weigh(normed, dqkv, ow, 1)

        for d, buf, step in ((0, right, 1), (1, left, -1)):
            p = z if d == 0 else n - 1 - z
            c = s - lag * p

            @pl.when((c >= 0) & (c < count))
            def _():
                r = chunk_rows(c)
                for b in range(n - 1, 0, -1) if d == 0 else range(n - 1):
                    k = pl.ds(b * w, w)

                    @pl.when((b > z) if d == 0 else (b < z))
                    def _():
                        @pl.when(p == 0)
                        def _():
                            rcopy(at(part, c, b), at(buf, c, b), ss.at[d, b, c], rs.at[d, b, c], z + step).start()

                        @pl.when(p > 0)
                        def _():
                            rcopy(at(buf, c, b), at(buf, c, b), ss.at[d, b, c], rs.at[d, b, c], z).wait_recv()
                            buf[r, k] = (part[r, k].astype(F32) + buf[r, k].astype(F32)).astype(BF)
                            rcopy(at(buf, c, b), at(buf, c, b), ss.at[d, b, c], rs.at[d, b, c], z + step).start()

        c = s - lag * (n - 1)

        @pl.when((c >= 0) & (c < count))
        def _():
            r = chunk_rows(c)
            for b in range(n):
                k = pl.ds(b * w, w)

                @pl.when(z == b)
                def _():
                    total = part[r, k].astype(F32)
                    if b > 0:
                        rcopy(at(right, c, b), at(right, c, b), ss.at[0, b, c], rs.at[0, b, c], z).wait_recv()
                        total = total + right[r, k].astype(F32)
                    if b < n - 1:
                        rcopy(at(left, c, b), at(left, c, b), ss.at[1, b, c], rs.at[1, b, c], z).wait_recv()
                        total = total + left[r, k].astype(F32)
                    fb[r, :] = total

        @pl.when((c >= 0) & (c < count) & (lax.rem(jnp.maximum(c, 0), per) == per - 1))
        def _():
            open_tile(tiles - 1 - lax.div(c, per))

        c = c - 2

        @pl.when((c >= 0) & (lax.rem(jnp.maximum(c, 0), per) == per - 1))
        def _():
            close_tile(tiles - 1 - lax.div(c, per))

        return 0

    lax.fori_loop(0, count + lag * (n - 1) + 2, flows, 0)

    others(lambda other: width_copy(other, other).wait_recv())
    cols = gsrc.shape[2]
    first_gain = jnp.concatenate([widths[j] for j in range(n)], axis=1)
    second_gain = jnp.broadcast_to(gain2[...], first_gain.shape)
    for i in range(groups):
        gsrc[i, :8, :] = first_gain[:, i * cols : (i + 1) * cols]
        gsrc[i, 8:, :] = second_gain[:, i * cols : (i + 1) * cols]
    pltpu.make_async_copy(gsrc.at[me], gdst.at[me], own.at[1 + tiles]).start()

    def send_gain(off, _):
        peer = lax.rem(me + off, groups)
        pcopy(gsrc.at[peer], gdst.at[me], es.at[peer], er.at[me], peer).start()
        return 0

    lax.fori_loop(1, groups, send_gain, 0)

    def got_gain(off, _):
        peer = lax.rem(me + off, groups)
        copy = pcopy(gsrc.at[peer], gdst.at[peer], es.at[peer], er.at[peer], peer)
        copy.wait_recv()
        copy.wait_send()
        return 0

    lax.fori_loop(1, groups, got_gain, 0)
    pltpu.make_async_copy(gsrc.at[me], gdst.at[me], own.at[1 + tiles]).wait()
    total = gdst[0]
    for i in range(1, groups):
        total = total + gdst[i]
    gains[...] = total

    def got_weight(off, _):
        m = lax.rem(seat + off, half)
        for kind, (at_column, wide) in enumerate(joined):
            copy = weight_copy(kind, 2 * m + parity, wdst, (qs, qr), me, m, at_column, wide)
            copy.wait_recv()
            copy.wait_send()
        return 0

    def sent_weight(m, _):
        for kind, (at_column, wide) in enumerate(joined):
            weight_copy(kind, 2 * m + 1 - parity, pair, (ps, pr), partner, m, at_column, wide).wait_send()
        return 0

    lax.fori_loop(1, half, got_weight, 0)
    lax.fori_loop(0, half, sent_weight, 0)
    at_column = 0
    for share_ref in (o_share, q_share, k_share, v_share):
        columns = slice(at_column, at_column + share_ref.shape[1])
        at_column += share_ref.shape[1]
        total = wdst[0, :, columns].astype(F32)
        for i in range(1, half):
            total = total + wdst[i, :, columns].astype(F32)
        share_ref[...] = total

    def finish(off, _):
        peer = lax.rem(me + off, groups)
        copy = pcopy(result.at[:, peer], back_out.at[peer], os.at[peer], orr.at[peer], peer)
        copy.wait_recv()
        copy.wait_send()
        for t in range(tiles):
            copy = pcopy(dx.at[t, peer], back_dx.at[peer, t], xs.at[t, peer], xr.at[t, peer], peer)
            copy.wait_recv()
            copy.wait_send()
        return 0

    lax.fori_loop(1, groups, finish, 0)
    pltpu.make_async_copy(result.at[:, me], back_out.at[me], own.at[0]).wait()
    for t in range(tiles):
        pltpu.make_async_copy(dx.at[t, me], back_dx.at[me, t], own.at[1 + t]).wait()
        others(lambda other: line_copy(t, z, other).wait_send())
    others(lambda other: width_copy(z, other).wait_send())

    def drain(c, _):
        for d, buf in ((0, right), (1, left)):
            for b in range(n):

                @pl.when((b > z) if d == 0 else (b < z))
                def _():
                    rcopy(at(buf, c, b), at(buf, c, b), ss.at[d, b, c], rs.at[d, b, c], z).wait_send()

        return 0

    lax.fori_loop(0, count, drain, 0)


def deal_out(n, groups, tiles, x, dh, scale1, gain1, result, gain2, normed, *attention, chunk=64, lag=2):
    rows, w = x.shape
    width = n * w
    sub = rows // tiles // groups
    count = rows // chunk
    cols = width // groups
    joined = sum(a.shape[1] for a in attention[1:4])
    narrow = attention[2].shape[1]
    both = attention[8].shape[1] + joined
    dma = pltpu.SemaphoreType.DMA
    dealt = (groups, tiles, sub, w)
    return pl.pallas_call(
        functools.partial(deal_out_kernel, n, groups, tiles, chunk, lag),
        out_shape=[
            jax.ShapeDtypeStruct(dealt, BF),
            jax.ShapeDtypeStruct(dealt, BF),
            jax.ShapeDtypeStruct((16, cols), F32),
            jax.ShapeDtypeStruct((cols, attention[8].shape[1]), F32),
            *(jax.ShapeDtypeStruct((cols, a.shape[1]), F32) for a in attention[1:4]),
        ],
        in_specs=[VM] * 22,
        out_specs=[VM] * 7,
        scratch_shapes=[
            pltpu.VMEM((rows, width), BF),
            pltpu.VMEM((rows, joined), BF),
            pltpu.VMEM((rows, narrow), F32),
            pltpu.VMEM((rows, narrow), F32),
            pltpu.VMEM((rows, width), BF),
            pltpu.VMEM((rows, width), BF),
            pltpu.VMEM((rows, w), F32),
            pltpu.VMEM((tiles, groups, sub, w), BF),
            pltpu.VMEM((n, 8, rows), F32),
            pltpu.VMEM((n, 8, w), F32),
            pltpu.VMEM((groups, 16, cols), F32),
            pltpu.VMEM((groups, 16, cols), F32),
            pltpu.VMEM((width, both), BF),
            pltpu.VMEM((groups // 2, cols, both), BF),
            pltpu.VMEM((groups // 2, cols, both), BF),
            dma((2, n, count)),
            dma((2, n, count)),
            dma((groups,)),
            dma((groups,)),
            dma((tiles, groups)),
            dma((tiles, groups)),
            dma((n, tiles)),
            dma((n, tiles)),
            dma((n,)),
            dma((n,)),
            dma((groups,)),
            dma((groups,)),
            dma((2, groups // 2)),
            dma((2, groups // 2)),
            dma((2, groups // 2)),
            dma((2, groups // 2)),
            dma((tiles + 2,)),
        ],
        compiler_params=pltpu.CompilerParams(collective_id=5, has_side_effects=True, vmem_limit_bytes=62 << 20),
    )(x, dh, scale1, gain1, result.reshape(tiles, groups, sub, w), gain2, normed, *attention)


def rotary_tables(token_positions, head_size):
    half = head_size // 2
    freqs = rope_base ** (-(jnp.arange(half).astype(jnp.float32) * 2.0) / head_size)
    angles = token_positions.astype(jnp.float32)[:, None] * freqs[None, :]
    angles = jnp.concatenate([angles, angles], axis=1)
    return (jnp.cos(angles), jnp.sin(angles))


def matmul(left, right):
    return jnp.dot(left, right, preferred_element_type=jnp.float32)


def per_device(
    tokens,
    cotangent,
    first_gain,
    query_weight,
    key_matrix,
    value_matrix,
    output_weight,
    second_gain,
    gate_weight,
    up_weight,
    down_weight,
    seq_lengths,
    owner_order,
    skip_mask,
):
    groups = lax.axis_size("dp")
    member = lax.axis_index("dp")
    width_part = tokens.shape[1]
    row_count = tokens.shape[0]
    per_owner = row_count // groups
    seq_count = seq_lengths.shape[0]
    seq_index = jnp.arange(seq_count, dtype=jnp.int32)
    before = (seq_index[None, :] < seq_index[:, None]).astype(jnp.int32)
    unit_lengths = seq_lengths // groups
    unit_starts = jnp.sum(before * unit_lengths[None, :], axis=1)
    placed = (owner_order[:, None] == seq_index[None, :]).astype(jnp.int32)
    order_lengths = jnp.sum(placed * unit_lengths[None, :], axis=1)
    order_starts = jnp.sum(placed * unit_starts[None, :], axis=1)
    order_keep = jnp.sum(placed * skip_mask[None, :], axis=1)
    order_before = jnp.sum(before * order_lengths[None, :], axis=1)
    places = jnp.arange(row_count, dtype=jnp.int32)
    covers = (
        (places[:, None] >= order_before[None, :])
        & (places[:, None] < (order_before + order_lengths)[None, :])
    ).astype(jnp.int32)
    send_rows = places + jnp.sum(covers * (order_starts - order_before)[None, :], axis=1)
    given_before = jnp.sum(placed * order_before[:, None], axis=0)
    given_covers = (
        (places[:, None] >= unit_starts[None, :])
        & (places[:, None] < (unit_starts + unit_lengths)[None, :])
    ).astype(jnp.int32)
    slot_of = places + jnp.sum(given_covers * (given_before - unit_starts)[None, :], axis=1)
    my_places = member * per_owner + jnp.arange(per_owner, dtype=jnp.int32)
    my_covers = (
        (my_places[:, None] >= order_before[None, :])
        & (my_places[:, None] < (order_before + order_lengths)[None, :])
    ).astype(jnp.int32)
    slot_seq = jnp.sum(my_covers * seq_index[None, :], axis=1)
    slot_step = my_places - jnp.sum(my_covers * order_before[None, :], axis=1)
    slot_keep = jnp.sum(my_covers * order_keep[None, :], axis=1)
    tiles = max(1, per_owner // 32)
    sources = jnp.arange(groups, dtype=jnp.int32)[None, :, None]

    def spread(values):
        values = values.reshape(tiles, 1, per_owner // tiles)
        return jnp.broadcast_to(values, (tiles, groups, per_owner // tiles)).reshape(row_count)

    token_positions = (
        sources + groups * slot_step.reshape(tiles, 1, per_owner // tiles)
    ).reshape(row_count)
    lowest = spread(slot_seq) * row_count
    code = lowest + token_positions
    keep_rows = spread(slot_keep).reshape(row_count, 1).astype(jnp.float32)
    chosen = (send_rows[:, None] == places[None, :]).astype(jnp.bfloat16)
    put_back = (slot_of[:, None] == places[None, :]).astype(jnp.bfloat16)

    tensor_count = lax.axis_size("tensor")
    tensor_member = lax.axis_index("tensor")
    dealt_shape = (groups, tiles, per_owner // tiles, width_part)
    cosine, sine = rotary_tables(token_positions, HEAD_WIDTH)
    half = HEAD_WIDTH // 2
    tables = (
        cosine,
        jnp.concatenate([-sine[:, :half], sine[:, half:]], axis=1),
        code[None, :],
        code[:, None],
        lowest[:, None],
    )
    weights = (query_weight, key_matrix, value_matrix, output_weight)
    dealt_tokens, dealt_cotangent = (
        matmul(chosen, values).astype(BF).reshape(dealt_shape) for values in (tokens, cotangent)
    )
    owned_tokens, part_cotangent, part_tokens, attn_part, normed_one, *kept, scale_one = deal_in(
        tensor_count,
        groups,
        dealt_tokens,
        dealt_cotangent,
        first_gain[None, :],
        weights,
        tables,
    )
    owned_tokens = owned_tokens.reshape(row_count, -1)
    part_cotangent = part_cotangent.reshape(row_count, width_part)

    def my_part(values):
        return lax.dynamic_slice_in_dim(values, tensor_member * width_part, width_part, 1)

    result, attn_sum, owned_cotangent, normed_two, inner_low, both, second_term = middle(
        tensor_count,
        attn_part,
        owned_tokens,
        part_cotangent,
        keep_rows,
        second_gain[None, :],
        gate_weight,
        up_weight,
        down_weight,
    )
    hidden = gate_weight.shape[1]

    def shared(values):
        return lax.psum_scatter(
            values.astype(jnp.bfloat16), "dp", scatter_dimension=0, tiled=True
        )

    both_grad = matmul(normed_two.T, both).astype(BF)
    second_term, both_grad = lax.optimization_barrier((second_term, both_grad))
    both_share = shared(both_grad)
    grad_attn, grad_res, second_gain_grad, down_grad = second_back_of(
        tensor_count,
        second_term,
        owned_tokens,
        attn_sum,
        owned_cotangent,
        keep_rows,
        second_gain[None, :],
        inner_low,
    )
    both_share, down_grad, grad_attn = lax.optimization_barrier(
        (both_share, down_grad, grad_attn)
    )
    down_share = shared(down_grad)
    back_out, back_grad, gains, o_share, q_share, k_share, v_share = deal_out(
        tensor_count,
        groups,
        tiles,
        part_tokens.reshape(row_count, width_part),
        grad_res,
        scale_one,
        first_gain.reshape(tensor_count, width_part),
        result,
        second_gain_grad,
        normed_one,
        grad_attn,
        *weights,
        *kept,
        *tables,
    )
    down_share, back_out = lax.optimization_barrier((down_share, back_out))
    layer_output = matmul(put_back, back_out.reshape(row_count, width_part)).astype(BF)
    input_grad = matmul(put_back, back_grad.reshape(row_count, width_part)).astype(BF)
    summed = (
        gains[0],
        q_share,
        k_share,
        v_share,
        o_share.T,
        both_share[:, :hidden].astype(F32),
        both_share[:, hidden:].astype(F32),
        down_share.T.astype(F32),
        gains[8],
    )
    return (
        layer_output,
        input_grad,
        summed[0],
        summed[1],
        summed[2],
        summed[3],
        summed[4],
        summed[8],
        summed[5],
        summed[6],
        summed[7],
    )


def solution(mesh):
    placed = (
        P(None, ("dp", "tensor")),
        P(None, ("dp", "tensor")),
        P(),
        P(None, "tensor"),
        P(None, "tensor"),
        P(None, "tensor"),
        P("tensor", None),
        P(),
        P(None, "tensor"),
        P(None, "tensor"),
        P("tensor", None),
        P(),
        P(),
        P(),
    )
    return jax.shard_map(
        per_device,
        mesh=mesh,
        in_specs=placed,
        out_specs=(
            P(None, ("dp", "tensor")),
            P(None, ("dp", "tensor")),
            P("dp"),
            P("dp", "tensor"),
            P("dp", "tensor"),
            P("dp", "tensor"),
            P("tensor", "dp"),
            P("dp"),
            P("dp", "tensor"),
            P("dp", "tensor"),
            P("tensor", "dp"),
        ),
        check_vma=False,
    )
```

```python
import functools
import math

import jax
import jax.numpy as jnp
from jax import lax
from jax.experimental import pallas as pl
from jax.experimental.pallas import tpu as pltpu
from jax.sharding import PartitionSpec as P

HEAD_WIDTH = 128

MESH = pl.DeviceIdType.MESH
VM = pl.BlockSpec(memory_space=pltpu.VMEM)
F32 = jnp.float32
BF = jnp.bfloat16

def neighbour_barrier(z, n, axis):
    barrier = pltpu.get_barrier_semaphore()
    @pl.when(z > 0)
    def _():
        pl.semaphore_signal(barrier, inc=1, device_id={axis: z - 1}, device_id_type=MESH)
    @pl.when(z < n - 1)
    def _():
        pl.semaphore_signal(barrier, inc=1, device_id={axis: z + 1}, device_id_type=MESH)
    ends = jnp.where(z > 0, 1, 0) + jnp.where(z < n - 1, 1, 0)
    pl.semaphore_wait(barrier, ends)

def rcopy(src, dst, ss, rs, dev):
    return pltpu.make_async_remote_copy(src_ref=src, dst_ref=dst, send_sem=ss, recv_sem=rs, device_id={"tensor": dev}, device_id_type=MESH)


eps = 1e-05
rope_base = 10000.0


def nt(left, right):
    return lax.dot_general(left, right, (((1,), (1,)), ((), ())), preferred_element_type=F32)


def tn(left, right):
    return lax.dot_general(left, right, (((0,), (0,)), ((), ())), preferred_element_type=F32)


def mm(left, right):
    return jnp.dot(left, right, preferred_element_type=F32)


def spin(values, cosine, signed_sine):
    return values * cosine + pltpu.roll(values, HEAD_WIDTH // 2, 1) * signed_sine


def visible(code_row, code_col, low_col):
    return jnp.where((code_row <= code_col) & (code_row >= low_col), 0.0, -1e30)


def attend_tile(t, tiles, xt, gain, wq, wk, wv, wo, cosine, sine, code_row, code_col, low_col,
                part, normed, q, k, v, o, lse, scales):
    rows = normed.shape[0]
    tile = rows // tiles
    heads = wq.shape[1] // HEAD_WIDTH
    kv = wk.shape[1] // HEAD_WIDTH
    group = heads // kv
    factor = math.log2(math.e) / math.sqrt(HEAD_WIDTH)
    r = pl.ds(t * tile, tile)
    xt = xt.astype(F32)
    scale = lax.rsqrt(jnp.mean(xt * xt, axis=1, keepdims=True) + eps)
    scales[r, :] = scale
    n1 = (xt * scale * gain[...]).astype(BF)
    normed[r, :] = n1
    c, s = cosine[r, :], sine[r, :]
    pre = mm(n1, wq[...])
    for h in range(heads):
        cut = slice(h * HEAD_WIDTH, (h + 1) * HEAD_WIDTH)
        q[r, cut] = spin(pre[:, cut], c, s).astype(BF)
    pre = mm(n1, wk[...])
    for h in range(kv):
        cut = slice(h * HEAD_WIDTH, (h + 1) * HEAD_WIDTH)
        k[r, cut] = spin(pre[:, cut], c, s).astype(BF)
    v[r, :] = mm(n1, wv[...]).astype(BF)
    seen = (t + 1) * tile
    block = min(tile, 256)
    for at in range(t * tile, (t + 1) * tile, block):
        r = pl.ds(at, block)
        bias = visible(code_row[:, :seen], code_col[r, :], low_col[r, :])
        logs = []
        for h in range(heads):
            cut = slice(h * HEAD_WIDTH, (h + 1) * HEAD_WIDTH)
            mine = slice(h // group * HEAD_WIDTH, (h // group + 1) * HEAD_WIDTH)
            scores = nt(q[r, cut], k[:seen, mine]) * factor + bias
            top = jnp.max(scores, axis=1, keepdims=True)
            expo = jnp.exp2(scores - top)
            total = jnp.sum(expo, axis=1, keepdims=True)
            probs = (expo * (1.0 / total)).astype(BF)
            o[r, cut] = mm(probs, v[:seen, mine]).astype(BF)
            logs.append(top + jnp.log2(total))
        lse[r, :] = jnp.concatenate(logs, axis=1)
        part[r, :] = mm(o[r, :], wo[...]).astype(BF)


def attend_back_tile(t, tiles, ga, wq, wk, wv, wo, q, k, v, o, lse, cosine, sine, code_row, code_col, low_col,
                     part, dqkv, dk, dv):
    rows = ga.shape[0]
    tile = rows // tiles
    heads = wq.shape[1] // HEAD_WIDTH
    kv = wk.shape[1] // HEAD_WIDTH
    group = heads // kv
    wide = heads * HEAD_WIDTH
    narrow = kv * HEAD_WIDTH
    score_scale = 1.0 / math.sqrt(HEAD_WIDTH)
    factor = math.log2(math.e) / math.sqrt(HEAD_WIDTH)
    seen = (t + 1) * tile
    block = min(tile, 256)
    for at in range(t * tile, (t + 1) * tile, block):
        r = pl.ds(at, block)
        do = nt(ga[r, :], wo[...]).astype(BF)
        c, s = cosine[r, :], sine[r, :]
        bias = visible(code_row[:, :seen], code_col[r, :], low_col[r, :])
        logs = lse[r, :]
        for h in range(heads):
            cut = slice(h * HEAD_WIDTH, (h + 1) * HEAD_WIDTH)
            mine = slice(h // group * HEAD_WIDTH, (h // group + 1) * HEAD_WIDTH)
            do_h = do[:, cut]
            qh = q[r, cut]
            probs = jnp.exp2(nt(qh, k[:seen, mine]) * factor + bias - logs[:, h : h + 1])
            along = jnp.sum(do_h.astype(F32) * o[r, cut].astype(F32), axis=1, keepdims=True)
            ds = (probs * (nt(do_h, v[:seen, mine]) - along)).astype(BF)
            pb = probs.astype(BF)
            dq = mm(ds, k[:seen, mine]) * score_scale
            dqkv[r, cut] = spin(dq, c, -s).astype(BF)
            more_k = tn(ds, qh)
            more_v = tn(pb, do_h)
            if t == tiles - 1 and at == t * tile and h % group == 0:
                dk[:seen, mine] = more_k
                dv[:seen, mine] = more_v
            else:
                dk[:seen, mine] += more_k
                dv[:seen, mine] += more_v
    for at in range(t * tile, (t + 1) * tile, block):
        r = pl.ds(at, block)
        c, s = cosine[r, :], sine[r, :]
        for h in range(kv):
            cut = slice(h * HEAD_WIDTH, (h + 1) * HEAD_WIDTH)
            low = wide + h * HEAD_WIDTH
            dqkv[r, low : low + HEAD_WIDTH] = spin(dk[r, cut] * score_scale, c, -s).astype(BF)
        dqkv[r, wide + narrow :] = dv[r, :].astype(BF)
        part[r, :] = (
            nt(dqkv[r, :wide], wq[...])
            + nt(dqkv[r, wide : wide + narrow], wk[...])
            + nt(dqkv[r, wide + narrow :], wv[...])
        ).astype(BF)


ANY = pl.BlockSpec(memory_space=pl.ANY)
LAG = 2
CHUNK = 32
BLOCK = 128


def line_row(f, c):
    per = BLOCK // CHUNK
    return pl.ds(pl.multiple_of(lax.div(c, per) * (2 * BLOCK) + f * BLOCK + lax.rem(c, per) * CHUNK, CHUNK), CHUNK)


def line_steps(n, rows):
    return rows // 2 // CHUNK + 2 * LAG * (n - 1)


def line_sum_step(n, z, t, part, up, out, sems):
    us, ur, ds, dr = sems
    count = part.shape[0] // 2 // CHUNK
    for f in range(2):
        p = z if f == 0 else n - 1 - z
        step = 1 if f == 0 else -1
        c = t - LAG * p

        @pl.when((c >= 0) & (c < count))
        def _():
            r = line_row(f, c)

            @pl.when(p == 0)
            def _():
                rcopy(part.at[r], up.at[r], us.at[f, c], ur.at[f, c], z + step).start()

            @pl.when(p > 0)
            def _():
                rcopy(up.at[r], up.at[r], us.at[f, c], ur.at[f, c], z).wait_recv()
                s = (part[r, :].astype(F32) + up[r, :].astype(F32)).astype(BF)

                @pl.when(p < n - 1)
                def _():
                    up[r, :] = s
                    rcopy(up.at[r], up.at[r], us.at[f, c], ur.at[f, c], z + step).start()

                @pl.when(p == n - 1)
                def _():
                    out[r, :] = s
                    rcopy(out.at[r], out.at[r], ds.at[f, c], dr.at[f, c], z - step).start()

    for f in range(2):
        p = z if f == 0 else n - 1 - z
        step = 1 if f == 0 else -1
        c = t - LAG * (2 * (n - 1) - p)

        @pl.when((c >= 0) & (c < count) & (p < n - 1))
        def _():
            r = line_row(f, c)
            rcopy(out.at[r], out.at[r], ds.at[f, c], dr.at[f, c], z).wait_recv()

            @pl.when(p > 0)
            def _():
                rcopy(out.at[r], out.at[r], ds.at[f, c], dr.at[f, c], z - step).start()


def line_sum_drain(n, z, part, up, out, sems):
    us, ur, ds, dr = sems
    count = part.shape[0] // 2 // CHUNK

    def drain(c, _):
        for f in range(2):
            p = z if f == 0 else n - 1 - z
            r = line_row(f, c)

            @pl.when(p < n - 1)
            def _():
                rcopy(up.at[r], up.at[r], us.at[f, c], ur.at[f, c], z).wait_send()

            @pl.when(p > 0)
            def _():
                rcopy(out.at[r], out.at[r], ds.at[f, c], dr.at[f, c], z).wait_send()

        return 0

    lax.fori_loop(0, count, drain, 0)


def line_sum_sems(rows):
    return [pltpu.SemaphoreType.DMA((2, rows // 2 // CHUNK))] * 4


def gather_cut(ref, o, c, w):
    return ref.at[pl.ds(pl.multiple_of(c * BLOCK, BLOCK), BLOCK), pl.ds(pl.multiple_of(o * w, w), w)]


def line_gather_step(n, z, t, src, out, ss, rs):
    rows, w = src.shape
    count = rows // BLOCK

    @pl.when(t < count)
    def _():
        mine = src.at[pl.ds(pl.multiple_of(t * BLOCK, BLOCK), BLOCK)]

        @pl.when(z < n - 1)
        def _():
            rcopy(mine, gather_cut(out, z, t, w), ss.at[0, z, t], rs.at[0, z, t], z + 1).start()

        @pl.when(z > 0)
        def _():
            rcopy(mine, gather_cut(out, z, t, w), ss.at[1, z, t], rs.at[1, z, t], z - 1).start()

    for hop in range(1, n):
        c = t - hop
        for d, step in ((0, 1), (1, -1)):
            o = z - hop * step

            @pl.when((c >= 0) & (c < count) & (o >= 0) & (o < n))
            def _():
                cut = gather_cut(out, o, c, w)
                rcopy(cut, cut, ss.at[d, o, c], rs.at[d, o, c], z).wait_recv()
                after = z + step

                @pl.when((after >= 0) & (after < n))
                def _():
                    rcopy(cut, cut, ss.at[d, o, c], rs.at[d, o, c], after).start()


def line_gather_drain(n, z, src, out, ss, rs):
    rows, w = src.shape

    def drain(c, _):
        for d in range(2):
            for o in range(n):
                on = (o <= z) & (z < n - 1) if d == 0 else (o >= z) & (z > 0)

                @pl.when(on)
                def _():
                    cut = gather_cut(out, o, c, w)
                    rcopy(cut, cut, ss.at[d, o, c], rs.at[d, o, c], z).wait_send()

        return 0

    lax.fori_loop(0, rows // BLOCK, drain, 0)


def middle_kernel(n, part, x_far, g_part, keep, gain, wg_far, wu_far, wd_far,
                  result, a_far, g_far, n2_far, inner_far, both_far, dn2_far,
                  wg, wu, wd, x, up, total, g, right, left, gate_s, upper_s, n2_s, inner_s, both_s, f_s, dn2_s,
                  us, ur, ds, dr, ss, rs, fs, fr, load, own, save, late):
    z = lax.axis_index("tensor")
    rows, width = part.shape
    w = g_part.shape[1]
    hidden = wg.shape[1]
    tile = 2 * BLOCK
    sums = (us, ur, ds, dr)
    loads = [pltpu.make_async_copy(a, b, load.at[i]) for i, (a, b) in enumerate(((x_far, x), (wg_far, wg), (wu_far, wu), (wd_far, wd)))]
    for copy in loads:
        copy.start()
    mine = pltpu.make_async_copy(g_part, g.at[:, pl.ds(pl.multiple_of(z * w, w), w)], own)
    mine.start()
    neighbour_barrier(z, n, "tensor")

    def saves(d):
        r = pl.ds(pl.multiple_of(d * tile, tile), tile)
        pairs = ((n2_s, n2_far), (inner_s, inner_far), (both_s, both_far), (dn2_s, dn2_far))
        return [pltpu.make_async_copy(a, b.at[r], save.at[i]) for i, (a, b) in enumerate(pairs)]

    first = BLOCK // CHUNK - 1 + 2 * LAG * (n - 1)

    def body(t, _):
        line_sum_step(n, z, t, part, up, total, sums)

        @pl.when(lax.rem(t, 2) == 0)
        def _():
            line_gather_step(n, z, lax.div(t, 2), g_part, g, ss, rs)

        q = t - first
        d = lax.div(jnp.maximum(q, 0), 4)
        k = lax.rem(jnp.maximum(q, 0), 4)
        r = pl.ds(pl.multiple_of(d * tile, tile), tile)

        @pl.when((q >= 0) & (d < rows // tile) & (k == 0))
        def _():
            @pl.when(d == 0)
            def _():
                for copy in loads:
                    copy.wait()
                mine.wait()

            @pl.when(d > 0)
            def _():
                for copy in saves(d - 1):
                    copy.wait()

            h = x[r, :].astype(F32) + keep[r, :] * total[r, :].astype(F32)
            scale = lax.rsqrt(jnp.mean(h * h, axis=1, keepdims=True) + eps)
            n2_s[...] = (h * scale * gain[...]).astype(BF)
            gate_s[...] = mm(n2_s[...], wg[...])

        @pl.when((q >= 0) & (d < rows // tile) & (k == 1))
        def _():
            upper_s[...] = mm(n2_s[...], wu[...])
            gate = gate_s[...]
            inner_s[...] = (gate * jax.nn.sigmoid(gate) * upper_s[...]).astype(BF)

        @pl.when((q >= 0) & (d < rows // tile) & (k == 2))
        def _():
            f_s[lax.rem(d, 2)] = mm(inner_s[...], wd[...]).astype(BF)
            gf = (keep[r, :] * g[r, :].astype(F32)).astype(BF)
            back = nt(gf, wd[...])
            gate = gate_s[...]
            s = jax.nn.sigmoid(gate)
            both_s[:, :hidden] = (back * upper_s[...] * s * (1.0 + gate * (1.0 - s))).astype(BF)
            both_s[:, hidden:] = (back * (gate * s)).astype(BF)

        @pl.when((q >= 0) & (d < rows // tile) & (k == 3))
        def _():
            dn2_s[...] = (nt(both_s[:, :hidden], wg[...]) + nt(both_s[:, hidden:], wu[...])).astype(BF)
            for copy in saves(d):
                copy.start()

        scatter_step(t - first - 2)
        return 0

    chunk = tile // 4
    count = rows // chunk

    def at(ref, c, b):
        return ref.at[pl.ds(pl.multiple_of(c * chunk, chunk), chunk), pl.ds(b * w, w)]

    def scatter_copy(buf, d, c, b, to):
        return rcopy(at(buf, c, b), at(buf, c, b), fs.at[d, b, c], fr.at[d, b, c], to)

    def scatter_step(s):
        for d, buf, step in ((0, right, 1), (1, left, -1)):
            p = z if d == 0 else n - 1 - z
            c = s - p

            @pl.when((c >= 0) & (c < count))
            def _():
                r = pl.ds(pl.multiple_of(c * chunk, chunk), chunk)
                slot = lax.rem(lax.div(c, 4), 2)
                inner = pl.ds(pl.multiple_of(lax.rem(c, 4) * chunk, chunk), chunk)
                for b in range(n - 1, 0, -1) if d == 0 else range(n - 1):
                    k = pl.ds(b * w, w)

                    @pl.when((b > z) if d == 0 else (b < z))
                    def _():
                        @pl.when(p == 0)
                        def _():
                            buf[r, k] = f_s[slot, inner, k]

                        @pl.when(p > 0)
                        def _():
                            scatter_copy(buf, d, c, b, z).wait_recv()
                            buf[r, k] = (f_s[slot, inner, k].astype(F32) + buf[r, k].astype(F32)).astype(BF)

                        scatter_copy(buf, d, c, b, z + step).start()

        c = s - (n - 1)

        @pl.when((c >= 0) & (c < count))
        def _():
            r = pl.ds(pl.multiple_of(c * chunk, chunk), chunk)
            slot = lax.rem(lax.div(c, 4), 2)
            inner = pl.ds(pl.multiple_of(lax.rem(c, 4) * chunk, chunk), chunk)
            for b in range(n):
                k = pl.ds(b * w, w)

                @pl.when(z == b)
                def _():
                    f = f_s[slot, inner, k].astype(F32)
                    if b > 0:
                        scatter_copy(right, 0, c, b, z).wait_recv()
                        f = f + right[r, k].astype(F32)
                    if b < n - 1:
                        scatter_copy(left, 1, c, b, z).wait_recv()
                        f = f + left[r, k].astype(F32)
                    kept = keep[r, :]
                    h = x[r, k].astype(F32) + kept * total[r, k].astype(F32)
                    result[r, :] = (h + kept * f).astype(BF)

    lax.fori_loop(0, first + 2 + count + n, body, 0)

    def drain(c, _):
        for d, buf in ((0, right), (1, left)):
            for b in range(n):

                @pl.when((b > z) if d == 0 else (b < z))
                def _():
                    scatter_copy(buf, d, c, b, z).wait_send()

        return 0

    lax.fori_loop(0, count, drain, 0)
    ends = [pltpu.make_async_copy(a, b, late.at[i]) for i, (a, b) in enumerate(((total, a_far), (g, g_far)))]
    for copy in ends:
        copy.start()
    line_sum_drain(n, z, part, up, total, sums)
    line_gather_drain(n, z, g_part, g, ss, rs)
    for copy in saves(rows // tile - 1) + ends:
        copy.wait()


def middle(n, part, x, g_part, keep, gain, wg, wu, wd):
    rows, width = part.shape
    hidden = wg.shape[1]
    tile = 2 * BLOCK
    blocks = rows // BLOCK
    w = g_part.shape[1]
    widths = (w, width, width, width, hidden, 2 * hidden, width)
    return pl.pallas_call(
        functools.partial(middle_kernel, n),
        out_shape=[jax.ShapeDtypeStruct((rows, k), BF) for k in widths],
        in_specs=[VM, ANY] + [VM] * 3 + [ANY] * 3,
        out_specs=[VM] + [ANY] * 6,
        scratch_shapes=[
            pltpu.VMEM(wg.shape, BF),
            pltpu.VMEM(wu.shape, BF),
            pltpu.VMEM(wd.shape, BF),
            pltpu.VMEM((rows, width), BF),
            pltpu.VMEM((rows, width), BF),
            pltpu.VMEM((rows, width), BF),
            pltpu.VMEM((rows, width), BF),
            pltpu.VMEM((rows, width), BF),
            pltpu.VMEM((rows, width), BF),
            pltpu.VMEM((tile, hidden), F32),
            pltpu.VMEM((tile, hidden), F32),
            pltpu.VMEM((tile, width), BF),
            pltpu.VMEM((tile, hidden), BF),
            pltpu.VMEM((tile, 2 * hidden), BF),
            pltpu.VMEM((2, tile, width), BF),
            pltpu.VMEM((tile, width), BF),
            *line_sum_sems(rows),
            pltpu.SemaphoreType.DMA((2, n, blocks)),
            pltpu.SemaphoreType.DMA((2, n, blocks)),
            pltpu.SemaphoreType.DMA((2, n, rows // tile * 4)),
            pltpu.SemaphoreType.DMA((2, n, rows // tile * 4)),
            pltpu.SemaphoreType.DMA((4,)),
            pltpu.SemaphoreType.DMA,
            pltpu.SemaphoreType.DMA((4,)),
            pltpu.SemaphoreType.DMA((2,)),
        ],
        compiler_params=pltpu.CompilerParams(collective_id=3, has_side_effects=True, vmem_limit_bytes=63 << 20),
    )(part, x, g_part, keep, gain, wg, wu, wd)


def second_back_kernel(n, part, x_far, a_far, g_far, keep, gain, inner_far, ga, dh, gain_grad, grad_far,
                       up, total, x, a, g, inner, stage, us, ur, ds, dr, load, save):
    z = lax.axis_index("tensor")
    rows, width = part.shape
    w = dh.shape[1]
    piece = BLOCK // 2
    sums = (us, ur, ds, dr)
    pairs = ((g_far, g), (inner_far, inner), (x_far, x), (a_far, a))
    loads = [pltpu.make_async_copy(far, near, load.at[i]) for i, (far, near) in enumerate(pairs)]
    for copy in loads:
        copy.start()
    neighbour_barrier(z, n, "tensor")
    span = stage.shape[1]
    spans = width // span

    def saved(j):
        slot = lax.rem(j, 2)
        return pltpu.make_async_copy(stage.at[slot], grad_far.at[pl.ds(pl.multiple_of(j * span, span), span)], save.at[slot])

    gain_grad[...] = jnp.zeros_like(gain_grad)
    first = BLOCK // CHUNK - 1 + 2 * LAG * (n - 1)

    def body(t, _):
        line_sum_step(n, z, t, part, up, total, sums)
        j = t - 3

        @pl.when((j >= 0) & (j < spans))
        def _():
            @pl.when(j == 0)
            def _():
                for copy in loads:
                    copy.wait()

            @pl.when(j >= 2)
            def _():
                saved(j - 2).wait()

            cut = pl.ds(pl.multiple_of(j * span, span), span)
            gf = (keep[...] * g[:, cut].astype(F32)).astype(BF)
            stage[lax.rem(j, 2)] = tn(gf, inner[...]).astype(BF)
            saved(j).start()

        q = t - first

        @pl.when(q >= 0)
        def _():
            r = pl.ds(pl.multiple_of(q * piece, piece), piece)
            h = x[r, :].astype(F32) + keep[r, :] * a[r, :].astype(F32)
            scale = lax.rsqrt(jnp.mean(h * h, axis=1, keepdims=True) + eps)
            back = total[r, :].astype(F32)
            gain_grad[...] += jnp.sum(back * h * scale, axis=0, keepdims=True)
            e = back * gain[...]
            along = jnp.mean(e * h, axis=1, keepdims=True)
            full = g[r, :].astype(F32) + scale * e - h * (scale * scale * scale * along)
            ga[r, :] = (keep[r, :] * full).astype(BF)
            for b in range(n):

                @pl.when(z == b)
                def _():
                    dh[r, :] = full[:, b * w : (b + 1) * w]

        return 0

    lax.fori_loop(0, first + rows // piece, body, 0)
    line_sum_drain(n, z, part, up, total, sums)
    for j in range(spans - 2, spans):
        saved(j).wait()


def second_back_of(n, part, x, a, g, keep, gain, inner):
    rows, width = part.shape
    return pl.pallas_call(
        functools.partial(second_back_kernel, n),
        out_shape=[
            jax.ShapeDtypeStruct((rows, width), BF),
            jax.ShapeDtypeStruct((rows, width // n), F32),
            jax.ShapeDtypeStruct((1, width), F32),
            jax.ShapeDtypeStruct((width, inner.shape[1]), BF),
        ],
        in_specs=[VM] + [ANY] * 3 + [VM] * 2 + [ANY],
        out_specs=[VM] * 3 + [ANY],
        scratch_shapes=[
            pltpu.VMEM((rows, width), BF),
            pltpu.VMEM((rows, width), BF),
            *(pltpu.VMEM((rows, width), BF) for _ in range(3)),
            pltpu.VMEM(inner.shape, BF),
            pltpu.VMEM((2, 256, inner.shape[1]), BF),
            *line_sum_sems(rows),
            pltpu.SemaphoreType.DMA((4,)),
            pltpu.SemaphoreType.DMA((2,)),
        ],
        compiler_params=pltpu.CompilerParams(collective_id=4, has_side_effects=True, vmem_limit_bytes=60 << 20),
    )(part, x, a, g, keep, gain, inner)


def peers_barrier(z, n, me, groups, everyone):
    barrier = pltpu.get_barrier_semaphore()

    def greet(off, _):
        peer = lax.rem(me + off, groups)
        pl.semaphore_signal(barrier, inc=1, device_id={"dp": peer}, device_id_type=MESH)
        return 0

    lax.fori_loop(1, groups, greet, 0)
    if everyone:
        for off in range(1, n):
            other = lax.rem(z + off, n)
            pl.semaphore_signal(barrier, inc=1, device_id={"tensor": other}, device_id_type=MESH)
        pl.semaphore_wait(barrier, groups - 1 + n - 1)
    else:

        @pl.when(z > 0)
        def _():
            pl.semaphore_signal(barrier, inc=1, device_id={"tensor": z - 1}, device_id_type=MESH)

        @pl.when(z < n - 1)
        def _():
            pl.semaphore_signal(barrier, inc=1, device_id={"tensor": z + 1}, device_id_type=MESH)

        ends = jnp.where(z > 0, 1, 0) + jnp.where(z < n - 1, 1, 0)
        pl.semaphore_wait(barrier, groups - 1 + ends)


def pcopy(src, dst, ss, rs, peer):
    return pltpu.make_async_remote_copy(
        src_ref=src, dst_ref=dst, send_sem=ss, recv_sem=rs, device_id={"dp": peer}, device_id_type=MESH
    )


def deal_in_kernel(n, groups, dealt_x, dealt_g, gain, cosine, sine, code_row, code_col, low_col, *refs):
    far, (full, g_part, x_part), results = refs[:4], refs[4:7], refs[7:15]
    near, (xs, xr, gs, gr, ss, rs, own, load) = refs[15:19], refs[19:]
    loads = [pltpu.make_async_copy(a, b, load.at[i]) for i, (a, b) in enumerate(zip(far, near))]
    for copy in loads:
        copy.start()
    z = lax.axis_index("tensor")
    me = lax.axis_index("dp")
    tiles, sub, w = dealt_x.shape[1:]
    cols = pl.ds(pl.multiple_of(z * w, w), w)

    def place(t, i):
        return full.at[t, i, :, cols]

    for t in range(tiles):
        pltpu.make_async_copy(dealt_x.at[me, t], place(t, me), own.at[t]).start()
    pltpu.make_async_copy(dealt_g.at[me], g_part.at[:, me], own.at[tiles]).start()
    peers_barrier(z, n, me, groups, False)

    def send(t):
        def one(off, _):
            peer = lax.rem(me + off, groups)
            pcopy(dealt_x.at[peer, t], place(t, me), xs.at[t, peer], xr.at[t, me], peer).start()
            return 0

        lax.fori_loop(1, groups, one, 0)

    def cut(o, t):
        return full.at[t, :, :, pl.ds(pl.multiple_of(o * w, w), w)]

    for t in range(tiles):
        send(t)

    def send_g(off, _):
        peer = lax.rem(me + off, groups)
        pcopy(dealt_g.at[peer], g_part.at[:, me], gs.at[peer], gr.at[me], peer).start()
        return 0

    lax.fori_loop(1, groups, send_g, 0)
    for s in range(tiles + n - 1):
        if s < tiles:

            def got(off, _):
                peer = lax.rem(me + off, groups)
                pcopy(dealt_x.at[peer, s], place(s, peer), xs.at[s, peer], xr.at[s, peer], peer).wait_recv()
                return 0

            lax.fori_loop(1, groups, got, 0)
            pltpu.make_async_copy(dealt_x.at[me, s], place(s, me), own.at[s]).wait()

            @pl.when(z < n - 1)
            def _():
                rcopy(cut(z, s), cut(z, s), ss.at[0, z, s], rs.at[0, z, s], z + 1).start()

            @pl.when(z > 0)
            def _():
                rcopy(cut(z, s), cut(z, s), ss.at[1, z, s], rs.at[1, z, s], z - 1).start()

        for hop in range(1, n):
            c = s - hop
            if 0 <= c < tiles:
                for d, step in ((0, 1), (1, -1)):
                    o = z - hop * step

                    @pl.when((o >= 0) & (o < n))
                    def _():
                        rcopy(cut(o, c), cut(o, c), ss.at[d, o, c], rs.at[d, o, c], z).wait_recv()
                        after = z + step

                        @pl.when((after >= 0) & (after < n))
                        def _():
                            rcopy(cut(o, c), cut(o, c), ss.at[d, o, c], rs.at[d, o, c], after).start()

        if s == tiles - 1:
            pltpu.make_async_copy(full.at[:, :, :, cols], x_part, own.at[tiles + 1]).start()
        t = s - (n - 1)
        if t >= 0:
            if t == 0:
                for copy in loads:
                    copy.wait()
            attend_tile(
                t,
                tiles,
                full[t].reshape(groups * sub, n * w),
                gain,
                *near,
                cosine,
                sine,
                code_row,
                code_col,
                low_col,
                *results,
            )

    def finish(off, _):
        peer = lax.rem(me + off, groups)
        copy = pcopy(dealt_g.at[peer], g_part.at[:, peer], gs.at[peer], gr.at[peer], peer)
        copy.wait_recv()
        copy.wait_send()
        for t in range(tiles):
            pcopy(dealt_x.at[peer, t], place(t, peer), xs.at[t, peer], xr.at[t, peer], peer).wait_send()
        return 0

    lax.fori_loop(1, groups, finish, 0)
    pltpu.make_async_copy(dealt_g.at[me], g_part.at[:, me], own.at[tiles]).wait()
    pltpu.make_async_copy(full.at[:, :, :, cols], x_part, own.at[tiles + 1]).wait()
    for c in range(tiles):
        for d in range(2):
            for o in range(n):

                @pl.when((o <= z) & (z < n - 1) if d == 0 else (o >= z) & (z > 0))
                def _():
                    rcopy(cut(o, c), cut(o, c), ss.at[d, o, c], rs.at[d, o, c], z).wait_send()


def deal_in(n, groups, dealt_x, dealt_g, gain, weights, tables):
    tiles, sub, w = dealt_x.shape[1:]
    rows = tiles * groups * sub
    wq, wk, wv, wo = weights
    dma = pltpu.SemaphoreType.DMA
    widths = (n * w, n * w, wq.shape[1], wk.shape[1], wv.shape[1], wq.shape[1])
    return pl.pallas_call(
        functools.partial(deal_in_kernel, n, groups),
        out_shape=[
            jax.ShapeDtypeStruct((tiles, groups, sub, n * w), BF),
            jax.ShapeDtypeStruct((tiles, groups, sub, w), BF),
            jax.ShapeDtypeStruct((tiles, groups, sub, w), BF),
            *(jax.ShapeDtypeStruct((rows, k), BF) for k in widths),
            jax.ShapeDtypeStruct((rows, wq.shape[1] // HEAD_WIDTH), F32),
            jax.ShapeDtypeStruct((rows, 1), F32),
        ],
        in_specs=[VM] * 8 + [ANY] * 4,
        out_specs=[VM] * 11,
        scratch_shapes=[
            *(pltpu.VMEM(a.shape, BF) for a in weights),
            dma((tiles, groups)),
            dma((tiles, groups)),
            dma((groups,)),
            dma((groups,)),
            dma((2, n, tiles)),
            dma((2, n, tiles)),
            dma((tiles + 2,)),
            dma((4,)),
        ],
        compiler_params=pltpu.CompilerParams(collective_id=6, has_side_effects=True, vmem_limit_bytes=60 << 20),
    )(dealt_x, dealt_g, gain, *tables, *weights)


def exact(left, right, contract):
    return lax.dot_general(
        left, right, (contract, ((), ())), preferred_element_type=F32, precision=lax.Precision.HIGHEST
    )


def deal_out_kernel(n, groups, tiles, chunk, lag, x, dh, scale1, gain1, result, gain2, normed_far, *refs):
    attention = refs[:15]
    (back_out, back_dx, gains, o_share, q_share, k_share, v_share, part, dqkv, dk, dv, right, left, fb, dx, lines, widths, gsrc, gdst, wsrc, wdst, pair, normed,
     ss, rs, os, orr, xs, xr, ls, lr, ws, wr, es, er, qs, qr, ps, pr, own) = refs[15:]
    ga, o = attention[0], attention[8]
    z = lax.axis_index("tensor")
    me = lax.axis_index("dp")
    rows, w = x.shape
    tile = rows // tiles
    count = rows // chunk
    per = tile // chunk
    sub = result.shape[2]
    pltpu.make_async_copy(result.at[:, me], back_out.at[me], own.at[0]).start()
    fetch = pltpu.make_async_copy(normed_far, normed, own.at[2 + tiles])
    fetch.start()
    peers_barrier(z, n, me, groups, True)

    def send_out(off, _):
        peer = lax.rem(me + off, groups)
        pcopy(result.at[:, peer], back_out.at[me], os.at[peer], orr.at[me], peer).start()
        return 0

    lax.fori_loop(1, groups, send_out, 0)

    def chunk_rows(c):
        t = tiles - 1 - lax.div(c, per)
        return pl.ds(pl.multiple_of(t * tile + lax.rem(c, per) * chunk, chunk), chunk)

    def at(ref, c, b):
        return ref.at[chunk_rows(c), pl.ds(b * w, w)]

    widths[...] = jnp.zeros_like(widths)

    def others(f):
        for off in range(1, n):
            f(lax.rem(z + off, n))

    def line_copy(t, slot, other):
        cut = lines.at[slot, :, pl.ds(pl.multiple_of(t * tile, tile), tile)]
        return rcopy(cut, cut, ls.at[other, t], lr.at[slot, t], other)

    def width_copy(slot, other):
        cut = widths.at[slot]
        return rcopy(cut, cut, ws.at[other], wr.at[slot], other)

    def open_tile(t):
        r = pl.ds(pl.multiple_of(t * tile, tile), tile)
        e = fb[r, :] * gain1[pl.ds(z, 1), :]
        xt = x[r, :].astype(F32)
        lines[z, :, r] = exact(jnp.ones((8, w), F32), e * xt, ((1,), (1,)))
        others(lambda other: line_copy(t, z, other).start())
        grown = jnp.sum(fb[r, :] * xt * scale1[r, :], axis=0, keepdims=True)
        widths[z, :, :] += jnp.broadcast_to(grown, (8, w))

        @pl.when(t == 0)
        def _():
            others(lambda other: width_copy(z, other).start())

    def close_tile(t):
        r = pl.ds(pl.multiple_of(t * tile, tile), tile)
        others(lambda other: line_copy(t, other, other).wait_recv())
        total = lines[0, :, r]
        for j in range(1, n):
            total = total + lines[j, :, r]
        along = exact(total * (1.0 / (8 * n * w)), jnp.ones((8, w), F32), ((0,), (0,)))
        e = fb[r, :] * gain1[pl.ds(z, 1), :]
        s = scale1[r, :]
        full = dh[r, :] + s * e - x[r, :].astype(F32) * (s * s * s * along)
        dx[t] = full.astype(BF).reshape(groups, sub, w)
        pltpu.make_async_copy(dx.at[t, me], back_dx.at[me, t], own.at[1 + t]).start()

        def one(off, _):
            peer = lax.rem(me + off, groups)
            pcopy(dx.at[t, peer], back_dx.at[me, t], xs.at[t, peer], xr.at[t, me], peer).start()
            return 0

        lax.fori_loop(1, groups, one, 0)

    ow = o.shape[1]
    share = normed.shape[1] // groups
    span = max(share, 256)

    half = groups // 2
    seat = lax.div(me, 2)
    parity = lax.rem(me, 2)
    partner = me + 1 - 2 * parity

    def rows_of(owner):
        return pl.ds(pl.multiple_of(owner * share, share), share)

    def weight_copy(kind, src, dst, sems, to, slot, at_column, wide):
        columns = pl.ds(at_column, wide)
        return pltpu.make_async_remote_copy(
            src_ref=wsrc.at[rows_of(src), columns],
            dst_ref=dst.at[slot, :, columns],
            send_sem=sems[0].at[kind, lax.div(src, 2)],
            recv_sem=sems[1].at[kind, slot],
            device_id={"dp": to},
            device_id_type=MESH,
        )

    def weigh(left_ref, right_ref, at_column, kind):
        wide = right_ref.shape[1]

        def one(j, _):
            base = pl.multiple_of(j * span, span)
            cut = pl.ds(base, span)
            wsrc[cut, at_column : at_column + wide] = tn(left_ref[:, cut], right_ref[...]).astype(BF)
            for i in range(span // share):
                owner = lax.div(base, share) + i

                @pl.when(lax.rem(owner, 2) != parity)
                def _():
                    weight_copy(kind, owner, pair, (ps, pr), partner, lax.div(owner, 2), at_column, wide).start()

            return 0

        lax.fori_loop(0, normed.shape[1] // span, one, 0)

    def join(at_column, wide, kind):
        columns = slice(at_column, at_column + wide)

        def one(off, _):
            m = lax.rem(seat + off, half)
            owner = 2 * m + parity
            weight_copy(kind, owner, pair, (ps, pr), partner, m, at_column, wide).wait_recv()
            r = rows_of(owner)
            total = (wsrc[r, columns].astype(F32) + pair[m, :, columns].astype(F32)).astype(BF)

            @pl.when(owner == me)
            def _():
                wdst[seat, :, columns] = total

            @pl.when(owner != me)
            def _():
                wsrc[r, columns] = total
                weight_copy(kind, owner, wdst, (qs, qr), owner, seat, at_column, wide).start()

            return 0

        lax.fori_loop(1, half + 1, one, 0)

    joined = ((0, ow), (ow, dqkv.shape[1]))

    def flows(s, _):
        for k in range(tiles):

            @pl.when(s == k * 3)
            def _():
                attend_back_tile(tiles - 1 - k, tiles, *attention, part, dqkv, dk, dv)

        @pl.when(s == 2)
        def _():
            weigh(ga, o, 0, 0)

        @pl.when(s == 5)
        def _():
            join(*joined[0], 0)

        @pl.when(s == (tiles - 1) * 3 + 3)
        def _():
            join(*joined[1], 1)

        @pl.when(s == (tiles - 1) * 3 + 1)
        def _():
            fetch.wait()
            weigh(normed, dqkv, ow, 1)

        for d, buf, step in ((0, right, 1), (1, left, -1)):
            p = z if d == 0 else n - 1 - z
            c = s - lag * p

            @pl.when((c >= 0) & (c < count))
            def _():
                r = chunk_rows(c)
                for b in range(n - 1, 0, -1) if d == 0 else range(n - 1):
                    k = pl.ds(b * w, w)

                    @pl.when((b > z) if d == 0 else (b < z))
                    def _():
                        @pl.when(p == 0)
                        def _():
                            rcopy(at(part, c, b), at(buf, c, b), ss.at[d, b, c], rs.at[d, b, c], z + step).start()

                        @pl.when(p > 0)
                        def _():
                            rcopy(at(buf, c, b), at(buf, c, b), ss.at[d, b, c], rs.at[d, b, c], z).wait_recv()
                            buf[r, k] = (part[r, k].astype(F32) + buf[r, k].astype(F32)).astype(BF)
                            rcopy(at(buf, c, b), at(buf, c, b), ss.at[d, b, c], rs.at[d, b, c], z + step).start()

        c = s - lag * (n - 1)

        @pl.when((c >= 0) & (c < count))
        def _():
            r = chunk_rows(c)
            for b in range(n):
                k = pl.ds(b * w, w)

                @pl.when(z == b)
                def _():
                    total = part[r, k].astype(F32)
                    if b > 0:
                        rcopy(at(right, c, b), at(right, c, b), ss.at[0, b, c], rs.at[0, b, c], z).wait_recv()
                        total = total + right[r, k].astype(F32)
                    if b < n - 1:
                        rcopy(at(left, c, b), at(left, c, b), ss.at[1, b, c], rs.at[1, b, c], z).wait_recv()
                        total = total + left[r, k].astype(F32)
                    fb[r, :] = total

        @pl.when((c >= 0) & (c < count) & (lax.rem(jnp.maximum(c, 0), per) == per - 1))
        def _():
            open_tile(tiles - 1 - lax.div(c, per))

        c = c - 2

        @pl.when((c >= 0) & (lax.rem(jnp.maximum(c, 0), per) == per - 1))
        def _():
            close_tile(tiles - 1 - lax.div(c, per))

        return 0

    lax.fori_loop(0, count + lag * (n - 1) + 2, flows, 0)

    others(lambda other: width_copy(other, other).wait_recv())
    cols = gsrc.shape[2]
    first_gain = jnp.concatenate([widths[j] for j in range(n)], axis=1)
    second_gain = jnp.broadcast_to(gain2[...], first_gain.shape)
    for i in range(groups):
        gsrc[i, :8, :] = first_gain[:, i * cols : (i + 1) * cols]
        gsrc[i, 8:, :] = second_gain[:, i * cols : (i + 1) * cols]
    pltpu.make_async_copy(gsrc.at[me], gdst.at[me], own.at[1 + tiles]).start()

    def send_gain(off, _):
        peer = lax.rem(me + off, groups)
        pcopy(gsrc.at[peer], gdst.at[me], es.at[peer], er.at[me], peer).start()
        return 0

    lax.fori_loop(1, groups, send_gain, 0)

    def got_gain(off, _):
        peer = lax.rem(me + off, groups)
        copy = pcopy(gsrc.at[peer], gdst.at[peer], es.at[peer], er.at[peer], peer)
        copy.wait_recv()
        copy.wait_send()
        return 0

    lax.fori_loop(1, groups, got_gain, 0)
    pltpu.make_async_copy(gsrc.at[me], gdst.at[me], own.at[1 + tiles]).wait()
    total = gdst[0]
    for i in range(1, groups):
        total = total + gdst[i]
    gains[...] = total

    def got_weight(off, _):
        m = lax.rem(seat + off, half)
        for kind, (at_column, wide) in enumerate(joined):
            copy = weight_copy(kind, 2 * m + parity, wdst, (qs, qr), me, m, at_column, wide)
            copy.wait_recv()
            copy.wait_send()
        return 0

    def sent_weight(m, _):
        for kind, (at_column, wide) in enumerate(joined):
            weight_copy(kind, 2 * m + 1 - parity, pair, (ps, pr), partner, m, at_column, wide).wait_send()
        return 0

    lax.fori_loop(1, half, got_weight, 0)
    lax.fori_loop(0, half, sent_weight, 0)
    at_column = 0
    for share_ref in (o_share, q_share, k_share, v_share):
        columns = slice(at_column, at_column + share_ref.shape[1])
        at_column += share_ref.shape[1]
        total = wdst[0, :, columns].astype(F32)
        for i in range(1, half):
            total = total + wdst[i, :, columns].astype(F32)
        share_ref[...] = total

    def finish(off, _):
        peer = lax.rem(me + off, groups)
        copy = pcopy(result.at[:, peer], back_out.at[peer], os.at[peer], orr.at[peer], peer)
        copy.wait_recv()
        copy.wait_send()
        for t in range(tiles):
            copy = pcopy(dx.at[t, peer], back_dx.at[peer, t], xs.at[t, peer], xr.at[t, peer], peer)
            copy.wait_recv()
            copy.wait_send()
        return 0

    lax.fori_loop(1, groups, finish, 0)
    pltpu.make_async_copy(result.at[:, me], back_out.at[me], own.at[0]).wait()
    for t in range(tiles):
        pltpu.make_async_copy(dx.at[t, me], back_dx.at[me, t], own.at[1 + t]).wait()
        others(lambda other: line_copy(t, z, other).wait_send())
    others(lambda other: width_copy(z, other).wait_send())

    def drain(c, _):
        for d, buf in ((0, right), (1, left)):
            for b in range(n):

                @pl.when((b > z) if d == 0 else (b < z))
                def _():
                    rcopy(at(buf, c, b), at(buf, c, b), ss.at[d, b, c], rs.at[d, b, c], z).wait_send()

        return 0

    lax.fori_loop(0, count, drain, 0)


def deal_out(n, groups, tiles, x, dh, scale1, gain1, result, gain2, normed, *attention, chunk=64, lag=2):
    rows, w = x.shape
    width = n * w
    sub = rows // tiles // groups
    count = rows // chunk
    cols = width // groups
    joined = sum(a.shape[1] for a in attention[1:4])
    narrow = attention[2].shape[1]
    both = attention[8].shape[1] + joined
    dma = pltpu.SemaphoreType.DMA
    dealt = (groups, tiles, sub, w)
    return pl.pallas_call(
        functools.partial(deal_out_kernel, n, groups, tiles, chunk, lag),
        out_shape=[
            jax.ShapeDtypeStruct(dealt, BF),
            jax.ShapeDtypeStruct(dealt, BF),
            jax.ShapeDtypeStruct((16, cols), F32),
            jax.ShapeDtypeStruct((cols, attention[8].shape[1]), F32),
            *(jax.ShapeDtypeStruct((cols, a.shape[1]), F32) for a in attention[1:4]),
        ],
        in_specs=[VM] * 6 + [ANY] + [VM] * 15,
        out_specs=[VM] * 7,
        scratch_shapes=[
            pltpu.VMEM((rows, width), BF),
            pltpu.VMEM((rows, joined), BF),
            pltpu.VMEM((rows, narrow), F32),
            pltpu.VMEM((rows, narrow), F32),
            pltpu.VMEM((rows, width), BF),
            pltpu.VMEM((rows, width), BF),
            pltpu.VMEM((rows, w), F32),
            pltpu.VMEM((tiles, groups, sub, w), BF),
            pltpu.VMEM((n, 8, rows), F32),
            pltpu.VMEM((n, 8, w), F32),
            pltpu.VMEM((groups, 16, cols), F32),
            pltpu.VMEM((groups, 16, cols), F32),
            pltpu.VMEM((width, both), BF),
            pltpu.VMEM((groups // 2, cols, both), BF),
            pltpu.VMEM((groups // 2, cols, both), BF),
            pltpu.VMEM(normed.shape, BF),
            dma((2, n, count)),
            dma((2, n, count)),
            dma((groups,)),
            dma((groups,)),
            dma((tiles, groups)),
            dma((tiles, groups)),
            dma((n, tiles)),
            dma((n, tiles)),
            dma((n,)),
            dma((n,)),
            dma((groups,)),
            dma((groups,)),
            dma((2, groups // 2)),
            dma((2, groups // 2)),
            dma((2, groups // 2)),
            dma((2, groups // 2)),
            dma((tiles + 3,)),
        ],
        compiler_params=pltpu.CompilerParams(collective_id=5, has_side_effects=True, vmem_limit_bytes=62 << 20),
    )(x, dh, scale1, gain1, result.reshape(tiles, groups, sub, w), gain2, normed, *attention)


def rotary_tables(token_positions, head_size):
    half = head_size // 2
    freqs = rope_base ** (-(jnp.arange(half).astype(jnp.float32) * 2.0) / head_size)
    angles = token_positions.astype(jnp.float32)[:, None] * freqs[None, :]
    angles = jnp.concatenate([angles, angles], axis=1)
    return (jnp.cos(angles), jnp.sin(angles))


def matmul(left, right):
    return jnp.dot(left, right, preferred_element_type=jnp.float32)


def per_device(
    tokens,
    cotangent,
    first_gain,
    query_weight,
    key_matrix,
    value_matrix,
    output_weight,
    second_gain,
    gate_weight,
    up_weight,
    down_weight,
    seq_lengths,
    owner_order,
    skip_mask,
):
    groups = lax.axis_size("dp")
    member = lax.axis_index("dp")
    width_part = tokens.shape[1]
    row_count = tokens.shape[0]
    per_owner = row_count // groups
    seq_count = seq_lengths.shape[0]
    seq_index = jnp.arange(seq_count, dtype=jnp.int32)
    before = (seq_index[None, :] < seq_index[:, None]).astype(jnp.int32)
    unit_lengths = seq_lengths // groups
    unit_starts = jnp.sum(before * unit_lengths[None, :], axis=1)
    placed = (owner_order[:, None] == seq_index[None, :]).astype(jnp.int32)
    order_lengths = jnp.sum(placed * unit_lengths[None, :], axis=1)
    order_starts = jnp.sum(placed * unit_starts[None, :], axis=1)
    order_keep = jnp.sum(placed * skip_mask[None, :], axis=1)
    order_before = jnp.sum(before * order_lengths[None, :], axis=1)
    places = jnp.arange(row_count, dtype=jnp.int32)
    covers = (
        (places[:, None] >= order_before[None, :])
        & (places[:, None] < (order_before + order_lengths)[None, :])
    ).astype(jnp.int32)
    send_rows = places + jnp.sum(covers * (order_starts - order_before)[None, :], axis=1)
    given_before = jnp.sum(placed * order_before[:, None], axis=0)
    given_covers = (
        (places[:, None] >= unit_starts[None, :])
        & (places[:, None] < (unit_starts + unit_lengths)[None, :])
    ).astype(jnp.int32)
    slot_of = places + jnp.sum(given_covers * (given_before - unit_starts)[None, :], axis=1)
    my_places = member * per_owner + jnp.arange(per_owner, dtype=jnp.int32)
    my_covers = (
        (my_places[:, None] >= order_before[None, :])
        & (my_places[:, None] < (order_before + order_lengths)[None, :])
    ).astype(jnp.int32)
    slot_seq = jnp.sum(my_covers * seq_index[None, :], axis=1)
    slot_step = my_places - jnp.sum(my_covers * order_before[None, :], axis=1)
    slot_keep = jnp.sum(my_covers * order_keep[None, :], axis=1)
    tiles = max(1, per_owner // 32)
    sources = jnp.arange(groups, dtype=jnp.int32)[None, :, None]

    def spread(values):
        values = values.reshape(tiles, 1, per_owner // tiles)
        return jnp.broadcast_to(values, (tiles, groups, per_owner // tiles)).reshape(row_count)

    token_positions = (
        sources + groups * slot_step.reshape(tiles, 1, per_owner // tiles)
    ).reshape(row_count)
    lowest = spread(slot_seq) * row_count
    code = lowest + token_positions
    keep_rows = spread(slot_keep).reshape(row_count, 1).astype(jnp.float32)
    chosen = (send_rows[:, None] == places[None, :]).astype(jnp.bfloat16)
    put_back = (slot_of[:, None] == places[None, :]).astype(jnp.bfloat16)

    tensor_count = lax.axis_size("tensor")
    tensor_member = lax.axis_index("tensor")
    dealt_shape = (groups, tiles, per_owner // tiles, width_part)
    cosine, sine = rotary_tables(token_positions, HEAD_WIDTH)
    half = HEAD_WIDTH // 2
    tables = (
        cosine,
        jnp.concatenate([-sine[:, :half], sine[:, half:]], axis=1),
        code[None, :],
        code[:, None],
        lowest[:, None],
    )
    weights = (query_weight, key_matrix, value_matrix, output_weight)
    dealt_tokens, dealt_cotangent = (
        matmul(chosen, values).astype(BF).reshape(dealt_shape) for values in (tokens, cotangent)
    )
    owned_tokens, part_cotangent, part_tokens, attn_part, normed_one, *kept, scale_one = deal_in(
        tensor_count,
        groups,
        dealt_tokens,
        dealt_cotangent,
        first_gain[None, :],
        weights,
        tables,
    )
    owned_tokens = owned_tokens.reshape(row_count, -1)
    part_cotangent = part_cotangent.reshape(row_count, width_part)

    def my_part(values):
        return lax.dynamic_slice_in_dim(values, tensor_member * width_part, width_part, 1)

    result, attn_sum, owned_cotangent, normed_two, inner_low, both, second_term = middle(
        tensor_count,
        attn_part,
        owned_tokens,
        part_cotangent,
        keep_rows,
        second_gain[None, :],
        gate_weight,
        up_weight,
        down_weight,
    )
    hidden = gate_weight.shape[1]

    def shared(values):
        return lax.psum_scatter(
            values.astype(jnp.bfloat16), "dp", scatter_dimension=0, tiled=True
        )

    both_grad = matmul(normed_two.T, both).astype(BF)
    second_term, both_grad = lax.optimization_barrier((second_term, both_grad))
    both_share = shared(both_grad)
    grad_attn, grad_res, second_gain_grad, down_grad = second_back_of(
        tensor_count,
        second_term,
        owned_tokens,
        attn_sum,
        owned_cotangent,
        keep_rows,
        second_gain[None, :],
        inner_low,
    )
    both_share, down_grad, grad_attn = lax.optimization_barrier(
        (both_share, down_grad, grad_attn)
    )
    down_share = shared(down_grad)
    back_out, back_grad, gains, o_share, q_share, k_share, v_share = deal_out(
        tensor_count,
        groups,
        tiles,
        part_tokens.reshape(row_count, width_part),
        grad_res,
        scale_one,
        first_gain.reshape(tensor_count, width_part),
        result,
        second_gain_grad,
        normed_one,
        grad_attn,
        *weights,
        *kept,
        *tables,
    )
    down_share, back_out = lax.optimization_barrier((down_share, back_out))
    layer_output = matmul(put_back, back_out.reshape(row_count, width_part)).astype(BF)
    input_grad = matmul(put_back, back_grad.reshape(row_count, width_part)).astype(BF)
    summed = (
        gains[0],
        q_share,
        k_share,
        v_share,
        o_share.T,
        both_share[:, :hidden].astype(F32),
        both_share[:, hidden:].astype(F32),
        down_share.T.astype(F32),
        gains[8],
    )
    return (
        layer_output,
        input_grad,
        summed[0],
        summed[1],
        summed[2],
        summed[3],
        summed[4],
        summed[8],
        summed[5],
        summed[6],
        summed[7],
    )


def solution(mesh):
    placed = (
        P(None, ("dp", "tensor")),
        P(None, ("dp", "tensor")),
        P(),
        P(None, "tensor"),
        P(None, "tensor"),
        P(None, "tensor"),
        P("tensor", None),
        P(),
        P(None, "tensor"),
        P(None, "tensor"),
        P("tensor", None),
        P(),
        P(),
        P(),
    )
    return jax.shard_map(
        per_device,
        mesh=mesh,
        in_specs=placed,
        out_specs=(
            P(None, ("dp", "tensor")),
            P(None, ("dp", "tensor")),
            P("dp"),
            P("dp", "tensor"),
            P("dp", "tensor"),
            P("dp", "tensor"),
            P("tensor", "dp"),
            P("dp"),
            P("dp", "tensor"),
            P("dp", "tensor"),
            P("tensor", "dp"),
        ),
        check_vma=False,
    )
```

```python
import functools
import math

import jax
import jax.numpy as jnp
from jax import lax
from jax.experimental import pallas as pl
from jax.experimental.pallas import tpu as pltpu
from jax.sharding import PartitionSpec as P

HEAD_WIDTH = 128

MESH = pl.DeviceIdType.MESH
VM = pl.BlockSpec(memory_space=pltpu.VMEM)
F32 = jnp.float32
BF = jnp.bfloat16

def neighbour_barrier(z, n, axis):
    barrier = pltpu.get_barrier_semaphore()
    @pl.when(z > 0)
    def _():
        pl.semaphore_signal(barrier, inc=1, device_id={axis: z - 1}, device_id_type=MESH)
    @pl.when(z < n - 1)
    def _():
        pl.semaphore_signal(barrier, inc=1, device_id={axis: z + 1}, device_id_type=MESH)
    ends = jnp.where(z > 0, 1, 0) + jnp.where(z < n - 1, 1, 0)
    pl.semaphore_wait(barrier, ends)

def rcopy(src, dst, ss, rs, dev):
    return pltpu.make_async_remote_copy(src_ref=src, dst_ref=dst, send_sem=ss, recv_sem=rs, device_id={"tensor": dev}, device_id_type=MESH)


eps = 1e-05
rope_base = 10000.0


def nt(left, right):
    return lax.dot_general(left, right, (((1,), (1,)), ((), ())), preferred_element_type=F32)


def tn(left, right):
    return lax.dot_general(left, right, (((0,), (0,)), ((), ())), preferred_element_type=F32)


def mm(left, right):
    return jnp.dot(left, right, preferred_element_type=F32)


def spin(values, cosine, signed_sine):
    return values * cosine + pltpu.roll(values, HEAD_WIDTH // 2, 1) * signed_sine


def visible(code_row, code_col, low_col):
    return jnp.where((code_row <= code_col) & (code_row >= low_col), 0.0, -1e30)


def attend_tile(t, tiles, xt, gain, wq, wk, wv, wo, cosine, sine, code_row, code_col, low_col,
                part, normed, q, k, v, o, lse, scales):
    rows = normed.shape[0]
    tile = rows // tiles
    heads = wq.shape[1] // HEAD_WIDTH
    kv = wk.shape[1] // HEAD_WIDTH
    group = heads // kv
    factor = math.log2(math.e) / math.sqrt(HEAD_WIDTH)
    r = pl.ds(t * tile, tile)
    xt = xt.astype(F32)
    scale = lax.rsqrt(jnp.mean(xt * xt, axis=1, keepdims=True) + eps)
    scales[r, :] = scale
    n1 = (xt * scale * gain[...]).astype(BF)
    normed[r, :] = n1
    c, s = cosine[r, :], sine[r, :]
    pre = mm(n1, wq[...])
    for h in range(heads):
        cut = slice(h * HEAD_WIDTH, (h + 1) * HEAD_WIDTH)
        q[r, cut] = spin(pre[:, cut], c, s).astype(BF)
    pre = mm(n1, wk[...])
    for h in range(kv):
        cut = slice(h * HEAD_WIDTH, (h + 1) * HEAD_WIDTH)
        k[r, cut] = spin(pre[:, cut], c, s).astype(BF)
    v[r, :] = mm(n1, wv[...]).astype(BF)
    seen = (t + 1) * tile
    block = min(tile, 256)
    for at in range(t * tile, (t + 1) * tile, block):
        r = pl.ds(at, block)
        bias = visible(code_row[:, :seen], code_col[r, :], low_col[r, :])
        logs = []
        for h in range(heads):
            cut = slice(h * HEAD_WIDTH, (h + 1) * HEAD_WIDTH)
            mine = slice(h // group * HEAD_WIDTH, (h // group + 1) * HEAD_WIDTH)
            scores = nt(q[r, cut], k[:seen, mine]) * factor + bias
            top = jnp.max(scores, axis=1, keepdims=True)
            expo = jnp.exp2(scores - top)
            total = jnp.sum(expo, axis=1, keepdims=True)
            probs = (expo * (1.0 / total)).astype(BF)
            o[r, cut] = mm(probs, v[:seen, mine]).astype(BF)
            logs.append(top + jnp.log2(total))
        lse[r, :] = jnp.concatenate(logs, axis=1)
        part[r, :] = mm(o[r, :], wo[...]).astype(BF)


def attend_back_tile(t, tiles, ga, wq, wk, wv, wo, q, k, v, o, lse, cosine, sine, code_row, code_col, low_col,
                     part, dqkv, dk, dv):
    rows = ga.shape[0]
    tile = rows // tiles
    heads = wq.shape[1] // HEAD_WIDTH
    kv = wk.shape[1] // HEAD_WIDTH
    group = heads // kv
    wide = heads * HEAD_WIDTH
    narrow = kv * HEAD_WIDTH
    score_scale = 1.0 / math.sqrt(HEAD_WIDTH)
    factor = math.log2(math.e) / math.sqrt(HEAD_WIDTH)
    seen = (t + 1) * tile
    block = min(tile, 256)
    for at in range(t * tile, (t + 1) * tile, block):
        r = pl.ds(at, block)
        do = nt(ga[r, :], wo[...]).astype(BF)
        c, s = cosine[r, :], sine[r, :]
        bias = visible(code_row[:, :seen], code_col[r, :], low_col[r, :])
        logs = lse[r, :]
        for h in range(heads):
            cut = slice(h * HEAD_WIDTH, (h + 1) * HEAD_WIDTH)
            mine = slice(h // group * HEAD_WIDTH, (h // group + 1) * HEAD_WIDTH)
            do_h = do[:, cut]
            qh = q[r, cut]
            probs = jnp.exp2(nt(qh, k[:seen, mine]) * factor + bias - logs[:, h : h + 1])
            along = jnp.sum(do_h.astype(F32) * o[r, cut].astype(F32), axis=1, keepdims=True)
            ds = (probs * (nt(do_h, v[:seen, mine]) - along)).astype(BF)
            pb = probs.astype(BF)
            dq = mm(ds, k[:seen, mine]) * score_scale
            dqkv[r, cut] = spin(dq, c, -s).astype(BF)
            more_k = tn(ds, qh)
            more_v = tn(pb, do_h)
            if t == tiles - 1 and at == t * tile and h % group == 0:
                dk[:seen, mine] = more_k
                dv[:seen, mine] = more_v
            else:
                dk[:seen, mine] += more_k
                dv[:seen, mine] += more_v
    for at in range(t * tile, (t + 1) * tile, block):
        r = pl.ds(at, block)
        c, s = cosine[r, :], sine[r, :]
        for h in range(kv):
            cut = slice(h * HEAD_WIDTH, (h + 1) * HEAD_WIDTH)
            low = wide + h * HEAD_WIDTH
            dqkv[r, low : low + HEAD_WIDTH] = spin(dk[r, cut] * score_scale, c, -s).astype(BF)
        dqkv[r, wide + narrow :] = dv[r, :].astype(BF)
        part[r, :] = (
            nt(dqkv[r, :wide], wq[...])
            + nt(dqkv[r, wide : wide + narrow], wk[...])
            + nt(dqkv[r, wide + narrow :], wv[...])
        ).astype(BF)


ANY = pl.BlockSpec(memory_space=pl.ANY)
LAG = 2
CHUNK = 32
BLOCK = 128


def line_row(f, c):
    per = BLOCK // CHUNK
    return pl.ds(pl.multiple_of(lax.div(c, per) * (2 * BLOCK) + f * BLOCK + lax.rem(c, per) * CHUNK, CHUNK), CHUNK)


def line_steps(n, rows):
    return rows // 2 // CHUNK + 2 * LAG * (n - 1)


def line_sum_step(n, z, t, part, up, out, sems):
    us, ur, ds, dr = sems
    count = part.shape[0] // 2 // CHUNK
    for f in range(2):
        p = z if f == 0 else n - 1 - z
        step = 1 if f == 0 else -1
        c = t - LAG * p

        @pl.when((c >= 0) & (c < count))
        def _():
            r = line_row(f, c)

            @pl.when(p == 0)
            def _():
                rcopy(part.at[r], up.at[r], us.at[f, c], ur.at[f, c], z + step).start()

            @pl.when(p > 0)
            def _():
                rcopy(up.at[r], up.at[r], us.at[f, c], ur.at[f, c], z).wait_recv()
                s = (part[r, :].astype(F32) + up[r, :].astype(F32)).astype(BF)

                @pl.when(p < n - 1)
                def _():
                    up[r, :] = s
                    rcopy(up.at[r], up.at[r], us.at[f, c], ur.at[f, c], z + step).start()

                @pl.when(p == n - 1)
                def _():
                    out[r, :] = s
                    rcopy(out.at[r], out.at[r], ds.at[f, c], dr.at[f, c], z - step).start()

    for f in range(2):
        p = z if f == 0 else n - 1 - z
        step = 1 if f == 0 else -1
        c = t - LAG * (2 * (n - 1) - p)

        @pl.when((c >= 0) & (c < count) & (p < n - 1))
        def _():
            r = line_row(f, c)
            rcopy(out.at[r], out.at[r], ds.at[f, c], dr.at[f, c], z).wait_recv()

            @pl.when(p > 0)
            def _():
                rcopy(out.at[r], out.at[r], ds.at[f, c], dr.at[f, c], z - step).start()


def line_sum_drain(n, z, part, up, out, sems):
    us, ur, ds, dr = sems
    count = part.shape[0] // 2 // CHUNK

    def drain(c, _):
        for f in range(2):
            p = z if f == 0 else n - 1 - z
            r = line_row(f, c)

            @pl.when(p < n - 1)
            def _():
                rcopy(up.at[r], up.at[r], us.at[f, c], ur.at[f, c], z).wait_send()

            @pl.when(p > 0)
            def _():
                rcopy(out.at[r], out.at[r], ds.at[f, c], dr.at[f, c], z).wait_send()

        return 0

    lax.fori_loop(0, count, drain, 0)


def line_sum_sems(rows):
    return [pltpu.SemaphoreType.DMA((2, rows // 2 // CHUNK))] * 4


def gather_cut(ref, o, c, w):
    return ref.at[pl.ds(pl.multiple_of(c * BLOCK, BLOCK), BLOCK), pl.ds(pl.multiple_of(o * w, w), w)]


def line_gather_step(n, z, t, src, out, ss, rs):
    rows, w = src.shape
    count = rows // BLOCK

    @pl.when(t < count)
    def _():
        mine = src.at[pl.ds(pl.multiple_of(t * BLOCK, BLOCK), BLOCK)]

        @pl.when(z < n - 1)
        def _():
            rcopy(mine, gather_cut(out, z, t, w), ss.at[0, z, t], rs.at[0, z, t], z + 1).start()

        @pl.when(z > 0)
        def _():
            rcopy(mine, gather_cut(out, z, t, w), ss.at[1, z, t], rs.at[1, z, t], z - 1).start()

    for hop in range(1, n):
        c = t - hop
        for d, step in ((0, 1), (1, -1)):
            o = z - hop * step

            @pl.when((c >= 0) & (c < count) & (o >= 0) & (o < n))
            def _():
                cut = gather_cut(out, o, c, w)
                rcopy(cut, cut, ss.at[d, o, c], rs.at[d, o, c], z).wait_recv()
                after = z + step

                @pl.when((after >= 0) & (after < n))
                def _():
                    rcopy(cut, cut, ss.at[d, o, c], rs.at[d, o, c], after).start()


def line_gather_drain(n, z, src, out, ss, rs):
    rows, w = src.shape

    def drain(c, _):
        for d in range(2):
            for o in range(n):
                on = (o <= z) & (z < n - 1) if d == 0 else (o >= z) & (z > 0)

                @pl.when(on)
                def _():
                    cut = gather_cut(out, o, c, w)
                    rcopy(cut, cut, ss.at[d, o, c], rs.at[d, o, c], z).wait_send()

        return 0

    lax.fori_loop(0, rows // BLOCK, drain, 0)


def middle_kernel(n, part, x_far, g_part, keep, gain, wg_far, wu_far, wd_far,
                  result, a_far, g_far, n2_far, inner_far, both_far, dn2_far,
                  wg, wu, wd, x, up, total, g, right, left, gate_s, upper_s, n2_s, inner_s, both_s, f_s, dn2_s,
                  us, ur, ds, dr, ss, rs, fs, fr, load, own, save, late):
    z = lax.axis_index("tensor")
    rows, width = part.shape
    w = g_part.shape[1]
    hidden = wg.shape[1]
    tile = 2 * BLOCK
    sums = (us, ur, ds, dr)
    loads = [pltpu.make_async_copy(a, b, load.at[i]) for i, (a, b) in enumerate(((x_far, x), (wg_far, wg), (wu_far, wu), (wd_far, wd)))]
    for copy in loads:
        copy.start()
    mine = pltpu.make_async_copy(g_part, g.at[:, pl.ds(pl.multiple_of(z * w, w), w)], own)
    mine.start()
    neighbour_barrier(z, n, "tensor")

    def saves(d):
        r = pl.ds(pl.multiple_of(d * tile, tile), tile)
        pairs = ((n2_s, n2_far), (inner_s, inner_far), (both_s, both_far), (dn2_s, dn2_far))
        return [pltpu.make_async_copy(a, b.at[r], save.at[i]) for i, (a, b) in enumerate(pairs)]

    first = BLOCK // CHUNK - 1 + 2 * LAG * (n - 1)

    def body(t, _):
        line_sum_step(n, z, t, part, up, total, sums)

        @pl.when(lax.rem(t, 2) == 0)
        def _():
            line_gather_step(n, z, lax.div(t, 2), g_part, g, ss, rs)

        q = t - first
        d = lax.div(jnp.maximum(q, 0), 4)
        k = lax.rem(jnp.maximum(q, 0), 4)
        r = pl.ds(pl.multiple_of(d * tile, tile), tile)

        @pl.when((q >= 0) & (d < rows // tile) & (k == 0))
        def _():
            @pl.when(d == 0)
            def _():
                for copy in loads:
                    copy.wait()
                mine.wait()

            @pl.when(d > 0)
            def _():
                for copy in saves(d - 1):
                    copy.wait()

            h = x[r, :].astype(F32) + keep[r, :] * total[r, :].astype(F32)
            scale = lax.rsqrt(jnp.mean(h * h, axis=1, keepdims=True) + eps)
            n2_s[...] = (h * scale * gain[...]).astype(BF)
            gate_s[...] = mm(n2_s[...], wg[...])

        @pl.when((q >= 0) & (d < rows // tile) & (k == 1))
        def _():
            upper_s[...] = mm(n2_s[...], wu[...])
            gate = gate_s[...]
            inner_s[...] = (gate * jax.nn.sigmoid(gate) * upper_s[...]).astype(BF)

        @pl.when((q >= 0) & (d < rows // tile) & (k == 2))
        def _():
            f_s[lax.rem(d, 2)] = mm(inner_s[...], wd[...]).astype(BF)
            gf = (keep[r, :] * g[r, :].astype(F32)).astype(BF)
            back = nt(gf, wd[...])
            gate = gate_s[...]
            s = jax.nn.sigmoid(gate)
            both_s[:, :hidden] = (back * upper_s[...] * s * (1.0 + gate * (1.0 - s))).astype(BF)
            both_s[:, hidden:] = (back * (gate * s)).astype(BF)

        @pl.when((q >= 0) & (d < rows // tile) & (k == 3))
        def _():
            dn2_s[...] = (nt(both_s[:, :hidden], wg[...]) + nt(both_s[:, hidden:], wu[...])).astype(BF)
            for copy in saves(d):
                copy.start()

        scatter_step(t - first - 2)
        return 0

    chunk = tile // 4
    count = rows // chunk

    def at(ref, c, b):
        return ref.at[pl.ds(pl.multiple_of(c * chunk, chunk), chunk), pl.ds(b * w, w)]

    def scatter_copy(buf, d, c, b, to):
        return rcopy(at(buf, c, b), at(buf, c, b), fs.at[d, b, c], fr.at[d, b, c], to)

    def scatter_step(s):
        for d, buf, step in ((0, right, 1), (1, left, -1)):
            p = z if d == 0 else n - 1 - z
            c = s - p

            @pl.when((c >= 0) & (c < count))
            def _():
                r = pl.ds(pl.multiple_of(c * chunk, chunk), chunk)
                slot = lax.rem(lax.div(c, 4), 2)
                inner = pl.ds(pl.multiple_of(lax.rem(c, 4) * chunk, chunk), chunk)
                for b in range(n - 1, 0, -1) if d == 0 else range(n - 1):
                    k = pl.ds(b * w, w)

                    @pl.when((b > z) if d == 0 else (b < z))
                    def _():
                        @pl.when(p == 0)
                        def _():
                            buf[r, k] = f_s[slot, inner, k]

                        @pl.when(p > 0)
                        def _():
                            scatter_copy(buf, d, c, b, z).wait_recv()
                            buf[r, k] = (f_s[slot, inner, k].astype(F32) + buf[r, k].astype(F32)).astype(BF)

                        scatter_copy(buf, d, c, b, z + step).start()

        c = s - (n - 1)

        @pl.when((c >= 0) & (c < count))
        def _():
            r = pl.ds(pl.multiple_of(c * chunk, chunk), chunk)
            slot = lax.rem(lax.div(c, 4), 2)
            inner = pl.ds(pl.multiple_of(lax.rem(c, 4) * chunk, chunk), chunk)
            for b in range(n):
                k = pl.ds(b * w, w)

                @pl.when(z == b)
                def _():
                    f = f_s[slot, inner, k].astype(F32)
                    if b > 0:
                        scatter_copy(right, 0, c, b, z).wait_recv()
                        f = f + right[r, k].astype(F32)
                    if b < n - 1:
                        scatter_copy(left, 1, c, b, z).wait_recv()
                        f = f + left[r, k].astype(F32)
                    kept = keep[r, :]
                    h = x[r, k].astype(F32) + kept * total[r, k].astype(F32)
                    result[r, :] = (h + kept * f).astype(BF)

    lax.fori_loop(0, first + 2 + count + n, body, 0)

    def drain(c, _):
        for d, buf in ((0, right), (1, left)):
            for b in range(n):

                @pl.when((b > z) if d == 0 else (b < z))
                def _():
                    scatter_copy(buf, d, c, b, z).wait_send()

        return 0

    lax.fori_loop(0, count, drain, 0)
    ends = [pltpu.make_async_copy(a, b, late.at[i]) for i, (a, b) in enumerate(((total, a_far), (g, g_far)))]
    for copy in ends:
        copy.start()
    line_sum_drain(n, z, part, up, total, sums)
    line_gather_drain(n, z, g_part, g, ss, rs)
    for copy in saves(rows // tile - 1) + ends:
        copy.wait()


def middle(n, part, x, g_part, keep, gain, wg, wu, wd):
    rows, width = part.shape
    hidden = wg.shape[1]
    tile = 2 * BLOCK
    blocks = rows // BLOCK
    w = g_part.shape[1]
    widths = (w, width, width, width, hidden, 2 * hidden, width)
    return pl.pallas_call(
        functools.partial(middle_kernel, n),
        out_shape=[jax.ShapeDtypeStruct((rows, k), BF) for k in widths],
        in_specs=[VM, ANY] + [VM] * 3 + [ANY] * 3,
        out_specs=[VM] + [ANY] * 6,
        scratch_shapes=[
            pltpu.VMEM(wg.shape, BF),
            pltpu.VMEM(wu.shape, BF),
            pltpu.VMEM(wd.shape, BF),
            pltpu.VMEM((rows, width), BF),
            pltpu.VMEM((rows, width), BF),
            pltpu.VMEM((rows, width), BF),
            pltpu.VMEM((rows, width), BF),
            pltpu.VMEM((rows, width), BF),
            pltpu.VMEM((rows, width), BF),
            pltpu.VMEM((tile, hidden), F32),
            pltpu.VMEM((tile, hidden), F32),
            pltpu.VMEM((tile, width), BF),
            pltpu.VMEM((tile, hidden), BF),
            pltpu.VMEM((tile, 2 * hidden), BF),
            pltpu.VMEM((2, tile, width), BF),
            pltpu.VMEM((tile, width), BF),
            *line_sum_sems(rows),
            pltpu.SemaphoreType.DMA((2, n, blocks)),
            pltpu.SemaphoreType.DMA((2, n, blocks)),
            pltpu.SemaphoreType.DMA((2, n, rows // tile * 4)),
            pltpu.SemaphoreType.DMA((2, n, rows // tile * 4)),
            pltpu.SemaphoreType.DMA((4,)),
            pltpu.SemaphoreType.DMA,
            pltpu.SemaphoreType.DMA((4,)),
            pltpu.SemaphoreType.DMA((2,)),
        ],
        compiler_params=pltpu.CompilerParams(collective_id=3, has_side_effects=True, vmem_limit_bytes=63 << 20),
    )(part, x, g_part, keep, gain, wg, wu, wd)


def second_back_kernel(n, part, x_far, a_far, g_far, keep, gain, inner_far, ga, dh, gain_grad, grad_far,
                       up, total, x, a, g, inner, stage, us, ur, ds, dr, load, save):
    z = lax.axis_index("tensor")
    rows, width = part.shape
    w = dh.shape[1]
    piece = BLOCK // 2
    sums = (us, ur, ds, dr)
    pairs = ((g_far, g), (inner_far, inner), (x_far, x), (a_far, a))
    loads = [pltpu.make_async_copy(far, near, load.at[i]) for i, (far, near) in enumerate(pairs)]
    for copy in loads:
        copy.start()
    neighbour_barrier(z, n, "tensor")
    span = stage.shape[1]
    spans = width // span

    def saved(j):
        slot = lax.rem(j, 2)
        return pltpu.make_async_copy(stage.at[slot], grad_far.at[pl.ds(pl.multiple_of(j * span, span), span)], save.at[slot])

    gain_grad[...] = jnp.zeros_like(gain_grad)
    first = BLOCK // CHUNK - 1 + 2 * LAG * (n - 1)

    def body(t, _):
        line_sum_step(n, z, t, part, up, total, sums)
        j = t - 3

        @pl.when((j >= 0) & (j < spans))
        def _():
            @pl.when(j == 0)
            def _():
                for copy in loads:
                    copy.wait()

            @pl.when(j >= 2)
            def _():
                saved(j - 2).wait()

            cut = pl.ds(pl.multiple_of(j * span, span), span)
            gf = (keep[...] * g[:, cut].astype(F32)).astype(BF)
            stage[lax.rem(j, 2)] = tn(gf, inner[...]).astype(BF)
            saved(j).start()

        q = t - first

        @pl.when(q >= 0)
        def _():
            r = pl.ds(pl.multiple_of(q * piece, piece), piece)
            h = x[r, :].astype(F32) + keep[r, :] * a[r, :].astype(F32)
            scale = lax.rsqrt(jnp.mean(h * h, axis=1, keepdims=True) + eps)
            back = total[r, :].astype(F32)
            gain_grad[...] += jnp.sum(back * h * scale, axis=0, keepdims=True)
            e = back * gain[...]
            along = jnp.mean(e * h, axis=1, keepdims=True)
            full = g[r, :].astype(F32) + scale * e - h * (scale * scale * scale * along)
            ga[r, :] = (keep[r, :] * full).astype(BF)
            for b in range(n):

                @pl.when(z == b)
                def _():
                    dh[r, :] = full[:, b * w : (b + 1) * w]

        return 0

    lax.fori_loop(0, first + rows // piece, body, 0)
    line_sum_drain(n, z, part, up, total, sums)
    for j in range(spans - 2, spans):
        saved(j).wait()


def second_back_of(n, part, x, a, g, keep, gain, inner):
    rows, width = part.shape
    return pl.pallas_call(
        functools.partial(second_back_kernel, n),
        out_shape=[
            jax.ShapeDtypeStruct((rows, width), BF),
            jax.ShapeDtypeStruct((rows, width // n), F32),
            jax.ShapeDtypeStruct((1, width), F32),
            jax.ShapeDtypeStruct((width, inner.shape[1]), BF),
        ],
        in_specs=[VM] + [ANY] * 3 + [VM] * 2 + [ANY],
        out_specs=[VM] * 3 + [ANY],
        scratch_shapes=[
            pltpu.VMEM((rows, width), BF),
            pltpu.VMEM((rows, width), BF),
            *(pltpu.VMEM((rows, width), BF) for _ in range(3)),
            pltpu.VMEM(inner.shape, BF),
            pltpu.VMEM((2, 256, inner.shape[1]), BF),
            *line_sum_sems(rows),
            pltpu.SemaphoreType.DMA((4,)),
            pltpu.SemaphoreType.DMA((2,)),
        ],
        compiler_params=pltpu.CompilerParams(collective_id=4, has_side_effects=True, vmem_limit_bytes=60 << 20),
    )(part, x, a, g, keep, gain, inner)


def peers_barrier(z, n, me, groups, everyone):
    barrier = pltpu.get_barrier_semaphore()

    def greet(off, _):
        peer = lax.rem(me + off, groups)
        pl.semaphore_signal(barrier, inc=1, device_id={"dp": peer}, device_id_type=MESH)
        return 0

    lax.fori_loop(1, groups, greet, 0)
    if everyone:
        for off in range(1, n):
            other = lax.rem(z + off, n)
            pl.semaphore_signal(barrier, inc=1, device_id={"tensor": other}, device_id_type=MESH)
        pl.semaphore_wait(barrier, groups - 1 + n - 1)
    else:

        @pl.when(z > 0)
        def _():
            pl.semaphore_signal(barrier, inc=1, device_id={"tensor": z - 1}, device_id_type=MESH)

        @pl.when(z < n - 1)
        def _():
            pl.semaphore_signal(barrier, inc=1, device_id={"tensor": z + 1}, device_id_type=MESH)

        ends = jnp.where(z > 0, 1, 0) + jnp.where(z < n - 1, 1, 0)
        pl.semaphore_wait(barrier, groups - 1 + ends)


def pcopy(src, dst, ss, rs, peer):
    return pltpu.make_async_remote_copy(
        src_ref=src, dst_ref=dst, send_sem=ss, recv_sem=rs, device_id={"dp": peer}, device_id_type=MESH
    )


def deal_in_kernel(n, groups, dealt_x, dealt_g, gain, cosine, sine, code_row, code_col, low_col, *refs):
    far, (full, g_part, x_part), results = refs[:4], refs[4:7], refs[7:15]
    near, (xs, xr, gs, gr, ss, rs, own, load) = refs[15:19], refs[19:]
    loads = [pltpu.make_async_copy(a, b, load.at[i]) for i, (a, b) in enumerate(zip(far, near))]
    for copy in loads:
        copy.start()
    z = lax.axis_index("tensor")
    me = lax.axis_index("dp")
    tiles, sub, w = dealt_x.shape[1:]
    cols = pl.ds(pl.multiple_of(z * w, w), w)

    def place(t, i):
        return full.at[t, i, :, cols]

    for t in range(tiles):
        pltpu.make_async_copy(dealt_x.at[me, t], place(t, me), own.at[t]).start()
    pltpu.make_async_copy(dealt_g.at[me], g_part.at[:, me], own.at[tiles]).start()
    peers_barrier(z, n, me, groups, False)

    def send(t):
        def one(off, _):
            peer = lax.rem(me + off, groups)
            pcopy(dealt_x.at[peer, t], place(t, me), xs.at[t, peer], xr.at[t, me], peer).start()
            return 0

        lax.fori_loop(1, groups, one, 0)

    def cut(o, t):
        return full.at[t, :, :, pl.ds(pl.multiple_of(o * w, w), w)]

    for t in range(tiles):
        send(t)

    def send_g(off, _):
        peer = lax.rem(me + off, groups)
        pcopy(dealt_g.at[peer], g_part.at[:, me], gs.at[peer], gr.at[me], peer).start()
        return 0

    lax.fori_loop(1, groups, send_g, 0)
    for s in range(tiles + n - 1):
        if s < tiles:

            def got(off, _):
                peer = lax.rem(me + off, groups)
                pcopy(dealt_x.at[peer, s], place(s, peer), xs.at[s, peer], xr.at[s, peer], peer).wait_recv()
                return 0

            lax.fori_loop(1, groups, got, 0)
            pltpu.make_async_copy(dealt_x.at[me, s], place(s, me), own.at[s]).wait()

            @pl.when(z < n - 1)
            def _():
                rcopy(cut(z, s), cut(z, s), ss.at[0, z, s], rs.at[0, z, s], z + 1).start()

            @pl.when(z > 0)
            def _():
                rcopy(cut(z, s), cut(z, s), ss.at[1, z, s], rs.at[1, z, s], z - 1).start()

        for hop in range(1, n):
            c = s - hop
            if 0 <= c < tiles:
                for d, step in ((0, 1), (1, -1)):
                    o = z - hop * step

                    @pl.when((o >= 0) & (o < n))
                    def _():
                        rcopy(cut(o, c), cut(o, c), ss.at[d, o, c], rs.at[d, o, c], z).wait_recv()
                        after = z + step

                        @pl.when((after >= 0) & (after < n))
                        def _():
                            rcopy(cut(o, c), cut(o, c), ss.at[d, o, c], rs.at[d, o, c], after).start()

        if s == tiles - 1:
            pltpu.make_async_copy(full.at[:, :, :, cols], x_part, own.at[tiles + 1]).start()
        t = s - (n - 1)
        if t >= 0:
            if t == 0:
                for copy in loads:
                    copy.wait()
            attend_tile(
                t,
                tiles,
                full[t].reshape(groups * sub, n * w),
                gain,
                *near,
                cosine,
                sine,
                code_row,
                code_col,
                low_col,
                *results,
            )

    def finish(off, _):
        peer = lax.rem(me + off, groups)
        copy = pcopy(dealt_g.at[peer], g_part.at[:, peer], gs.at[peer], gr.at[peer], peer)
        copy.wait_recv()
        copy.wait_send()
        for t in range(tiles):
            pcopy(dealt_x.at[peer, t], place(t, peer), xs.at[t, peer], xr.at[t, peer], peer).wait_send()
        return 0

    lax.fori_loop(1, groups, finish, 0)
    pltpu.make_async_copy(dealt_g.at[me], g_part.at[:, me], own.at[tiles]).wait()
    pltpu.make_async_copy(full.at[:, :, :, cols], x_part, own.at[tiles + 1]).wait()
    for c in range(tiles):
        for d in range(2):
            for o in range(n):

                @pl.when((o <= z) & (z < n - 1) if d == 0 else (o >= z) & (z > 0))
                def _():
                    rcopy(cut(o, c), cut(o, c), ss.at[d, o, c], rs.at[d, o, c], z).wait_send()


def deal_in(n, groups, dealt_x, dealt_g, gain, weights, tables):
    tiles, sub, w = dealt_x.shape[1:]
    rows = tiles * groups * sub
    wq, wk, wv, wo = weights
    dma = pltpu.SemaphoreType.DMA
    widths = (n * w, n * w, wq.shape[1], wk.shape[1], wv.shape[1], wq.shape[1])
    return pl.pallas_call(
        functools.partial(deal_in_kernel, n, groups),
        out_shape=[
            jax.ShapeDtypeStruct((tiles, groups, sub, n * w), BF),
            jax.ShapeDtypeStruct((tiles, groups, sub, w), BF),
            jax.ShapeDtypeStruct((tiles, groups, sub, w), BF),
            *(jax.ShapeDtypeStruct((rows, k), BF) for k in widths),
            jax.ShapeDtypeStruct((rows, wq.shape[1] // HEAD_WIDTH), F32),
            jax.ShapeDtypeStruct((rows, 1), F32),
        ],
        in_specs=[VM] * 8 + [ANY] * 4,
        out_specs=[VM] * 11,
        scratch_shapes=[
            *(pltpu.VMEM(a.shape, BF) for a in weights),
            dma((tiles, groups)),
            dma((tiles, groups)),
            dma((groups,)),
            dma((groups,)),
            dma((2, n, tiles)),
            dma((2, n, tiles)),
            dma((tiles + 2,)),
            dma((4,)),
        ],
        compiler_params=pltpu.CompilerParams(collective_id=6, has_side_effects=True, vmem_limit_bytes=60 << 20),
    )(dealt_x, dealt_g, gain, *tables, *weights)


def exact(left, right, contract):
    return lax.dot_general(
        left, right, (contract, ((), ())), preferred_element_type=F32, precision=lax.Precision.HIGHEST
    )


def deal_out_kernel(n, groups, tiles, chunk, lag, x, dh, scale1, gain1, result, gain2, normed_far, *refs):
    attention = refs[:15]
    (back_out, back_dx, gains, o_share, q_share, k_share, v_share, part, dqkv, dk, dv, right, left, fb, dx, lines, widths, gsrc, gdst, wsrc, wdst, pair, normed,
     ss, rs, os, orr, xs, xr, ls, lr, ws, wr, es, er, qs, qr, ps, pr, own) = refs[15:]
    ga, o = attention[0], attention[8]
    z = lax.axis_index("tensor")
    me = lax.axis_index("dp")
    rows, w = x.shape
    tile = rows // tiles
    count = rows // chunk
    per = tile // chunk
    sub = result.shape[2]
    pltpu.make_async_copy(result.at[:, me], back_out.at[me], own.at[0]).start()
    fetch = pltpu.make_async_copy(normed_far, normed, own.at[2 + tiles])
    fetch.start()
    peers_barrier(z, n, me, groups, True)

    def send_out(off, _):
        peer = lax.rem(me + off, groups)
        pcopy(result.at[:, peer], back_out.at[me], os.at[peer], orr.at[me], peer).start()
        return 0

    lax.fori_loop(1, groups, send_out, 0)

    def chunk_rows(c):
        t = tiles - 1 - lax.div(c, per)
        return pl.ds(pl.multiple_of(t * tile + lax.rem(c, per) * chunk, chunk), chunk)

    def at(ref, c, b):
        return ref.at[chunk_rows(c), pl.ds(b * w, w)]

    widths[...] = jnp.zeros_like(widths)

    def others(f):
        for off in range(1, n):
            f(lax.rem(z + off, n))

    def line_copy(t, slot, other):
        cut = lines.at[slot, :, pl.ds(pl.multiple_of(t * tile, tile), tile)]
        return rcopy(cut, cut, ls.at[other, t], lr.at[slot, t], other)

    def width_copy(slot, other):
        cut = widths.at[slot]
        return rcopy(cut, cut, ws.at[other], wr.at[slot], other)

    def open_tile(t):
        r = pl.ds(pl.multiple_of(t * tile, tile), tile)
        e = fb[r, :] * gain1[pl.ds(z, 1), :]
        xt = x[r, :].astype(F32)
        lines[z, :, r] = exact(jnp.ones((8, w), F32), e * xt, ((1,), (1,)))
        others(lambda other: line_copy(t, z, other).start())
        grown = jnp.sum(fb[r, :] * xt * scale1[r, :], axis=0, keepdims=True)
        widths[z, :, :] += jnp.broadcast_to(grown, (8, w))

        @pl.when(t == 0)
        def _():
            others(lambda other: width_copy(z, other).start())

    def close_tile(t):
        r = pl.ds(pl.multiple_of(t * tile, tile), tile)
        others(lambda other: line_copy(t, other, other).wait_recv())
        total = lines[0, :, r]
        for j in range(1, n):
            total = total + lines[j, :, r]
        along = exact(total * (1.0 / (8 * n * w)), jnp.ones((8, w), F32), ((0,), (0,)))
        e = fb[r, :] * gain1[pl.ds(z, 1), :]
        s = scale1[r, :]
        full = dh[r, :] + s * e - x[r, :].astype(F32) * (s * s * s * along)
        dx[t] = full.astype(BF).reshape(groups, sub, w)
        pltpu.make_async_copy(dx.at[t, me], back_dx.at[me, t], own.at[1 + t]).start()

        def one(off, _):
            peer = lax.rem(me + off, groups)
            pcopy(dx.at[t, peer], back_dx.at[me, t], xs.at[t, peer], xr.at[t, me], peer).start()
            return 0

        lax.fori_loop(1, groups, one, 0)

    ow = o.shape[1]
    share = normed.shape[1] // groups
    span = max(share, 256)

    half = groups // 2
    seat = lax.div(me, 2)
    parity = lax.rem(me, 2)
    partner = me + 1 - 2 * parity

    def rows_of(owner):
        return pl.ds(pl.multiple_of(owner * share, share), share)

    def weight_copy(kind, src, dst, sems, to, slot, at_column, wide):
        columns = pl.ds(at_column, wide)
        return pltpu.make_async_remote_copy(
            src_ref=wsrc.at[rows_of(src), columns],
            dst_ref=dst.at[slot, :, columns],
            send_sem=sems[0].at[kind, lax.div(src, 2)],
            recv_sem=sems[1].at[kind, slot],
            device_id={"dp": to},
            device_id_type=MESH,
        )

    def weigh(left_ref, right_ref, at_column, kind):
        wide = right_ref.shape[1]

        def one(j, _):
            base = pl.multiple_of(j * span, span)
            cut = pl.ds(base, span)
            wsrc[cut, at_column : at_column + wide] = tn(left_ref[:, cut], right_ref[...]).astype(BF)
            for i in range(span // share):
                owner = lax.div(base, share) + i

                @pl.when(lax.rem(owner, 2) != parity)
                def _():
                    weight_copy(kind, owner, pair, (ps, pr), partner, lax.div(owner, 2), at_column, wide).start()

            return 0

        lax.fori_loop(0, normed.shape[1] // span, one, 0)

    def join(at_column, wide, kind):
        columns = slice(at_column, at_column + wide)

        def one(off, _):
            m = lax.rem(seat + off, half)
            owner = 2 * m + parity
            weight_copy(kind, owner, pair, (ps, pr), partner, m, at_column, wide).wait_recv()
            r = rows_of(owner)
            total = (wsrc[r, columns].astype(F32) + pair[m, :, columns].astype(F32)).astype(BF)

            @pl.when(owner == me)
            def _():
                wdst[seat, :, columns] = total

            @pl.when(owner != me)
            def _():
                wsrc[r, columns] = total
                weight_copy(kind, owner, wdst, (qs, qr), owner, seat, at_column, wide).start()

            return 0

        lax.fori_loop(1, half + 1, one, 0)

    joined = ((0, ow), (ow, dqkv.shape[1]))

    def flows(s, _):
        for k in range(tiles):

            @pl.when(s == k * 3)
            def _():
                attend_back_tile(tiles - 1 - k, tiles, *attention, part, dqkv, dk, dv)

        @pl.when(s == 2)
        def _():
            weigh(ga, o, 0, 0)

        @pl.when(s == 5)
        def _():
            join(*joined[0], 0)

        @pl.when(s == (tiles - 1) * 3 + 3)
        def _():
            join(*joined[1], 1)

        @pl.when(s == (tiles - 1) * 3 + 1)
        def _():
            fetch.wait()
            weigh(normed, dqkv, ow, 1)

        for d, buf, step in ((0, right, 1), (1, left, -1)):
            p = z if d == 0 else n - 1 - z
            c = s - lag * p

            @pl.when((c >= 0) & (c < count))
            def _():
                r = chunk_rows(c)
                for b in range(n - 1, 0, -1) if d == 0 else range(n - 1):
                    k = pl.ds(b * w, w)

                    @pl.when((b > z) if d == 0 else (b < z))
                    def _():
                        @pl.when(p == 0)
                        def _():
                            rcopy(at(part, c, b), at(buf, c, b), ss.at[d, b, c], rs.at[d, b, c], z + step).start()

                        @pl.when(p > 0)
                        def _():
                            rcopy(at(buf, c, b), at(buf, c, b), ss.at[d, b, c], rs.at[d, b, c], z).wait_recv()
                            buf[r, k] = (part[r, k].astype(F32) + buf[r, k].astype(F32)).astype(BF)
                            rcopy(at(buf, c, b), at(buf, c, b), ss.at[d, b, c], rs.at[d, b, c], z + step).start()

        c = s - lag * (n - 1)

        @pl.when((c >= 0) & (c < count))
        def _():
            r = chunk_rows(c)
            for b in range(n):
                k = pl.ds(b * w, w)

                @pl.when(z == b)
                def _():
                    total = part[r, k].astype(F32)
                    if b > 0:
                        rcopy(at(right, c, b), at(right, c, b), ss.at[0, b, c], rs.at[0, b, c], z).wait_recv()
                        total = total + right[r, k].astype(F32)
                    if b < n - 1:
                        rcopy(at(left, c, b), at(left, c, b), ss.at[1, b, c], rs.at[1, b, c], z).wait_recv()
                        total = total + left[r, k].astype(F32)
                    fb[r, :] = total

        @pl.when((c >= 0) & (c < count) & (lax.rem(jnp.maximum(c, 0), per) == per - 1))
        def _():
            open_tile(tiles - 1 - lax.div(c, per))

        c = c - 2

        @pl.when((c >= 0) & (lax.rem(jnp.maximum(c, 0), per) == per - 1))
        def _():
            close_tile(tiles - 1 - lax.div(c, per))

        return 0

    lax.fori_loop(0, count + lag * (n - 1) + 2, flows, 0)

    others(lambda other: width_copy(other, other).wait_recv())
    cols = gsrc.shape[2]
    first_gain = jnp.concatenate([widths[j] for j in range(n)], axis=1)
    second_gain = jnp.broadcast_to(gain2[...], first_gain.shape)
    for i in range(groups):
        gsrc[i, :8, :] = first_gain[:, i * cols : (i + 1) * cols]
        gsrc[i, 8:, :] = second_gain[:, i * cols : (i + 1) * cols]
    pltpu.make_async_copy(gsrc.at[me], gdst.at[me], own.at[1 + tiles]).start()

    def send_gain(off, _):
        peer = lax.rem(me + off, groups)
        pcopy(gsrc.at[peer], gdst.at[me], es.at[peer], er.at[me], peer).start()
        return 0

    lax.fori_loop(1, groups, send_gain, 0)

    def got_gain(off, _):
        peer = lax.rem(me + off, groups)
        copy = pcopy(gsrc.at[peer], gdst.at[peer], es.at[peer], er.at[peer], peer)
        copy.wait_recv()
        copy.wait_send()
        return 0

    lax.fori_loop(1, groups, got_gain, 0)
    pltpu.make_async_copy(gsrc.at[me], gdst.at[me], own.at[1 + tiles]).wait()
    total = gdst[0]
    for i in range(1, groups):
        total = total + gdst[i]
    gains[...] = total

    def got_weight(off, _):
        m = lax.rem(seat + off, half)
        for kind, (at_column, wide) in enumerate(joined):
            copy = weight_copy(kind, 2 * m + parity, wdst, (qs, qr), me, m, at_column, wide)
            copy.wait_recv()
            copy.wait_send()
        return 0

    def sent_weight(m, _):
        for kind, (at_column, wide) in enumerate(joined):
            weight_copy(kind, 2 * m + 1 - parity, pair, (ps, pr), partner, m, at_column, wide).wait_send()
        return 0

    lax.fori_loop(1, half, got_weight, 0)
    lax.fori_loop(0, half, sent_weight, 0)
    at_column = 0
    for share_ref in (o_share, q_share, k_share, v_share):
        columns = slice(at_column, at_column + share_ref.shape[1])
        at_column += share_ref.shape[1]
        total = wdst[0, :, columns].astype(F32)
        for i in range(1, half):
            total = total + wdst[i, :, columns].astype(F32)
        share_ref[...] = total

    def finish(off, _):
        peer = lax.rem(me + off, groups)
        copy = pcopy(result.at[:, peer], back_out.at[peer], os.at[peer], orr.at[peer], peer)
        copy.wait_recv()
        copy.wait_send()
        for t in range(tiles):
            copy = pcopy(dx.at[t, peer], back_dx.at[peer, t], xs.at[t, peer], xr.at[t, peer], peer)
            copy.wait_recv()
            copy.wait_send()
        return 0

    lax.fori_loop(1, groups, finish, 0)
    pltpu.make_async_copy(result.at[:, me], back_out.at[me], own.at[0]).wait()
    for t in range(tiles):
        pltpu.make_async_copy(dx.at[t, me], back_dx.at[me, t], own.at[1 + t]).wait()
        others(lambda other: line_copy(t, z, other).wait_send())
    others(lambda other: width_copy(z, other).wait_send())

    def drain(c, _):
        for d, buf in ((0, right), (1, left)):
            for b in range(n):

                @pl.when((b > z) if d == 0 else (b < z))
                def _():
                    rcopy(at(buf, c, b), at(buf, c, b), ss.at[d, b, c], rs.at[d, b, c], z).wait_send()

        return 0

    lax.fori_loop(0, count, drain, 0)


def deal_out(n, groups, tiles, x, dh, scale1, gain1, result, gain2, normed, *attention, chunk=64, lag=1):
    rows, w = x.shape
    width = n * w
    sub = rows // tiles // groups
    count = rows // chunk
    cols = width // groups
    joined = sum(a.shape[1] for a in attention[1:4])
    narrow = attention[2].shape[1]
    both = attention[8].shape[1] + joined
    dma = pltpu.SemaphoreType.DMA
    dealt = (groups, tiles, sub, w)
    return pl.pallas_call(
        functools.partial(deal_out_kernel, n, groups, tiles, chunk, lag),
        out_shape=[
            jax.ShapeDtypeStruct(dealt, BF),
            jax.ShapeDtypeStruct(dealt, BF),
            jax.ShapeDtypeStruct((16, cols), F32),
            jax.ShapeDtypeStruct((cols, attention[8].shape[1]), F32),
            *(jax.ShapeDtypeStruct((cols, a.shape[1]), F32) for a in attention[1:4]),
        ],
        in_specs=[VM] * 6 + [ANY] + [VM] * 15,
        out_specs=[VM] * 7,
        scratch_shapes=[
            pltpu.VMEM((rows, width), BF),
            pltpu.VMEM((rows, joined), BF),
            pltpu.VMEM((rows, narrow), F32),
            pltpu.VMEM((rows, narrow), F32),
            pltpu.VMEM((rows, width), BF),
            pltpu.VMEM((rows, width), BF),
            pltpu.VMEM((rows, w), F32),
            pltpu.VMEM((tiles, groups, sub, w), BF),
            pltpu.VMEM((n, 8, rows), F32),
            pltpu.VMEM((n, 8, w), F32),
            pltpu.VMEM((groups, 16, cols), F32),
            pltpu.VMEM((groups, 16, cols), F32),
            pltpu.VMEM((width, both), BF),
            pltpu.VMEM((groups // 2, cols, both), BF),
            pltpu.VMEM((groups // 2, cols, both), BF),
            pltpu.VMEM(normed.shape, BF),
            dma((2, n, count)),
            dma((2, n, count)),
            dma((groups,)),
            dma((groups,)),
            dma((tiles, groups)),
            dma((tiles, groups)),
            dma((n, tiles)),
            dma((n, tiles)),
            dma((n,)),
            dma((n,)),
            dma((groups,)),
            dma((groups,)),
            dma((2, groups // 2)),
            dma((2, groups // 2)),
            dma((2, groups // 2)),
            dma((2, groups // 2)),
            dma((tiles + 3,)),
        ],
        compiler_params=pltpu.CompilerParams(collective_id=5, has_side_effects=True, vmem_limit_bytes=62 << 20),
    )(x, dh, scale1, gain1, result.reshape(tiles, groups, sub, w), gain2, normed, *attention)


def rotary_tables(token_positions, head_size):
    half = head_size // 2
    freqs = rope_base ** (-(jnp.arange(half).astype(jnp.float32) * 2.0) / head_size)
    angles = token_positions.astype(jnp.float32)[:, None] * freqs[None, :]
    angles = jnp.concatenate([angles, angles], axis=1)
    return (jnp.cos(angles), jnp.sin(angles))


def matmul(left, right):
    return jnp.dot(left, right, preferred_element_type=jnp.float32)


def per_device(
    tokens,
    cotangent,
    first_gain,
    query_weight,
    key_matrix,
    value_matrix,
    output_weight,
    second_gain,
    gate_weight,
    up_weight,
    down_weight,
    seq_lengths,
    owner_order,
    skip_mask,
):
    groups = lax.axis_size("dp")
    member = lax.axis_index("dp")
    width_part = tokens.shape[1]
    row_count = tokens.shape[0]
    per_owner = row_count // groups
    seq_count = seq_lengths.shape[0]
    seq_index = jnp.arange(seq_count, dtype=jnp.int32)
    before = (seq_index[None, :] < seq_index[:, None]).astype(jnp.int32)
    unit_lengths = seq_lengths // groups
    unit_starts = jnp.sum(before * unit_lengths[None, :], axis=1)
    placed = (owner_order[:, None] == seq_index[None, :]).astype(jnp.int32)
    order_lengths = jnp.sum(placed * unit_lengths[None, :], axis=1)
    order_starts = jnp.sum(placed * unit_starts[None, :], axis=1)
    order_keep = jnp.sum(placed * skip_mask[None, :], axis=1)
    order_before = jnp.sum(before * order_lengths[None, :], axis=1)
    places = jnp.arange(row_count, dtype=jnp.int32)
    covers = (
        (places[:, None] >= order_before[None, :])
        & (places[:, None] < (order_before + order_lengths)[None, :])
    ).astype(jnp.int32)
    send_rows = places + jnp.sum(covers * (order_starts - order_before)[None, :], axis=1)
    given_before = jnp.sum(placed * order_before[:, None], axis=0)
    given_covers = (
        (places[:, None] >= unit_starts[None, :])
        & (places[:, None] < (unit_starts + unit_lengths)[None, :])
    ).astype(jnp.int32)
    slot_of = places + jnp.sum(given_covers * (given_before - unit_starts)[None, :], axis=1)
    my_places = member * per_owner + jnp.arange(per_owner, dtype=jnp.int32)
    my_covers = (
        (my_places[:, None] >= order_before[None, :])
        & (my_places[:, None] < (order_before + order_lengths)[None, :])
    ).astype(jnp.int32)
    slot_seq = jnp.sum(my_covers * seq_index[None, :], axis=1)
    slot_step = my_places - jnp.sum(my_covers * order_before[None, :], axis=1)
    slot_keep = jnp.sum(my_covers * order_keep[None, :], axis=1)
    tiles = max(1, per_owner // 32)
    sources = jnp.arange(groups, dtype=jnp.int32)[None, :, None]

    def spread(values):
        values = values.reshape(tiles, 1, per_owner // tiles)
        return jnp.broadcast_to(values, (tiles, groups, per_owner // tiles)).reshape(row_count)

    token_positions = (
        sources + groups * slot_step.reshape(tiles, 1, per_owner // tiles)
    ).reshape(row_count)
    lowest = spread(slot_seq) * row_count
    code = lowest + token_positions
    keep_rows = spread(slot_keep).reshape(row_count, 1).astype(jnp.float32)
    chosen = (send_rows[:, None] == places[None, :]).astype(jnp.bfloat16)
    put_back = (slot_of[:, None] == places[None, :]).astype(jnp.bfloat16)

    tensor_count = lax.axis_size("tensor")
    tensor_member = lax.axis_index("tensor")
    dealt_shape = (groups, tiles, per_owner // tiles, width_part)
    cosine, sine = rotary_tables(token_positions, HEAD_WIDTH)
    half = HEAD_WIDTH // 2
    tables = (
        cosine,
        jnp.concatenate([-sine[:, :half], sine[:, half:]], axis=1),
        code[None, :],
        code[:, None],
        lowest[:, None],
    )
    weights = (query_weight, key_matrix, value_matrix, output_weight)
    dealt_tokens, dealt_cotangent = (
        matmul(chosen, values).astype(BF).reshape(dealt_shape) for values in (tokens, cotangent)
    )
    owned_tokens, part_cotangent, part_tokens, attn_part, normed_one, *kept, scale_one = deal_in(
        tensor_count,
        groups,
        dealt_tokens,
        dealt_cotangent,
        first_gain[None, :],
        weights,
        tables,
    )
    owned_tokens = owned_tokens.reshape(row_count, -1)
    part_cotangent = part_cotangent.reshape(row_count, width_part)

    def my_part(values):
        return lax.dynamic_slice_in_dim(values, tensor_member * width_part, width_part, 1)

    result, attn_sum, owned_cotangent, normed_two, inner_low, both, second_term = middle(
        tensor_count,
        attn_part,
        owned_tokens,
        part_cotangent,
        keep_rows,
        second_gain[None, :],
        gate_weight,
        up_weight,
        down_weight,
    )
    hidden = gate_weight.shape[1]

    def shared(values):
        return lax.psum_scatter(
            values.astype(jnp.bfloat16), "dp", scatter_dimension=0, tiled=True
        )

    both_grad = matmul(normed_two.T, both).astype(BF)
    second_term, both_grad = lax.optimization_barrier((second_term, both_grad))
    both_share = shared(both_grad)
    grad_attn, grad_res, second_gain_grad, down_grad = second_back_of(
        tensor_count,
        second_term,
        owned_tokens,
        attn_sum,
        owned_cotangent,
        keep_rows,
        second_gain[None, :],
        inner_low,
    )
    both_share, down_grad, grad_attn = lax.optimization_barrier(
        (both_share, down_grad, grad_attn)
    )
    down_share = shared(down_grad)
    back_out, back_grad, gains, o_share, q_share, k_share, v_share = deal_out(
        tensor_count,
        groups,
        tiles,
        part_tokens.reshape(row_count, width_part),
        grad_res,
        scale_one,
        first_gain.reshape(tensor_count, width_part),
        result,
        second_gain_grad,
        normed_one,
        grad_attn,
        *weights,
        *kept,
        *tables,
    )
    down_share, back_out = lax.optimization_barrier((down_share, back_out))
    layer_output = matmul(put_back, back_out.reshape(row_count, width_part)).astype(BF)
    input_grad = matmul(put_back, back_grad.reshape(row_count, width_part)).astype(BF)
    summed = (
        gains[0],
        q_share,
        k_share,
        v_share,
        o_share.T,
        both_share[:, :hidden].astype(F32),
        both_share[:, hidden:].astype(F32),
        down_share.T.astype(F32),
        gains[8],
    )
    return (
        layer_output,
        input_grad,
        summed[0],
        summed[1],
        summed[2],
        summed[3],
        summed[4],
        summed[8],
        summed[5],
        summed[6],
        summed[7],
    )


def solution(mesh):
    placed = (
        P(None, ("dp", "tensor")),
        P(None, ("dp", "tensor")),
        P(),
        P(None, "tensor"),
        P(None, "tensor"),
        P(None, "tensor"),
        P("tensor", None),
        P(),
        P(None, "tensor"),
        P(None, "tensor"),
        P("tensor", None),
        P(),
        P(),
        P(),
    )
    return jax.shard_map(
        per_device,
        mesh=mesh,
        in_specs=placed,
        out_specs=(
            P(None, ("dp", "tensor")),
            P(None, ("dp", "tensor")),
            P("dp"),
            P("dp", "tensor"),
            P("dp", "tensor"),
            P("dp", "tensor"),
            P("tensor", "dp"),
            P("dp"),
            P("dp", "tensor"),
            P("dp", "tensor"),
            P("tensor", "dp"),
        ),
        check_vma=False,
    )
```
